128 devices in a mesh: dp: 32 (over y, x, z_hi), tensor: 4 (over z_lo, core).
Axes of the slice: x: 4, y: 4, z: 4 (z_hi: 2, z_lo: 2; z = z_hi * 2 + z_lo), core: 2. Of those that a mesh axis runs over, the one named last changes fastest.
Arguments:
- tokens: bfloat16 [16384, 1024], P('dp'), may hold values from -6 to 6
- norm1_gain: float32 [1024], replicated, may hold values from 0.5 to 1.5
- w_query: bfloat16 [1024, 1024], P(None, 'tensor'), may hold values from -0.1875 to 0.1875
- w_key: bfloat16 [1024, 512], P(None, 'tensor'), may hold values from -0.1875 to 0.1875
- w_value: bfloat16 [1024, 512], P(None, 'tensor'), may hold values from -0.1875 to 0.1875
- w_out: bfloat16 [1024, 1024], P('tensor'), may hold values from -0.75 to 0.75
- norm2_gain: float32 [1024], replicated, may hold values from 0.5 to 1.5
- expert_gate: bfloat16 [8, 1024, 512], P(None, None, 'tensor'), may hold values from -0.1875 to 0.1875
- expert_up: bfloat16 [8, 1024, 512], P(None, None, 'tensor'), may hold values from -0.1875 to 0.1875
- expert_down: bfloat16 [8, 512, 1024], P(None, 'tensor'), may hold values from -1 to 1
- routes: int32 [16384, 4], P('dp'), may hold values from 0 to 7, all different within a row
- gate_weights: float32 [16384, 4], P('dp'), may hold values from 0.1 to 0.5
- segments: int32 [32, 512], P('dp'), may hold values from 0 to 3, never falling along the last dimension, each value on 1 to 320 neighbouring positions
- cotangent: bfloat16 [16384, 1024], P('dp'), may hold values from -6 to 6
Outputs:
- output: bfloat16 [16384, 1024], P('dp')
- input_grad: float32 [16384, 1024], P('dp')
- norm1_gain_grad: float32 [1024], replicated
- w_query_grad: float32 [1024, 1024], P(None, 'tensor')
- w_key_grad: float32 [1024, 512], P(None, 'tensor')
- w_value_grad: float32 [1024, 512], P(None, 'tensor')
- w_out_grad: float32 [1024, 1024], P('tensor')
- norm2_gain_grad: float32 [1024], replicated
- expert_gate_grad: float32 [8, 1024, 512], P(None, None, 'tensor')
- expert_up_grad: float32 [8, 1024, 512], P(None, None, 'tensor')
- expert_down_grad: float32 [8, 512, 1024], P(None, 'tensor')
The draws below stay inside these ranges and needn't reach their ends.
Inputs may be any that keep to these rules, and one draw needn't show every extreme that they name: `routes`: each row names 4 different experts. `segments`: document numbers never fall along a sequence; each document has at most 320 tokens and one has exactly that many.
All inputs are finite; a program needn't handle non-finite values.
Results may differ from the reference program's by a relative error of at most 0.015.
Values sent between devices are 32-bit elements; how exact they have to be, the bound alone decides.
A program may use at most 128 MiB of HBM per device.

```python
import math
import jax
import jax.numpy as jnp
import numpy as np
from jax import lax

D = 1024
H = 16
KV = 8
HD = 64
FF = 512
EXPERTS = 8
TOPK = 4
SEQ_LEN = 512
SEQS = 32
TOKENS = 16384


def block_scale(own_key, dims, split, low, top_value):
    def one(dim, shards_of):
        draws = jax.random.uniform(jax.random.fold_in(jax.random.fold_in(own_key, 6), dim), (shards_of,), jnp.float32, low / len(split), top_value / len(split))
        return jnp.repeat(jnp.exp(draws), dims[dim] // shards_of).reshape((-1,) + (1,) * (len(dims) - dim - 1))

    loudness = one(*split[0])
    for cut in split[1:]:
        loudness = loudness * one(*cut)
    return loudness


def different_ones(stream_key, rows, number_of, top, lift):
    order = jax.random.permutation(jax.random.fold_in(stream_key, 1), number_of)
    boost = order
    for power in range(3):
        boost = boost * boost // number_of
    boost = boost * lift // number_of
    lots = jax.random.randint(jax.random.fold_in(stream_key, 2), (rows, number_of), 0, 4096) + boost
    sure = jax.random.permutation(jax.random.fold_in(stream_key, 3), rows)[jnp.arange(number_of) % rows]
    lots = jnp.where(jnp.arange(rows)[:, None] == sure[None, :], 1 << 14, lots)
    priority = lots * number_of + jnp.arange(number_of)
    return lax.top_k(priority.astype(jnp.int32), top)[1].astype(jnp.int32)


def profile(count, total, reach, slope):
    portions = [(1 << 20) // math.isqrt(rank ** slope) + 1 for rank in range(2, count + 1)]
    rest, given = total - reach - (count - 1), [1] * (count - 1)
    while rest > 0:
        movable = [i for i in range(count - 1) if given[i] < reach]
        pool, left = sum([portions[i] for i in movable]), rest
        for i in movable:
            addition = min(reach - given[i], max(1, left * portions[i] // pool), rest)
            given[i] = given[i] + addition
            rest = rest - addition
    return np.array([reach] + given)


def ragged_sizes(rng, number_of, total, most, lean):
    if number_of == 2:
        one = jax.random.randint(rng, (), max(1, total - most), min(most, total - 1) + 1)
        return jnp.stack([one, total - one])
    tallies = jnp.asarray(profile(number_of, total, most, lean), jnp.int32)
    pairs = (number_of - 1) // 2
    donor, taker = tallies[1:1 + 2 * pairs:2], tallies[2:2 + 2 * pairs:2]
    margin = jnp.minimum(donor - 1, most - taker)
    shifted = jax.random.randint(jax.random.fold_in(rng, 1), (pairs,), 0, 1 << 20) % (margin + 1)
    tallies = tallies.at[1:1 + 2 * pairs:2].set(donor - shifted).at[2:2 + 2 * pairs:2].set(taker + shifted)
    return tallies[jax.random.permutation(jax.random.fold_in(rng, 2), number_of)]


def gaussian(rng, extent, deviation, bound, pieces=(), held_as=jnp.bfloat16):
    gain = block_scale(rng, extent, pieces, -0.22, 0.18) if pieces else 1.0
    values = jax.random.normal(rng, extent, jnp.float32) * deviation * gain
    return jnp.minimum(jnp.maximum(values, -bound), bound).astype(held_as)


def setup_inputs(seed: int = 0) -> dict:
    seeds = jax.random.split(jax.random.key(seed), 15)
    return {
        "tokens": gaussian(seeds[0], (TOKENS, D), 1.0, 6.0, ((0, 32),)),
        "norm1_gain": jnp.clip(1.0 + 0.1 * jax.random.normal(seeds[1], (D,), jnp.float32), 0.5, 1.5),
        "w_query": gaussian(seeds[2], (D, H * HD), D ** -0.5, 0.1875, ((1, 4),)),
        "w_key": gaussian(seeds[3], (D, KV * HD), D ** -0.5, 0.1875, ((1, 4),)),
        "w_value": gaussian(seeds[4], (D, KV * HD), D ** -0.5, 0.1875, ((1, 4),)),
        "w_out": gaussian(seeds[5], (H * HD, D), (H * HD // 16) ** -0.5, 0.75, ((0, 4),)),
        "norm2_gain": jnp.clip(1.0 + 0.1 * jax.random.normal(seeds[6], (D,), jnp.float32), 0.5, 1.5),
        "expert_gate": gaussian(seeds[7], (EXPERTS, D, FF), D ** -0.5, 0.1875, ((2, 4),)),
        "expert_up": gaussian(seeds[8], (EXPERTS, D, FF), D ** -0.5, 0.1875, ((2, 4),)),
        "expert_down": gaussian(seeds[9], (EXPERTS, FF, D), (FF // 16) ** -0.5, 1.0, ((1, 4),)),
        "routes": different_ones(seeds[10], TOKENS, EXPERTS, TOPK, 0),
        "gate_weights": jnp.clip(jnp.exp(math.log(0.5) - 1.609438 * jax.random.uniform(seeds[11], (TOKENS, TOPK), jnp.float32) ** block_scale(seeds[11], (TOKENS, TOPK), ((0, 32),), -0.2, 0.2)), 0.1, 0.5),
        "segments": jax.vmap(lambda own: jnp.searchsorted(jnp.cumsum(ragged_sizes(own, 4, SEQ_LEN, SEQ_LEN * 5 // 8, 0)), jnp.arange(SEQ_LEN), side="right"))(jax.random.split(seeds[12], SEQS)).reshape((SEQS, SEQ_LEN)).astype(jnp.int32),
        "cotangent": gaussian(seeds[13], (TOKENS, D), 1.0, 6.0, ((0, 32),)),
    }


NORM_EPS = 1e-06
ROPE_THETA = 10000.0
HIGHEST = lax.Precision.HIGHEST

@jax.custom_vjp
def low(v):
    return lax.optimization_barrier(v.astype(jnp.bfloat16)).astype(jnp.float32)

@jax.custom_vjp
def low_back(v):
    return v

def low_keep(v):
    return (low(v), None)

def low_pass(kept, grad):
    return (grad,)

def back_keep(v):
    return (v, None)

def back_low(kept, grad):
    return (low(grad),)
low.defvjp(low_keep, low_pass)
low_back.defvjp(back_keep, back_low)

def rms_norm(values, gain_vec):
    return values * lax.rsqrt(lax.optimization_barrier(jnp.mean(values * values, -1, keepdims=True)) + NORM_EPS) * gain_vec

def rotate(values, position):
    half_width = values.shape[-1] // 2
    frequency = ROPE_THETA ** (-jnp.arange(half_width, dtype=jnp.float32) * 2.0 / values.shape[-1])
    angles = position.astype(jnp.float32)[:, None] * frequency[None, :]
    cos_table = jnp.cos(angles)[:, None, :]
    sin_table = jnp.sin(angles)[:, None, :]
    first_half = values[..., :half_width]
    second_half = values[..., half_width:]
    return jnp.concatenate([first_half * cos_table - second_half * sin_table, second_half * cos_table + first_half * sin_table], -1)

def attend(block):
    queries, keys, values, segment_ids = block
    seq_length = segment_ids.shape[0]
    raw_scores = jnp.einsum('qngd,knd->ngqk', queries, keys, precision=HIGHEST) * HD ** (-0.5)
    raw_scores = low_back(raw_scores)
    position = jnp.arange(seq_length)
    allowed = (segment_ids[:, None] == segment_ids[None, :]) & (position[:, None] >= position[None, :])
    masked = jnp.where(allowed, raw_scores, -1e+30)
    row_max = lax.optimization_barrier(jnp.max(masked, -1, keepdims=True))
    weights = jnp.exp(masked - row_max)
    probabilities = weights / lax.optimization_barrier(jnp.sum(weights, -1, keepdims=True))
    mixed_heads = jnp.einsum('ngqk,knd->qngd', low(probabilities), values, precision=HIGHEST)
    return low(low_back(mixed_heads)).reshape(seq_length, H * HD)

def reference(tokens, norm1_gain, w_query, w_key, w_value, w_out, norm2_gain, expert_gate, expert_up, expert_down, routes, gate_weights, segments, cotangent):
    expert_ids = jnp.arange(EXPERTS).astype(jnp.int32)
    picked = (routes[:, :, None] == expert_ids[None, None, :]).astype(jnp.float32)
    expert_share = lax.optimization_barrier(jnp.sum(gate_weights[:, :, None] * picked, 1)).T
    position = jnp.tile(jnp.arange(SEQ_LEN), SEQS)

    def forward(inputs, gain_one, query_w, key_w, value_w, out_w, gain_two, gate_w, up_w, down_w):
        hidden1 = low(rms_norm(inputs, gain_one))
        queries = low(rotate(low_back(jnp.dot(hidden1, query_w, precision=HIGHEST)).reshape(TOKENS, H, HD), position))
        keys = low(rotate(low_back(jnp.dot(hidden1, key_w, precision=HIGHEST)).reshape(TOKENS, KV, HD), position))
        values = low(low_back(jnp.dot(hidden1, value_w, precision=HIGHEST)))
        queries = queries.reshape(SEQS, SEQ_LEN, KV, H // KV, HD)
        keys = keys.reshape(SEQS, SEQ_LEN, KV, HD)
        values = values.reshape(SEQS, SEQ_LEN, KV, HD)
        mixed = lax.map(jax.checkpoint(attend), (queries, keys, values, segments)).reshape(TOKENS, H * HD)
        attention = low_back(jnp.dot(mixed, out_w, precision=HIGHEST))
        residual = inputs + attention
        hidden2 = low(rms_norm(residual, gain_two))
        gate_pre = low_back(jnp.einsum('td,edf->etf', hidden2, gate_w, precision=HIGHEST))
        up_pre = low_back(jnp.einsum('td,edf->etf', hidden2, up_w, precision=HIGHEST))
        activated = low(jax.nn.silu(gate_pre) * up_pre * expert_share[:, :, None])
        expert_total = low_back(jnp.einsum('etf,efd->td', activated, down_w, precision=HIGHEST))
        return residual + expert_total
    result, pullback = jax.vjp(forward, tokens.astype(jnp.float32), norm1_gain, w_query.astype(jnp.float32), w_key.astype(jnp.float32), w_value.astype(jnp.float32), w_out.astype(jnp.float32), norm2_gain, expert_gate.astype(jnp.float32), expert_up.astype(jnp.float32), expert_down.astype(jnp.float32))
    grads = pullback(cotangent.astype(jnp.float32))
    return (result.astype(jnp.bfloat16), grads[0], grads[1], grads[2], grads[3], grads[4], grads[5], grads[6], grads[7], grads[8], grads[9])
```

```python
import functools

import jax
import jax.numpy as jnp
from jax import lax
from jax.experimental import pallas as pl
from jax.experimental.pallas import tpu as pltpu
from jax.sharding import PartitionSpec as P

MESH = pl.DeviceIdType.MESH


def ring_pos(dp):
    xy = dp // 2
    x, y = xy % 4, xy // 4
    turn = (x + y) % 4
    return 4 * y + turn, 4 * x + turn


def ring_dp(kind, pos, zhi):
    a = pos // 4
    b = (pos % 4 - a + 4) % 4
    x, y = (b, a) if kind == 0 else (a, b)
    return (y * 4 + x) * 2 + zhi


FLOWS = ((0, 1), (0, -1), (1, 1), (1, -1))


def dp_kernel(sub, g, out, land, zland, total, rs_s, rs_r, ag_s, ag_r, z_s, z_r, loc):
    dp = lax.axis_index("dp")
    tn = lax.axis_index("tensor")
    zhi = dp % 2
    zpeer = dp + 1 - 2 * zhi
    pos = ring_pos(dp)
    barrier = pltpu.get_barrier_semaphore()
    peers = []
    for kind in (0, 1):
        for d in (1, -1):
            peers.append(ring_dp(kind, (pos[kind] + d + 16) % 16, zhi))
    for q in peers + [zpeer]:
        pl.semaphore_signal(barrier, inc=1, device_id=(q, tn), device_id_type=MESH)
    pl.semaphore_wait(barrier, 5)

    def rs(u, f, s, src):
        kind, d = FLOWS[f]
        c = (pos[kind] - d * (1 + s) + 32) % 16
        return pltpu.make_async_remote_copy(
            src.at[u, f, c], land.at[u, f, c], rs_s.at[u, f, s], rs_r.at[u, f, s],
            device_id=(peers[f], tn), device_id_type=MESH)

    def ag(u, f, s, src):
        kind, d = FLOWS[f]
        c = (pos[kind] - d * s + 32) % 16
        return pltpu.make_async_remote_copy(
            src, out.at[u, f, c], ag_s.at[u, f, s], ag_r.at[u, f, s],
            device_id=(peers[f], tn), device_id_type=MESH)

    def rs_add(u, f, s):
        kind, d = FLOWS[f]
        c = (pos[kind] - d * (1 + s) + 32) % 16
        land[u, f, c] = land[u, f, c] + g[u, f, c]
        return c

    def zcopy(u, f):
        return pltpu.make_async_remote_copy(
            land.at[u, f, pos[FLOWS[f][0]]], zland.at[u, f], z_s.at[u, f], z_r.at[u, f],
            device_id=(zpeer, tn), device_id_type=MESH)

    def keep(u, f):
        return pltpu.make_async_copy(total.at[u, f], out.at[u, f, pos[FLOWS[f][0]]], loc.at[u, f])

    for u in range(sub):
        for f in range(4):
            rs(u, f, 0, g).start()

    def rs_step(s, _):
        for u in range(sub):
            for f in range(4):
                rs(u, f, s - 1, land).wait_recv()
                rs_add(u, f, s)
                rs(u, f, s, land).start()
        return 0
    lax.fori_loop(1, 15, rs_step, 0)
    for u in range(sub):
        for f in range(4):
            rs(u, f, 14, land).wait_recv()
            rs_add(u, f, 15)
            zcopy(u, f).start()
    for u in range(sub):
        for f in range(4):
            zcopy(u, f).wait_recv()
            total[u, f] = land[u, f, pos[FLOWS[f][0]]] + zland[u, f]
            ag(u, f, 0, total.at[u, f]).start()
            keep(u, f).start()

    def ag_step(s, _):
        for u in range(sub):
            for f in range(4):
                kind, d = FLOWS[f]
                c = (pos[kind] - d * s + 32) % 16
                ag(u, f, s - 1, out.at[u, f, c]).wait_recv()
                ag(u, f, s, out.at[u, f, c]).start()
        return 0
    lax.fori_loop(1, 15, ag_step, 0)
    for u in range(sub):
        for f in range(4):
            ag(u, f, 14, total.at[u, f]).wait_recv()

    def drain(s, _):
        for u in range(sub):
            for f in range(4):
                rs(u, f, s, land).wait_send()
                ag(u, f, s, total.at[u, f]).wait_send()
        return 0
    lax.fori_loop(0, 15, drain, 0)
    for u in range(sub):
        for f in range(4):
            zcopy(u, f).wait_send()
            keep(u, f).wait()


def dp_sum(g, cid=1):
    sub, _, _, m, _ = g.shape
    D = pltpu.SemaphoreType.DMA
    return pl.pallas_call(
        functools.partial(dp_kernel, sub),
        out_shape=jax.ShapeDtypeStruct(g.shape, jnp.float32),
        in_specs=[pl.BlockSpec(memory_space=pltpu.VMEM)],
        out_specs=pl.BlockSpec(memory_space=pl.ANY),
        scratch_shapes=[
            pltpu.VMEM(g.shape, jnp.float32),
            pltpu.VMEM((sub, 4, m, 128), jnp.float32),
            pltpu.VMEM((sub, 4, m, 128), jnp.float32),
            D((sub, 4, 15)), D((sub, 4, 15)), D((sub, 4, 15)), D((sub, 4, 15)),
            D((sub, 4)), D((sub, 4)), D((sub, 4)),
        ],
        compiler_params=pltpu.CompilerParams(collective_id=cid, has_side_effects=True, vmem_limit_bytes=60 << 20),
    )(g)


def ar4_kernel(K, x, out, buf, land1, land2, s1, r1, s2, r2, s3, r3):
    dp = lax.axis_index("dp")
    tn = lax.axis_index("tensor")
    core = tn % 2
    buddy = tn + 1 - 2 * core
    zlo = tn // 2
    zpeer = tn + 2 - 4 * zlo
    barrier = pltpu.get_barrier_semaphore()
    for q in (buddy, zpeer):
        pl.semaphore_signal(barrier, inc=1, device_id=(dp, q), device_id_type=MESH)
    pl.semaphore_wait(barrier, 2)
    half = x.shape[0] // 2
    n = half // K

    def one(k):
        return pltpu.make_async_remote_copy(
            x.at[pl.ds((1 - core) * half + k * n, n)], land1.at[pl.ds(k * n, n)], s1.at[k], r1.at[k],
            device_id=(dp, buddy), device_id_type=MESH)

    def two(k):
        return pltpu.make_async_remote_copy(
            buf.at[pl.ds(k * n, n)], land2.at[pl.ds(k * n, n)], s2.at[k], r2.at[k],
            device_id=(dp, zpeer), device_id_type=MESH)

    def three(k):
        rows = pl.ds(core * half + k * n, n)
        return pltpu.make_async_remote_copy(
            out.at[rows], out.at[rows], s3.at[k], r3.at[k],
            device_id=(dp, buddy), device_id_type=MESH)

    for k in range(K):
        one(k).start()
    for k in range(K):
        one(k).wait_recv()
        buf[pl.ds(k * n, n)] = land1[pl.ds(k * n, n)] + x[pl.ds(core * half + k * n, n)]
        two(k).start()
    for k in range(K):
        two(k).wait_recv()
        out[pl.ds(core * half + k * n, n)] = buf[pl.ds(k * n, n)] + land2[pl.ds(k * n, n)]
        three(k).start()
    for k in range(K):
        three(k).wait_recv()
    for k in range(K):
        one(k).wait_send()
        two(k).wait_send()
        three(k).wait_send()


def ar4(x, K, cid):
    D = pltpu.SemaphoreType.DMA
    h = (x.shape[0] // 2, x.shape[1])
    return pl.pallas_call(
        functools.partial(ar4_kernel, K),
        out_shape=jax.ShapeDtypeStruct(x.shape, jnp.float32),
        in_specs=[pl.BlockSpec(memory_space=pltpu.VMEM)],
        out_specs=pl.BlockSpec(memory_space=pltpu.VMEM),
        scratch_shapes=[pltpu.VMEM(h, jnp.float32), pltpu.VMEM(h, jnp.float32), pltpu.VMEM(h, jnp.float32),
            D((K,)), D((K,)), D((K,)), D((K,)), D((K,)), D((K,))],
        compiler_params=pltpu.CompilerParams(collective_id=cid, has_side_effects=True, vmem_limit_bytes=60 << 20),
    )(x)


HD = 64


NORM_EPS = 1e-06
ROPE_THETA = 10000.0


def normalize(values, gain_vec):
    inverse = lax.rsqrt(jnp.mean(values * values, -1, keepdims=True) + NORM_EPS)
    scaled = values * inverse
    return (scaled * gain_vec, scaled, inverse)


def norm_back(gradient, scaled, inverse, gain_vec):
    scaled_grad = gradient * gain_vec
    inner_sum = jnp.mean(scaled_grad * scaled, -1, keepdims=True)
    return (inverse * (scaled_grad - scaled * inner_sum), jnp.sum(gradient * scaled, 0))


def tables(seq_count, seq_length, head_width):
    half_width = head_width // 2
    frequency = ROPE_THETA ** (-jnp.arange(half_width, dtype=jnp.float32) * 2.0 / head_width)
    position = jnp.tile(jnp.arange(seq_length), seq_count).astype(jnp.float32)
    angles = position[:, None] * frequency[None, :]
    return (jnp.cos(angles)[:, None, :], jnp.sin(angles)[:, None, :])


def rotate(values, cos_table, sin_table):
    half_width = values.shape[-1] // 2
    first_half = values[..., :half_width]
    second_half = values[..., half_width:]
    return jnp.concatenate(
        [
            first_half * cos_table - second_half * sin_table,
            second_half * cos_table + first_half * sin_table,
        ],
        -1,
    )


def unrotate(gradient, cos_table, sin_table):
    half_width = gradient.shape[-1] // 2
    first_half = gradient[..., :half_width]
    second_half = gradient[..., half_width:]
    return jnp.concatenate(
        [
            first_half * cos_table + second_half * sin_table,
            second_half * cos_table - first_half * sin_table,
        ],
        -1,
    )


def scores_of(query_blocks, key_blocks, segments):
    raw_scores = jnp.einsum(
        "bqngd,bknd->bngqk", query_blocks, key_blocks, preferred_element_type=jnp.float32
    ) * HD ** (-0.5)
    position = jnp.arange(segments.shape[1])
    allowed = (segments[:, :, None] == segments[:, None, :]) & (
        position[:, None] >= position[None, :]
    )
    return jnp.where(allowed[:, None, None, :, :], raw_scores, -1e30)


def left_product(first_op, second_op):
    return lax.dot_general(
        first_op, second_op, (((0,), (0,)), ((), ())), preferred_element_type=jnp.float32
    )


def right_product(first_op, second_op):
    return lax.dot_general(
        first_op, second_op, (((1,), (1,)), ((), ())), preferred_element_type=jnp.float32
    )


def local(
    tokens,
    norm1_gain,
    w_query,
    w_key,
    w_value,
    w_out,
    norm2_gain,
    expert_gate,
    expert_up,
    expert_down,
    routes,
    gate_weights,
    segments,
    cotangent,
):
    seq_count, seq_length = segments.shape
    tok_rows = tokens.shape[0]
    head_count = w_query.shape[1] // HD
    groups = w_key.shape[1] // HD
    group_size = head_count // groups
    experts = expert_gate.shape[0]
    cos_table, sin_table = tables(seq_count, seq_length, HD)
    inputs = tokens.astype(jnp.float32)
    normed1, scaled1, inverse1 = normalize(inputs, norm1_gain)
    hidden1 = normed1.astype(jnp.bfloat16)
    queries = rotate(
        jnp.dot(hidden1, w_query, preferred_element_type=jnp.float32).reshape(
            tok_rows, head_count, HD
        ),
        cos_table,
        sin_table,
    ).astype(jnp.bfloat16)
    keys = rotate(
        jnp.dot(hidden1, w_key, preferred_element_type=jnp.float32).reshape(tok_rows, groups, HD),
        cos_table,
        sin_table,
    ).astype(jnp.bfloat16)
    values = jnp.dot(hidden1, w_value, preferred_element_type=jnp.float32).astype(jnp.bfloat16)
    query_blocks = queries.reshape(seq_count, seq_length, groups, group_size, HD)
    key_blocks = keys.reshape(seq_count, seq_length, groups, HD)
    value_blocks = values.reshape(seq_count, seq_length, groups, HD)
    scores = scores_of(query_blocks, key_blocks, segments)
    row_max = jnp.max(scores, -1, keepdims=True)
    weights = jnp.exp(scores - row_max)
    row_total = jnp.sum(weights, -1, keepdims=True)
    probabilities = weights / row_total
    log_total = row_max + jnp.log(row_total)
    mixed_heads = jnp.einsum(
        "bngqk,bknd->bqngd",
        probabilities.astype(jnp.bfloat16),
        value_blocks,
        preferred_element_type=jnp.float32,
    )
    mixed_heads = mixed_heads.reshape(tok_rows, head_count * HD).astype(jnp.bfloat16)
    attention = ar4(jnp.dot(mixed_heads, w_out, preferred_element_type=jnp.float32), 4, 2)
    residual = inputs + attention
    normed2, scaled2, inverse2 = normalize(residual, norm2_gain)
    hidden2 = normed2.astype(jnp.bfloat16)
    picked = (routes[:, :, None] == jnp.arange(experts)[None, None, :]).astype(jnp.float32)
    expert_share = jnp.sum(gate_weights[:, :, None] * picked, 1).T[:, :, None]
    gate_pre = jnp.einsum("td,edf->etf", hidden2, expert_gate, preferred_element_type=jnp.float32)
    up_pre = jnp.einsum("td,edf->etf", hidden2, expert_up, preferred_element_type=jnp.float32)
    sigmoid_gate = jax.nn.sigmoid(gate_pre)
    silu_gate = gate_pre * sigmoid_gate
    activated = (silu_gate * up_pre * expert_share).astype(jnp.bfloat16)
    expert_total = ar4(
        jnp.einsum("etf,efd->td", activated, expert_down, preferred_element_type=jnp.float32),
        4,
        3,
    )
    output = (residual + expert_total).astype(jnp.bfloat16)
    grad_out = cotangent.astype(jnp.float32)
    grad_act = jnp.einsum("td,efd->etf", cotangent, expert_down, preferred_element_type=jnp.float32)
    grad_gate = (
        grad_act * expert_share * up_pre * (sigmoid_gate * (1.0 + gate_pre * (1.0 - sigmoid_gate)))
    ).astype(jnp.bfloat16)
    grad_up = (grad_act * expert_share * silu_gate).astype(jnp.bfloat16)
    gate_grad = jnp.einsum("td,etf->edf", hidden2, grad_gate, preferred_element_type=jnp.float32)
    up_grad = jnp.einsum("td,etf->edf", hidden2, grad_up, preferred_element_type=jnp.float32)
    down_grad = jnp.einsum("etf,td->efd", activated, cotangent, preferred_element_type=jnp.float32)
    grad_hidden2 = ar4(
        jnp.einsum("etf,edf->td", grad_gate, expert_gate, preferred_element_type=jnp.float32)
        + jnp.einsum("etf,edf->td", grad_up, expert_up, preferred_element_type=jnp.float32),
        4,
        4,
    )
    back_two, gain2_grad = norm_back(grad_hidden2, scaled2, inverse2, norm2_gain)
    grad_residual = grad_out + back_two
    grad_branch = grad_residual.astype(jnp.bfloat16)
    out_w_grad = left_product(mixed_heads, grad_branch)
    grad_mixed = right_product(grad_branch, w_out).astype(jnp.bfloat16)
    grad_mixed = grad_mixed.reshape(seq_count, seq_length, groups, group_size, HD)
    scores = scores_of(query_blocks, key_blocks, segments)
    probabilities = jnp.exp(scores - log_total)
    grad_probs = jnp.einsum(
        "bqngd,bknd->bngqk", grad_mixed, value_blocks, preferred_element_type=jnp.float32
    )
    value_grad = jnp.einsum(
        "bngqk,bqngd->bknd",
        probabilities.astype(jnp.bfloat16),
        grad_mixed,
        preferred_element_type=jnp.float32,
    )
    value_grad = value_grad.reshape(tok_rows, groups * HD).astype(jnp.bfloat16)
    inner_sum = jnp.sum(probabilities * grad_probs, -1, keepdims=True)
    grad_scores = (probabilities * (grad_probs - inner_sum)).astype(jnp.bfloat16)
    query_grad = jnp.einsum(
        "bngqk,bknd->bqngd", grad_scores, key_blocks, preferred_element_type=jnp.float32
    ) * HD ** (-0.5)
    query_grad = unrotate(query_grad.reshape(tok_rows, head_count, HD), cos_table, sin_table)
    query_grad = query_grad.reshape(tok_rows, head_count * HD).astype(jnp.bfloat16)
    key_grad = jnp.einsum(
        "bngqk,bqngd->bknd", grad_scores, query_blocks, preferred_element_type=jnp.float32
    ) * HD ** (-0.5)
    key_grad = unrotate(key_grad.reshape(tok_rows, groups, HD), cos_table, sin_table)
    key_grad = key_grad.reshape(tok_rows, groups * HD).astype(jnp.bfloat16)
    query_w_grad = left_product(hidden1, query_grad)
    key_w_grad = left_product(hidden1, key_grad)
    value_w_grad = left_product(hidden1, value_grad)
    grad_hidden1 = ar4(
        right_product(query_grad, w_query)
        + right_product(key_grad, w_key)
        + right_product(value_grad, w_value),
        4,
        5,
    )
    back_one, gain1_grad = norm_back(grad_hidden1, scaled1, inverse1, norm1_gain)
    input_grad = grad_residual + back_one
    parts = (
        gate_grad, up_grad, down_grad, query_w_grad, key_w_grad, value_w_grad, out_w_grad,
        gain1_grad, gain2_grad,
    )
    rows = [part.size // 128 for part in parts]
    short = -sum(rows) % 1024
    packed = jnp.concatenate(
        [part.reshape(-1, 128) for part in parts] + [jnp.zeros((short, 128), jnp.float32)]
    )
    summed = dp_sum(packed.reshape(2, 4, 16, -1, 128)).reshape(-1, 128)
    done = []
    at = 0
    for part, count in zip(parts, rows):
        done.append(summed[at : at + count].reshape(part.shape))
        at += count
    return (
        output, input_grad, done[7], done[3], done[4], done[5], done[6], done[8],
        done[0], done[1], done[2],
    )


def solution(mesh):
    return jax.shard_map(
        local,
        mesh=mesh,
        in_specs=(
            P("dp", None),
            P(),
            P(None, "tensor"),
            P(None, "tensor"),
            P(None, "tensor"),
            P("tensor", None),
            P(),
            P(None, None, "tensor"),
            P(None, None, "tensor"),
            P(None, "tensor", None),
            P("dp", None),
            P("dp", None),
            P("dp", None),
            P("dp", None),
        ),
        out_specs=(
            P("dp", None),
            P("dp", None),
            P(),
            P(None, "tensor"),
            P(None, "tensor"),
            P(None, "tensor"),
            P("tensor", None),
            P(),
            P(None, None, "tensor"),
            P(None, None, "tensor"),
            P(None, "tensor", None),
        ),
        check_vma=False,
    )
```

```python
import functools

import jax
import jax.numpy as jnp
from jax import lax
from jax.experimental import pallas as pl
from jax.experimental.pallas import tpu as pltpu
from jax.sharding import PartitionSpec as P

MESH = pl.DeviceIdType.MESH
DMA = pltpu.SemaphoreType.DMA
F32 = jnp.float32
BF16 = jnp.bfloat16

HD = 64
NORM_EPS = 1e-06
ROPE_THETA = 10000.0
FLOWS = ((0, 1), (0, -1), (1, 1), (1, -1))
PIECES = 4
VMEM = pl.BlockSpec(memory_space=pltpu.VMEM)
ANY = pl.BlockSpec(memory_space=pl.ANY)


def dot_nn(first_op, second_op):
    return jnp.dot(first_op, second_op, preferred_element_type=F32)


def dot_tn(first_op, second_op):
    return lax.dot_general(
        first_op, second_op, (((0,), (0,)), ((), ())), preferred_element_type=F32
    )


def dot_nt(first_op, second_op):
    return lax.dot_general(
        first_op, second_op, (((1,), (1,)), ((), ())), preferred_element_type=F32
    )


def ring_pos(dp):
    xy = dp // 2
    x, y = xy % 4, xy // 4
    turn = (x + y) % 4
    return 4 * y + turn, 4 * x + turn


def ring_dp(kind, pos, zhi):
    along = pos // 4
    across = (pos % 4 - along + 4) % 4
    x, y = (across, along) if kind == 0 else (along, across)
    return (y * 4 + x) * 2 + zhi


class Place:
    def __init__(self):
        self.dp = lax.axis_index("dp")
        self.tensor = lax.axis_index("tensor")
        zhi = self.dp % 2
        self.z_far = self.dp + 1 - 2 * zhi
        self.pos = ring_pos(self.dp)
        self.next = [
            ring_dp(kind, (self.pos[kind] + step + 16) % 16, zhi) for kind, step in FLOWS
        ]
        self.core = self.tensor % 2
        self.buddy = self.tensor + 1 - 2 * self.core
        self.z_near = self.tensor + 2 - 4 * (self.tensor // 2)


class Ring:
    def __init__(self, place, first, mine, land, zland, total, out, sems):
        self.place, self.first, self.mine, self.land = place, first, mine, land
        self.zland, self.total, self.out = zland, total, out
        self.rs_s, self.rs_r, self.ag_s, self.ag_r, self.z_s, self.z_r, self.keep_s = sems

    def chunk(self, f, back):
        kind, step = FLOWS[f]
        return (self.place.pos[kind] - step * back + 32) % 16

    def rs(self, f, s, src):
        c = self.chunk(f, 1 + s)
        return pltpu.make_async_remote_copy(
            src.at[f, c], self.land.at[f, c], self.rs_s.at[f, s], self.rs_r.at[f, s],
            device_id=(self.place.next[f], self.place.tensor), device_id_type=MESH,
        )

    def ag(self, f, s, src):
        return pltpu.make_async_remote_copy(
            src, self.out.at[f, self.chunk(f, s)], self.ag_s.at[f, s], self.ag_r.at[f, s],
            device_id=(self.place.next[f], self.place.tensor), device_id_type=MESH,
        )

    def zcopy(self, f):
        return pltpu.make_async_remote_copy(
            self.land.at[f, self.chunk(f, 0)], self.zland.at[f], self.z_s.at[f], self.z_r.at[f],
            device_id=(self.place.z_far, self.place.tensor), device_id_type=MESH,
        )

    def keep(self, f):
        return pltpu.make_async_copy(
            self.total.at[f], self.out.at[f, self.chunk(f, 0)], self.keep_s.at[f]
        )

    def begin(self, f):
        self.rs(f, 0, self.first).start()

    def rs_step(self, s):
        for f in range(4):
            self.rs(f, s - 1, self.land).wait_recv()
            c = self.chunk(f, 1 + s)
            self.land[f, c] = self.land[f, c] + self.mine[f, c]
            self.rs(f, s, self.land).start()

    def turn(self):
        for f in range(4):
            self.rs(f, 14, self.land).wait_recv()
            c = self.chunk(f, 0)
            self.land[f, c] = self.land[f, c] + self.mine[f, c]
            self.zcopy(f).start()

    def back(self):
        for f in range(4):
            self.zcopy(f).wait_recv()
            self.total[f] = self.land[f, self.chunk(f, 0)] + self.zland[f]
            self.ag(f, 0, self.total.at[f]).start()
            self.keep(f).start()

    def ag_step(self, s):
        for f in range(4):
            held = self.out.at[f, self.chunk(f, s)]
            self.ag(f, s - 1, held).wait_recv()
            self.ag(f, s, held).start()

    def end(self):
        for f in range(4):
            self.ag(f, 14, self.total.at[f]).wait_recv()
            self.zcopy(f).wait_send()
            self.keep(f).wait()

    def drain(self, s):
        for f in range(4):
            self.rs(f, s, self.land).wait_send()
            self.ag(f, s, self.total.at[f]).wait_send()


class Sum4:
    def __init__(self, place, part, land1, land2, sems):
        self.place, self.part, self.land1, self.land2 = place, part, land1, land2
        self.s1, self.r1, self.s2, self.r2, self.s3, self.r3 = sems
        self.half = part.shape[0] // 2
        self.n = self.half // PIECES

    def local(self, k):
        return pl.ds(pl.multiple_of(k * self.n, self.n), self.n)

    def rows(self, k, core):
        return pl.ds(pl.multiple_of(core * self.half + k * self.n, self.n), self.n)

    def own(self, k):
        return self.rows(k, self.place.core)

    def other(self, k):
        return self.rows(k, 1 - self.place.core)

    def one(self, k):
        return pltpu.make_async_remote_copy(
            self.part.at[self.other(k)], self.land1.at[self.local(k)],
            self.s1.at[k], self.r1.at[k],
            device_id=(self.place.dp, self.place.buddy), device_id_type=MESH,
        )

    def two(self, k):
        return pltpu.make_async_remote_copy(
            self.land1.at[self.local(k)], self.land2.at[self.local(k)],
            self.s2.at[k], self.r2.at[k],
            device_id=(self.place.dp, self.place.z_near), device_id_type=MESH,
        )

    def three(self, k, src, dst):
        return pltpu.make_async_remote_copy(
            src, dst, self.s3.at[k], self.r3.at[k],
            device_id=(self.place.dp, self.place.buddy), device_id_type=MESH,
        )

    def begin(self):
        for k in range(PIECES):
            self.one(k).start()

    def middle(self, k):
        self.one(k).wait_recv()
        at = self.local(k)
        self.land1[at] = self.land1[at] + self.part[self.own(k)]
        self.two(k).start()

    def total(self, k):
        self.two(k).wait_recv()
        self.two(k).wait_send()
        at = self.local(k)
        return self.land1[at] + self.land2[at]


def greet(place, rings):
    barrier = pltpu.get_barrier_semaphore()
    peers = [(place.dp, place.buddy), (place.dp, place.z_near)]
    if rings:
        peers += [(q, place.tensor) for q in place.next + [place.z_far]]
    for peer in peers:
        pl.semaphore_signal(barrier, inc=1, device_id=peer, device_id_type=MESH)
    pl.semaphore_wait(barrier, len(peers))


def loop(low, high, body):
    def one(i, carry):
        body(i)
        return carry

    lax.fori_loop(low, high, one, 0)


def sum4_kernel(part, out, land1, land2, *sems):
    place = Place()
    greet(place, False)
    work = Sum4(place, part, land1, land2, sems)
    work.begin()
    loop(0, PIECES, work.middle)

    def finish(k):
        out[work.own(k)] = work.total(k)
        work.three(k, out.at[work.own(k)], out.at[work.own(k)]).start()

    loop(0, PIECES, finish)

    def close(k):
        work.three(k, out.at[work.own(k)], out.at[work.own(k)]).wait()
        work.one(k).wait_send()

    loop(0, PIECES, close)


def sum4(part):
    half = (part.shape[0] // 2, part.shape[1])
    return pl.pallas_call(
        sum4_kernel,
        out_shape=jax.ShapeDtypeStruct(part.shape, F32),
        in_specs=[VMEM],
        out_specs=VMEM,
        scratch_shapes=[pltpu.VMEM(half, F32)] * 2 + [DMA((PIECES,))] * 6,
        compiler_params=pltpu.CompilerParams(
            collective_id=1, has_side_effects=True, vmem_limit_bytes=32 << 20
        ),
    )(part)


def expert_kernel(
    hidden2, dy, w_gate, w_up, w_down, share, grads, dhidden2, out, hidden2_t
):
    step = pl.program_id(0)

    @pl.when(step == 0)
    def _():
        hidden2_t[...] = hidden2[...].T
        dhidden2[...] = jnp.zeros_like(dhidden2)
        out[...] = jnp.zeros_like(out)

    down_pair = w_down[...].reshape(256, 1024)
    dact_pair = dot_nt(dy[...], down_pair)
    acts = []
    for i in range(2):
        both_w = jnp.concatenate([w_gate[i], w_up[i]], 1)
        both = dot_nn(hidden2[...], both_w)
        gate, up = both[:, :128], both[:, 128:]
        sig = 1.0 / (1.0 + jnp.exp(-gate))
        silu = gate * sig
        weight = share[i]
        acts.append((silu * up * weight).astype(BF16))
        dact = dact_pair[:, 128 * i : 128 * i + 128] * weight
        dgate = (dact * up * (sig * (1.0 + gate * (1.0 - sig)))).astype(BF16)
        dup = (dact * silu).astype(BF16)
        dboth = jnp.concatenate([dgate, dup], 1)
        grad = dot_nn(hidden2_t[...], dboth)
        grads[i, :, 0:64] = grad[:, :128].reshape(16, 64, 128)
        grads[i, :, 64:128] = grad[:, 128:].reshape(16, 64, 128)
        dhidden2[...] += dot_nt(dboth, both_w)
    act_pair = jnp.concatenate(acts, 1)
    out[...] += dot_nn(act_pair, down_pair)
    down_grad = dot_tn(act_pair, dy[...])
    for i in range(2):
        for j in range(8):
            for half in range(2):
                at = 128 * i + 64 * half
                grads[i, 2 * j + half, 128:192] = down_grad[at : at + 64, 128 * j : 128 * j + 128]


def experts_part(hidden2, dy, w_gate, w_up, w_down, share):
    rows, width = hidden2.shape
    count = w_gate.shape[0]
    whole = pl.BlockSpec((rows, width), lambda p: (0, 0))
    return pl.pallas_call(
        expert_kernel,
        grid=(count // 2,),
        out_shape=(
            jax.ShapeDtypeStruct((count, 16, 192, 128), F32),
            jax.ShapeDtypeStruct((rows, width), F32),
            jax.ShapeDtypeStruct((rows, width), F32),
        ),
        in_specs=[
            whole,
            whole,
            pl.BlockSpec((2, width, 128), lambda p: (p, 0, 0)),
            pl.BlockSpec((2, width, 128), lambda p: (p, 0, 0)),
            pl.BlockSpec((2, 128, width), lambda p: (p, 0, 0)),
            pl.BlockSpec((2, rows, 1), lambda p: (p, 0, 0)),
        ],
        out_specs=(
            pl.BlockSpec((2, 16, 192, 128), lambda p: (p, 0, 0, 0)),
            whole,
            whole,
        ),
        scratch_shapes=[pltpu.VMEM((width, rows), BF16)],
        compiler_params=pltpu.CompilerParams(vmem_limit_bytes=48 << 20),
    )(hidden2, dy, w_gate, w_up, w_down, share)


def row_norm(values):
    inverse = lax.rsqrt(jnp.mean(values * values, -1, keepdims=True) + NORM_EPS)
    return values * inverse, inverse


def norm_back(gradient, scaled, inverse, gain_vec):
    scaled_grad = gradient * gain_vec
    inner_sum = jnp.mean(scaled_grad * scaled, -1, keepdims=True)
    return inverse * (scaled_grad - scaled * inner_sum)


def fold(values):
    return jnp.sum(values.reshape(-1, 8, values.shape[-1]), 0)


def back_kernel(
    grads, dhidden2, out_part, residual, tokens, dy, gain1, gain2, mixed, w_out, queries, keys,
    values, lse, seg_col, seg_row, cos_table, sin_table, hidden1, w_query, w_key, w_value,
    output, input_grad, grads_sum, attn_sum,
    mine, land, zland, total, attn, attn_land, attn_zland, attn_total,
    land1, land2, land3, dresidual, dhidden1, dqkv, gains, gains_in, *sems
):
    place = Place()
    greet(place, True)
    ring_sems, sems = sems[:7], sems[7:]
    attn_sems, sems = sems[:7], sems[7:]
    sum_sems, sems = sems[:6], sems[6:]
    load_sem, gain_s, gain_r = sems
    rings = [
        Ring(
            place, grads.at[u], mine.at[u], land.at[u], zland.at[u], total.at[u],
            grads_sum.at[u], [sem.at[u] for sem in ring_sems],
        )
        for u in range(2)
    ]
    attn_ring = Ring(
        place, attn, attn, attn_land, attn_zland, attn_total, attn_sum, attn_sems
    )
    sums = [
        Sum4(place, part, land1.at[i], land2.at[i], [sem.at[i] for sem in sum_sems])
        for i, part in enumerate((dhidden2, out_part, dhidden1))
    ]
    back2, forward2, back1 = sums

    back2.begin()
    for ring in rings:
        for f in range(4):
            ring.begin(f)
    loads = [pltpu.make_async_copy(grads.at[u], mine.at[u], load_sem.at[u]) for u in range(2)]
    for load in loads:
        load.start()
    gains[...] = jnp.zeros_like(gains)

    def step(s):
        for ring in rings:
            ring.rs_step(s)

    loop(0, PIECES, back2.middle)
    forward2.begin()
    for load in loads:
        load.wait()
    step(1)
    loop(0, PIECES, forward2.middle)
    step(2)

    def finish2(k):
        step(3 + k)
        d = back2.total(k)
        at = back2.own(k)
        scaled, inverse = row_norm(residual[at])
        gains[8:16] += fold(d * scaled)
        dresidual[at] = dy[at].astype(F32) + norm_back(d, scaled, inverse, gain2[...])
        back2.three(k, dresidual.at[at], dresidual.at[at]).start()

    loop(0, PIECES, finish2)

    def close2(k):
        at = back2.own(k)
        back2.three(k, dresidual.at[at], dresidual.at[at]).wait_recv()

    loop(0, PIECES, close2)

    dbranch = dresidual[...].astype(BF16)
    dmixed = dot_nt(dbranch, w_out[...]).astype(BF16)
    out_grad = dot_tn(mixed[...], dbranch)
    for j in range(8):
        piece = out_grad[:, 128 * j : 128 * j + 128].reshape(8, 32, 128)
        attn[j // 2, 8 * (j % 2) : 8 * (j % 2) + 8, 64:96] = piece
    attn[:, :, 96:104] = jnp.zeros((4, 16, 8, 128), F32)

    lane = lax.broadcasted_iota(jnp.int32, (512, 128), 1)
    first_half = lane % 64 < 32

    def unrotate(grad):
        swapped = jnp.where(first_half, pltpu.roll(grad, 96, 1), pltpu.roll(grad, 32, 1))
        return (grad * cos_table[...] + swapped * sin_table[...]).astype(BF16)

    dkeys, dvalues = [], []
    for g in range(2):
        key = keys[:, 64 * g : 64 * g + 64]
        value = values[:, 64 * g : 64 * g + 64]
        dkey = [0.0, 0.0]
        dvalue = [0.0, 0.0]
        dquery = []
        for h in (2 * g, 2 * g + 1):
            blocks = []
            for b in range(2):
                at = slice(256 * b, 256 * b + 256)
                until = 256 * b + 256
                query = queries[at, 64 * h : 64 * h + 64]
                dmix = dmixed[at, 64 * h : 64 * h + 64]
                raw = dot_nt(key[:until], query) * HD ** (-0.5)
                allowed = (seg_col[:until] == seg_row[:, at]) & (
                    lax.broadcasted_iota(jnp.int32, raw.shape, 0)
                    <= lax.broadcasted_iota(jnp.int32, raw.shape, 1) + 256 * b
                )
                probs = jnp.exp(jnp.where(allowed, raw, -1e30) - lse[h : h + 1, at])
                dprobs = dot_nt(value[:until], dmix)
                inner = jnp.sum(probs * dprobs, 0, keepdims=True)
                dscores = (probs * (dprobs - inner)).astype(BF16)
                dvalue_part = dot_nn(probs.astype(BF16), dmix)
                dkey_part = dot_nn(dscores, query)
                for t in range(b + 1):
                    dvalue[t] = dvalue[t] + dvalue_part[256 * t : 256 * t + 256]
                    dkey[t] = dkey[t] + dkey_part[256 * t : 256 * t + 256]
                blocks.append(dot_tn(dscores, key[:until]))
            dquery.append(jnp.concatenate(blocks, 0) * HD ** (-0.5))
            step(7 + h)
        dqkv[:, 128 * g : 128 * g + 128] = unrotate(jnp.concatenate(dquery, 1))
        dkeys.append(jnp.concatenate(dkey, 0) * HD ** (-0.5))
        dvalues.append(jnp.concatenate(dvalue, 0))
    dqkv[:, 256:384] = unrotate(jnp.concatenate(dkeys, 1))
    dqkv[:, 384:512] = jnp.concatenate(dvalues, 1).astype(BF16)

    dhidden1[...] = (
        dot_nt(dqkv[:, :256], w_query[...])
        + dot_nt(dqkv[:, 256:384], w_key[...])
        + dot_nt(dqkv[:, 384:512], w_value[...])
    )
    back1.begin()
    step(11)

    def finish_out(k):
        done = forward2.total(k) + residual[forward2.own(k)]
        at = forward2.local(k)
        output[forward2.own(k)] = done.astype(BF16)
        forward2.land1[at] = done
        forward2.three(k, forward2.land1.at[at], land3.at[at]).start()

    loop(0, PIECES, finish_out)
    loop(0, PIECES, back1.middle)
    step(12)
    hidden_grad = dot_tn(hidden1[...], dqkv[...])
    for j in range(4):
        piece = hidden_grad[:, 128 * j : 128 * j + 128].reshape(4, 16, 16, 128)
        attn[:, :, 16 * j : 16 * j + 16] = piece
    step(13)
    step(14)
    for ring in rings:
        ring.turn()

    def close_out(k):
        at = forward2.local(k)
        forward2.three(k, forward2.land1.at[at], land3.at[at]).wait_recv()
        output[forward2.other(k)] = land3[at].astype(BF16)

    loop(0, PIECES, close_out)
    for ring in rings:
        ring.back()

    def finish1(k):
        d = back1.total(k)
        at = back1.own(k)
        scaled, inverse = row_norm(tokens[at].astype(F32))
        gains[0:8] += fold(d * scaled)
        input_grad[at] = dresidual[at] + norm_back(d, scaled, inverse, gain1[...])
        back1.three(k, input_grad.at[at], input_grad.at[at]).start()

    loop(0, PIECES, finish1)
    swap = pltpu.make_async_remote_copy(
        gains, gains_in, gain_s, gain_r,
        device_id=(place.dp, place.buddy), device_id_type=MESH,
    )
    swap.start()
    for ring in rings:
        ring.ag_step(1)
    swap.wait_recv()
    for j in range(16):
        rows = slice(8 * (j // 8), 8 * (j // 8) + 8)
        lanes = slice(128 * (j % 8), 128 * (j % 8) + 128)
        attn[0, j, 96:104] = gains[rows, lanes] + gains_in[rows, lanes]
    for f in range(4):
        attn_ring.begin(f)

    def both(s):
        for ring in rings:
            ring.ag_step(s)
        attn_ring.rs_step(s - 1)

    loop(2, 15, both)
    attn_ring.rs_step(14)
    attn_ring.turn()
    for ring in rings:
        ring.end()
    attn_ring.back()
    loop(1, 15, attn_ring.ag_step)
    attn_ring.end()

    def drain(s):
        for ring in rings + [attn_ring]:
            ring.drain(s)

    loop(0, 15, drain)
    swap.wait_send()

    def close(k):
        for work in sums:
            work.one(k).wait_send()
        at = back2.own(k)
        back2.three(k, dresidual.at[at], dresidual.at[at]).wait_send()
        here = forward2.local(k)
        forward2.three(k, forward2.land1.at[here], land3.at[here]).wait_send()
        back1.three(k, input_grad.at[at], input_grad.at[at]).wait()

    loop(0, PIECES, close)


def back_part(grads, *rest):
    rows, width = rest[0].shape
    half = (rows // 2, width)
    m, n = grads.shape[3], 104
    S = pltpu.VMEM
    ring_sems = [DMA((2, 4, 15))] * 4 + [DMA((2, 4))] * 3
    attn_sems = [DMA((4, 15))] * 4 + [DMA((4,))] * 3
    return pl.pallas_call(
        back_kernel,
        out_shape=(
            jax.ShapeDtypeStruct((rows, width), BF16),
            jax.ShapeDtypeStruct((rows, width), F32),
            jax.ShapeDtypeStruct(grads.shape, F32),
            jax.ShapeDtypeStruct((4, 16, n, 128), F32),
        ),
        in_specs=[ANY] + [VMEM] * len(rest),
        out_specs=(VMEM, VMEM, ANY, ANY),
        scratch_shapes=[
            S(grads.shape, F32), S(grads.shape, F32), S((2, 4, m, 128), F32),
            S((2, 4, m, 128), F32),
            S((4, 16, n, 128), F32), S((4, 16, n, 128), F32), S((4, n, 128), F32),
            S((4, n, 128), F32),
            S((3,) + half, F32), S((3,) + half, F32), S(half, F32),
            S((rows, width), F32), S((rows, width), F32), S((rows, 512), BF16),
            S((16, width), F32), S((16, width), F32),
        ]
        + ring_sems
        + attn_sems
        + [DMA((3, PIECES))] * 6
        + [DMA((2,)), DMA, DMA],
        compiler_params=pltpu.CompilerParams(
            collective_id=2, has_side_effects=True, vmem_limit_bytes=63 << 20
        ),
    )(grads, *rest)


def tables(seq_count, seq_length, head_width):
    half_width = head_width // 2
    frequency = ROPE_THETA ** (-jnp.arange(half_width, dtype=jnp.float32) * 2.0 / head_width)
    position = jnp.tile(jnp.arange(seq_length), seq_count).astype(jnp.float32)
    angles = position[:, None] * frequency[None, :]
    return (jnp.cos(angles), jnp.sin(angles))


def rotate(values, cos_table, sin_table):
    half_width = values.shape[-1] // 2
    first_half = values[..., :half_width]
    second_half = values[..., half_width:]
    return jnp.concatenate(
        [
            first_half * cos_table - second_half * sin_table,
            second_half * cos_table + first_half * sin_table,
        ],
        -1,
    )


def local(
    tokens,
    norm1_gain,
    w_query,
    w_key,
    w_value,
    w_out,
    norm2_gain,
    expert_gate,
    expert_up,
    expert_down,
    routes,
    gate_weights,
    segments,
    cotangent,
):
    seq_count, seq_length = segments.shape
    tok_rows = tokens.shape[0]
    head_count = w_query.shape[1] // HD
    groups = w_key.shape[1] // HD
    group_size = head_count // groups
    experts = expert_gate.shape[0]
    cos_half, sin_half = tables(seq_count, seq_length, HD)
    cos_table, sin_table = cos_half[:, None, :], sin_half[:, None, :]
    inputs = tokens.astype(F32)
    scaled1, inverse1 = row_norm(inputs)
    hidden1 = (scaled1 * norm1_gain).astype(BF16)
    queries = rotate(
        dot_nn(hidden1, w_query).reshape(tok_rows, head_count, HD), cos_table, sin_table
    ).astype(BF16)
    keys = rotate(
        dot_nn(hidden1, w_key).reshape(tok_rows, groups, HD), cos_table, sin_table
    ).astype(BF16)
    values = dot_nn(hidden1, w_value).astype(BF16)
    query_blocks = queries.reshape(seq_count, seq_length, groups, group_size, HD)
    key_blocks = keys.reshape(seq_count, seq_length, groups, HD)
    value_blocks = values.reshape(seq_count, seq_length, groups, HD)
    raw_scores = jnp.einsum(
        "bqngd,bknd->bngqk", query_blocks, key_blocks, preferred_element_type=F32
    ) * HD ** (-0.5)
    position = jnp.arange(seq_length)
    allowed = (segments[:, :, None] == segments[:, None, :]) & (
        position[:, None] >= position[None, :]
    )
    scores = jnp.where(allowed[:, None, None, :, :], raw_scores, -1e30)
    row_max = jnp.max(scores, -1, keepdims=True)
    weights = jnp.exp(scores - row_max)
    row_total = jnp.sum(weights, -1, keepdims=True)
    probabilities = weights / row_total
    log_total = (row_max + jnp.log(row_total)).reshape(head_count, tok_rows)
    mixed_heads = jnp.einsum(
        "bngqk,bknd->bqngd",
        probabilities.astype(BF16),
        value_blocks,
        preferred_element_type=F32,
    )
    mixed_heads = mixed_heads.reshape(tok_rows, head_count * HD).astype(BF16)
    residual = inputs + sum4(dot_nn(mixed_heads, w_out))
    hidden2 = (row_norm(residual)[0] * norm2_gain).astype(BF16)
    picked = (routes[:, :, None] == jnp.arange(experts)[None, None, :]).astype(F32)
    expert_share = jnp.sum(gate_weights[:, :, None] * picked, 1).T[:, :, None]
    expert_grads, dhidden2, out_part = experts_part(
        hidden2, cotangent, expert_gate, expert_up, expert_down, expert_share
    )
    output, input_grad, grads, attn = back_part(
        expert_grads.reshape(2, 4, 16, 192, 128),
        dhidden2,
        out_part,
        residual,
        tokens,
        cotangent,
        norm1_gain[None],
        norm2_gain[None],
        mixed_heads,
        w_out,
        queries.reshape(tok_rows, -1),
        keys.reshape(tok_rows, -1),
        values,
        log_total,
        segments.reshape(tok_rows, 1),
        segments,
        jnp.tile(cos_half, (1, 4)),
        jnp.tile(jnp.concatenate([sin_half, -sin_half], 1), (1, 2)),
        hidden1,
        w_query,
        w_key,
        w_value,
    )
    grads = grads.reshape(experts, 16, 192, 128)
    gate_grad = grads[:, :, 0:64].reshape(experts, -1, 128)
    up_grad = grads[:, :, 64:128].reshape(experts, -1, 128)
    down_grad = grads[:, :, 128:192].reshape(experts, 8, 128, 128)
    down_grad = down_grad.transpose(0, 2, 1, 3).reshape(experts, 128, -1)
    attn = attn.reshape(64, 104, 128)
    query_grad = jnp.concatenate(
        [attn[:, 0:16].reshape(-1, 128), attn[:, 16:32].reshape(-1, 128)], 1
    )
    key_grad = attn[:, 32:48].reshape(-1, 128)
    value_grad = attn[:, 48:64].reshape(-1, 128)
    out_grad = attn[:, 64:96].reshape(8, 256, 128).transpose(1, 0, 2).reshape(256, -1)
    gain1_grad = jnp.sum(attn[0:8, 96:104], 1).reshape(-1)
    gain2_grad = jnp.sum(attn[8:16, 96:104], 1).reshape(-1)
    return (
        output,
        input_grad,
        gain1_grad,
        query_grad,
        key_grad,
        value_grad,
        out_grad,
        gain2_grad,
        gate_grad,
        up_grad,
        down_grad,
    )


def solution(mesh):
    return jax.shard_map(
        local,
        mesh=mesh,
        in_specs=(
            P("dp", None),
            P(),
            P(None, "tensor"),
            P(None, "tensor"),
            P(None, "tensor"),
            P("tensor", None),
            P(),
            P(None, None, "tensor"),
            P(None, None, "tensor"),
            P(None, "tensor", None),
            P("dp", None),
            P("dp", None),
            P("dp", None),
            P("dp", None),
        ),
        out_specs=(
            P("dp", None),
            P("dp", None),
            P(),
            P(None, "tensor"),
            P(None, "tensor"),
            P(None, "tensor"),
            P("tensor", None),
            P(),
            P(None, None, "tensor"),
            P(None, None, "tensor"),
            P(None, "tensor", None),
        ),
        check_vma=False,
    )
```

```python
import functools

import jax
import jax.numpy as jnp
from jax import lax
from jax.experimental import pallas as pl
from jax.experimental.pallas import tpu as pltpu
from jax.sharding import PartitionSpec as P

MESH = pl.DeviceIdType.MESH
DMA = pltpu.SemaphoreType.DMA
F32 = jnp.float32
BF16 = jnp.bfloat16

HD = 64
NORM_EPS = 1e-06
ROPE_THETA = 10000.0
FLOWS = ((0, 1), (0, -1), (1, 1), (1, -1))
PIECES = 4
VMEM = pl.BlockSpec(memory_space=pltpu.VMEM)
ANY = pl.BlockSpec(memory_space=pl.ANY)


def dot_nn(first_op, second_op):
    return jnp.dot(first_op, second_op, preferred_element_type=F32)


def dot_tn(first_op, second_op):
    return lax.dot_general(
        first_op, second_op, (((0,), (0,)), ((), ())), preferred_element_type=F32
    )


def dot_nt(first_op, second_op):
    return lax.dot_general(
        first_op, second_op, (((1,), (1,)), ((), ())), preferred_element_type=F32
    )


def ring_pos(dp):
    xy = dp // 2
    x, y = xy % 4, xy // 4
    turn = (x + y) % 4
    return 4 * y + turn, 4 * x + turn


def ring_dp(kind, pos, zhi):
    along = pos // 4
    across = (pos % 4 - along + 4) % 4
    x, y = (across, along) if kind == 0 else (along, across)
    return (y * 4 + x) * 2 + zhi


class Place:
    def __init__(self):
        self.dp = lax.axis_index("dp")
        self.tensor = lax.axis_index("tensor")
        zhi = self.dp % 2
        self.z_far = self.dp + 1 - 2 * zhi
        self.pos = ring_pos(self.dp)
        self.next = [
            ring_dp(kind, (self.pos[kind] + step + 16) % 16, zhi) for kind, step in FLOWS
        ]
        xy = self.dp // 2
        x, y = xy % 4, xy // 4
        self.x, self.y = x, y

        def at(dx, dy):
            return (((y + dy + 4) % 4) * 4 + (x + dx + 4) % 4) * 2 + zhi

        self.across = [at(1, 0), at(-1, 0), at(0, 1), at(0, -1)]
        self.pairs = [
            at(1 - 2 * (x % 2), 0), at(2, 0), at(0, 1 - 2 * (y % 2)), at(0, 2), self.z_far
        ]
        self.core = self.tensor % 2
        self.buddy = self.tensor + 1 - 2 * self.core
        self.z_near = self.tensor + 2 - 4 * (self.tensor // 2)


class Ring:
    def __init__(self, place, first, mine, land, zland, total, out, sems):
        self.place, self.first, self.mine, self.land = place, first, mine, land
        self.zland, self.total, self.out = zland, total, out
        self.rs_s, self.rs_r, self.ag_s, self.ag_r, self.z_s, self.z_r, self.keep_s = sems

    def chunk(self, f, back):
        kind, step = FLOWS[f]
        return (self.place.pos[kind] - step * back + 32) % 16

    def rs(self, f, s, src):
        c = self.chunk(f, 1 + s)
        return pltpu.make_async_remote_copy(
            src.at[f, c], self.land.at[f, c], self.rs_s.at[f, s], self.rs_r.at[f, s],
            device_id=(self.place.next[f], self.place.tensor), device_id_type=MESH,
        )

    def ag(self, f, s, src):
        return pltpu.make_async_remote_copy(
            src, self.out.at[f, self.chunk(f, s)], self.ag_s.at[f, s], self.ag_r.at[f, s],
            device_id=(self.place.next[f], self.place.tensor), device_id_type=MESH,
        )

    def zcopy(self, f):
        return pltpu.make_async_remote_copy(
            self.land.at[f, self.chunk(f, 0)], self.zland.at[f], self.z_s.at[f], self.z_r.at[f],
            device_id=(self.place.z_far, self.place.tensor), device_id_type=MESH,
        )

    def keep(self, f):
        return pltpu.make_async_copy(
            self.total.at[f], self.out.at[f, self.chunk(f, 0)], self.keep_s.at[f]
        )

    def begin(self, f):
        self.rs(f, 0, self.first).start()

    def rs_step(self, s):
        for f in range(4):
            self.rs(f, s - 1, self.land).wait_recv()
            c = self.chunk(f, 1 + s)
            self.land[f, c] = self.land[f, c] + self.mine[f, c]
            self.rs(f, s, self.land).start()

    def turn(self):
        for f in range(4):
            self.rs(f, 14, self.land).wait_recv()
            c = self.chunk(f, 0)
            self.land[f, c] = self.land[f, c] + self.mine[f, c]
            self.zcopy(f).start()

    def back(self):
        for f in range(4):
            self.zcopy(f).wait_recv()
            self.total[f] = self.land[f, self.chunk(f, 0)] + self.zland[f]
            self.ag(f, 0, self.total.at[f]).start()
            self.keep(f).start()

    def ag_step(self, s):
        for f in range(4):
            held = self.out.at[f, self.chunk(f, s)]
            self.ag(f, s - 1, held).wait_recv()
            self.ag(f, s, held).start()

    def end(self):
        for f in range(4):
            self.ag(f, 14, self.total.at[f]).wait_recv()
            self.zcopy(f).wait_send()
            self.keep(f).wait()

    def drain(self, s):
        for f in range(4):
            self.rs(f, s, self.land).wait_send()
            self.ag(f, s, self.total.at[f]).wait_send()


class AxisRing:
    def __init__(self, place, mine, land, land2, zland, total, out, sems):
        self.place, self.mine, self.land, self.land2 = place, mine, land, land2
        self.zland, self.total, self.out, self.sems = zland, total, out, sems

    def spots(self, f, back1, back2):
        step = 1 - 2 * (f % 2)
        pos1, pos2 = self.place.x, self.place.y
        if f >= 2:
            pos1, pos2 = pos2, pos1
        return (pos1 - step * back1 + 8) % 4, (pos2 - step * back2 + 8) % 4

    def send(self, f, s, stage, src, dst):
        axis = f // 2 if stage in (0, 3) else 1 - f // 2
        return pltpu.make_async_remote_copy(
            src, dst, self.sems[2 * stage].at[f, s], self.sems[2 * stage + 1].at[f, s],
            device_id=(self.place.across[2 * axis + f % 2], self.place.tensor),
            device_id_type=MESH,
        )

    def rs1(self, f, s, src):
        i = self.spots(f, 1 + s, 0)[0]
        return self.send(f, s, 0, src.at[f, i], self.land.at[f, i])

    def rs2(self, f, s, src):
        j = self.spots(f, 0, 1 + s)[1]
        return self.send(f, s, 1, src.at[j], self.land2.at[f, j])

    def ag2(self, f, s, src):
        i, j = self.spots(f, 0, s)
        return self.send(f, s, 2, src, self.out.at[f, i, j])

    def ag1(self, f, s, src):
        return self.send(f, s, 3, src, self.out.at[f, self.spots(f, s, 0)[0]])

    def zcopy(self, f):
        return pltpu.make_async_remote_copy(
            self.land2.at[f, self.spots(f, 0, 0)[1]], self.zland.at[f],
            self.sems[8].at[f], self.sems[9].at[f],
            device_id=(self.place.z_far, self.place.tensor), device_id_type=MESH,
        )

    def keep(self, f):
        i, j = self.spots(f, 0, 0)
        return pltpu.make_async_copy(
            self.total.at[f], self.out.at[f, i, j], self.sems[10].at[f]
        )

    def begin(self):
        for f in range(4):
            self.rs1(f, 0, self.mine).start()

    def rs1_step(self, s):
        for f in range(4):
            self.rs1(f, s - 1, self.land).wait_recv()
            i = self.spots(f, 1 + s, 0)[0]
            self.land[f, i] = self.land[f, i] + self.mine[f, i]
            if s < 3:
                self.rs1(f, s, self.land).start()
            else:
                self.rs2(f, 0, self.land.at[f, i]).start()

    def rs2_step(self, s):
        for f in range(4):
            i, j = self.spots(f, 0, 1 + s)
            self.rs2(f, s - 1, self.land2.at[f]).wait_recv()
            self.land2[f, j] = self.land2[f, j] + self.land[f, i, j]
            if s < 3:
                self.rs2(f, s, self.land2.at[f]).start()
            else:
                self.zcopy(f).start()

    def back(self):
        for f in range(4):
            self.zcopy(f).wait_recv()
            self.total[f] = self.land2[f, self.spots(f, 0, 0)[1]] + self.zland[f]
            self.ag2(f, 0, self.total.at[f]).start()
            self.keep(f).start()

    def ag2_step(self, s):
        for f in range(4):
            self.ag2(f, s - 1, self.total.at[f]).wait_recv()
            i, j = self.spots(f, 0, s)
            if s < 3:
                self.ag2(f, s, self.out.at[f, i, j]).start()
            else:
                self.keep(f).wait()
                self.ag1(f, 0, self.out.at[f, i]).start()

    def ag1_step(self, s):
        for f in range(4):
            held = self.out.at[f, self.spots(f, s, 0)[0]]
            self.ag1(f, s - 1, held).wait_recv()
            if s < 3:
                self.ag1(f, s, held).start()

    def drain(self, s):
        for f in range(4):
            self.rs1(f, s, self.land).wait_send()
            self.rs2(f, s, self.land2.at[f]).wait_send()
            self.ag2(f, s, self.total.at[f]).wait_send()
            self.ag1(f, s, self.out.at[f, 0]).wait_send()

    def close(self):
        for f in range(4):
            self.zcopy(f).wait_send()


class Sum4:
    def __init__(self, place, part, land1, land2, sems):
        self.place, self.part, self.land1, self.land2 = place, part, land1, land2
        self.s1, self.r1, self.s2, self.r2, self.s3, self.r3 = sems
        self.half = part.shape[0] // 2
        self.n = self.half // PIECES

    def local(self, k):
        return pl.ds(pl.multiple_of(k * self.n, self.n), self.n)

    def rows(self, k, core):
        return pl.ds(pl.multiple_of(core * self.half + k * self.n, self.n), self.n)

    def own(self, k):
        return self.rows(k, self.place.core)

    def other(self, k):
        return self.rows(k, 1 - self.place.core)

    def one(self, k):
        return pltpu.make_async_remote_copy(
            self.part.at[self.other(k)], self.land1.at[self.local(k)],
            self.s1.at[k], self.r1.at[k],
            device_id=(self.place.dp, self.place.buddy), device_id_type=MESH,
        )

    def two(self, k):
        return pltpu.make_async_remote_copy(
            self.land1.at[self.local(k)], self.land2.at[self.local(k)],
            self.s2.at[k], self.r2.at[k],
            device_id=(self.place.dp, self.place.z_near), device_id_type=MESH,
        )

    def three(self, k, src, dst):
        return pltpu.make_async_remote_copy(
            src, dst, self.s3.at[k], self.r3.at[k],
            device_id=(self.place.dp, self.place.buddy), device_id_type=MESH,
        )

    def begin(self):
        for k in range(PIECES):
            self.one(k).start()

    def middle(self, k):
        self.one(k).wait_recv()
        at = self.local(k)
        self.land1[at] = self.land1[at] + self.part[self.own(k)]
        self.two(k).start()

    def total(self, k):
        self.two(k).wait_recv()
        self.two(k).wait_send()
        at = self.local(k)
        return self.land1[at] + self.land2[at]


def greet(place, rings):
    barrier = pltpu.get_barrier_semaphore()
    peers = [(place.dp, place.buddy), (place.dp, place.z_near)]
    if rings:
        peers += [(q, place.tensor) for q in place.across + [place.z_far]]
        peers += [(place.pairs[1], place.tensor), (place.pairs[3], place.tensor)]
    for peer in peers:
        pl.semaphore_signal(barrier, inc=1, device_id=peer, device_id_type=MESH)
    pl.semaphore_wait(barrier, len(peers))


def loop(low, high, body):
    def one(i, carry):
        body(i)
        return carry

    lax.fori_loop(low, high, one, 0)


def sum4_kernel(part, out, land1, land2, *sems):
    place = Place()
    greet(place, False)
    work = Sum4(place, part, land1, land2, sems)
    work.begin()
    loop(0, PIECES, work.middle)

    def finish(k):
        out[work.own(k)] = work.total(k)
        work.three(k, out.at[work.own(k)], out.at[work.own(k)]).start()

    loop(0, PIECES, finish)

    def close(k):
        work.three(k, out.at[work.own(k)], out.at[work.own(k)]).wait()
        work.one(k).wait_send()

    loop(0, PIECES, close)


def sum4(part):
    half = (part.shape[0] // 2, part.shape[1])
    return pl.pallas_call(
        sum4_kernel,
        out_shape=jax.ShapeDtypeStruct(part.shape, F32),
        in_specs=[VMEM],
        out_specs=VMEM,
        scratch_shapes=[pltpu.VMEM(half, F32)] * 2 + [DMA((PIECES,))] * 6,
        compiler_params=pltpu.CompilerParams(
            collective_id=1, has_side_effects=True, vmem_limit_bytes=32 << 20
        ),
    )(part)


def expert_kernel(
    hidden2, dy, w_gate, w_up, w_down, share, grads, dhidden2, out, hidden2_t
):
    step = pl.program_id(0)

    @pl.when(step == 0)
    def _():
        hidden2_t[...] = hidden2[...].T
        dhidden2[...] = jnp.zeros_like(dhidden2)
        out[...] = jnp.zeros_like(out)

    down_pair = w_down[...].reshape(256, 1024)
    dact_pair = dot_nt(dy[...], down_pair)
    acts = []
    for i in range(2):
        both_w = jnp.concatenate([w_gate[i], w_up[i]], 1)
        both = dot_nn(hidden2[...], both_w)
        gate, up = both[:, :128], both[:, 128:]
        sig = 1.0 / (1.0 + jnp.exp(-gate))
        silu = gate * sig
        weight = share[i]
        acts.append((silu * up * weight).astype(BF16))
        dact = dact_pair[:, 128 * i : 128 * i + 128] * weight
        dgate = (dact * up * (sig * (1.0 + gate * (1.0 - sig)))).astype(BF16)
        dup = (dact * silu).astype(BF16)
        dboth = jnp.concatenate([dgate, dup], 1)
        grad = dot_nn(hidden2_t[...], dboth)
        grads[i, :, 0:64] = grad[:, :128].reshape(16, 64, 128)
        grads[i, :, 64:128] = grad[:, 128:].reshape(16, 64, 128)
        dhidden2[...] += dot_nt(dboth, both_w)
    act_pair = jnp.concatenate(acts, 1)
    out[...] += dot_nn(act_pair, down_pair)
    down_grad = dot_tn(act_pair, dy[...])
    for i in range(2):
        for j in range(8):
            for half in range(2):
                at = 128 * i + 64 * half
                grads[i, 2 * j + half, 128:192] = down_grad[at : at + 64, 128 * j : 128 * j + 128]


def experts_part(hidden2, dy, w_gate, w_up, w_down, share):
    rows, width = hidden2.shape
    count = w_gate.shape[0]
    whole = pl.BlockSpec((rows, width), lambda p: (0, 0))
    return pl.pallas_call(
        expert_kernel,
        grid=(count // 2,),
        out_shape=(
            jax.ShapeDtypeStruct((count, 16, 192, 128), F32),
            jax.ShapeDtypeStruct((rows, width), F32),
            jax.ShapeDtypeStruct((rows, width), F32),
        ),
        in_specs=[
            whole,
            whole,
            pl.BlockSpec((2, width, 128), lambda p: (p, 0, 0)),
            pl.BlockSpec((2, width, 128), lambda p: (p, 0, 0)),
            pl.BlockSpec((2, 128, width), lambda p: (p, 0, 0)),
            pl.BlockSpec((2, rows, 1), lambda p: (p, 0, 0)),
        ],
        out_specs=(
            pl.BlockSpec((2, 16, 192, 128), lambda p: (p, 0, 0, 0)),
            whole,
            whole,
        ),
        scratch_shapes=[pltpu.VMEM((width, rows), BF16)],
        compiler_params=pltpu.CompilerParams(vmem_limit_bytes=48 << 20),
    )(hidden2, dy, w_gate, w_up, w_down, share)


def row_norm(values):
    inverse = lax.rsqrt(jnp.mean(values * values, -1, keepdims=True) + NORM_EPS)
    return values * inverse, inverse


def norm_back(gradient, scaled, inverse, gain_vec):
    scaled_grad = gradient * gain_vec
    inner_sum = jnp.mean(scaled_grad * scaled, -1, keepdims=True)
    return inverse * (scaled_grad - scaled * inner_sum)


def fold(values):
    return jnp.sum(values.reshape(-1, 8, values.shape[-1]), 0)


def back_kernel(
    grads, dhidden2, out_part, residual, tokens, dy, gain1, gain2, mixed, w_out, queries, keys,
    values, lse, seg_col, seg_row, cos_table, sin_table, hidden1, w_query, w_key, w_value,
    output, input_grad, gain_sums, grads_sum, attn_sum,
    mine, land, zland, total, attn, attn_land, attn_land2, attn_zland, attn_total,
    land1, land2, land3, dresidual, dhidden1, dqkv, folded, gains, gains_in, *sems
):
    place = Place()
    greet(place, True)
    ring_sems, sems = sems[:7], sems[7:]
    attn_sems, sems = sems[:11], sems[11:]
    sum_sems, sems = sems[:6], sems[6:]
    load_sem, gain_s, gain_r = sems
    rings = [
        Ring(
            place, grads.at[u], mine.at[u], land.at[u], zland.at[u], total.at[u],
            grads_sum.at[u], [sem.at[u] for sem in ring_sems],
        )
        for u in range(2)
    ]
    attn_ring = AxisRing(
        place, attn, attn_land, attn_land2, attn_zland, attn_total, attn_sum, attn_sems
    )
    sums = [
        Sum4(place, part, land1.at[i], land2.at[i], [sem.at[i] for sem in sum_sems])
        for i, part in enumerate((dhidden2, out_part, dhidden1))
    ]
    back2, forward2, back1 = sums

    back2.begin()
    for ring in rings:
        for f in range(4):
            ring.begin(f)
    loads = [pltpu.make_async_copy(grads.at[u], mine.at[u], load_sem.at[u]) for u in range(2)]
    for load in loads:
        load.start()
    folded[...] = jnp.zeros_like(folded)

    def step(s):
        for ring in rings:
            ring.rs_step(s)

    def gather(s):
        for ring in rings:
            ring.ag_step(s)

    loop(0, PIECES, back2.middle)
    for load in loads:
        load.wait()
    step(1)

    def finish2(k):
        step(2 + k)
        d = back2.total(k)
        at = back2.own(k)
        scaled, inverse = row_norm(residual[at])
        folded[8:16] += fold(d * scaled)
        dresidual[at] = dy[at].astype(F32) + norm_back(d, scaled, inverse, gain2[...])
        back2.three(k, dresidual.at[at], dresidual.at[at]).start()

    loop(0, PIECES, finish2)

    def close2(k):
        at = back2.own(k)
        back2.three(k, dresidual.at[at], dresidual.at[at]).wait_recv()

    loop(0, PIECES, close2)

    dbranch = dresidual[...].astype(BF16)
    dmixed = dot_nt(dbranch, w_out[...]).astype(BF16)
    out_grad = dot_tn(mixed[...], dbranch)
    for j in range(8):
        piece = out_grad[:, 128 * j : 128 * j + 128].reshape(2, 4, 32, 128)
        attn[j // 2, 2 * (j % 2) : 2 * (j % 2) + 2, :, 64:96] = piece

    lane = lax.broadcasted_iota(jnp.int32, (512, 128), 1)
    first_half = lane % 64 < 32

    def unrotate(grad):
        swapped = jnp.where(first_half, pltpu.roll(grad, 96, 1), pltpu.roll(grad, 32, 1))
        return (grad * cos_table[...] + swapped * sin_table[...]).astype(BF16)

    dkeys, dvalues = [], []
    for g in range(2):
        key = keys[:, 64 * g : 64 * g + 64]
        value = values[:, 64 * g : 64 * g + 64]
        dkey = [0.0, 0.0]
        dvalue = [0.0, 0.0]
        dquery = []
        for h in (2 * g, 2 * g + 1):
            blocks = []
            for b in range(2):
                at = slice(256 * b, 256 * b + 256)
                until = 256 * b + 256
                query = queries[at, 64 * h : 64 * h + 64]
                dmix = dmixed[at, 64 * h : 64 * h + 64]
                raw = dot_nt(key[:until], query) * HD ** (-0.5)
                allowed = (seg_col[:until] == seg_row[:, at]) & (
                    lax.broadcasted_iota(jnp.int32, raw.shape, 0)
                    <= lax.broadcasted_iota(jnp.int32, raw.shape, 1) + 256 * b
                )
                probs = jnp.exp(jnp.where(allowed, raw, -1e30) - lse[h : h + 1, at])
                dprobs = dot_nt(value[:until], dmix)
                inner = jnp.sum(probs * dprobs, 0, keepdims=True)
                dscores = (probs * (dprobs - inner)).astype(BF16)
                dvalue_part = dot_nn(probs.astype(BF16), dmix)
                dkey_part = dot_nn(dscores, query)
                for t in range(b + 1):
                    dvalue[t] = dvalue[t] + dvalue_part[256 * t : 256 * t + 256]
                    dkey[t] = dkey[t] + dkey_part[256 * t : 256 * t + 256]
                blocks.append(dot_tn(dscores, key[:until]))
                step(6 + 2 * h + b)
            dquery.append(jnp.concatenate(blocks, 0) * HD ** (-0.5))
        dqkv[:, 128 * g : 128 * g + 128] = unrotate(jnp.concatenate(dquery, 1))
        dkeys.append(jnp.concatenate(dkey, 0) * HD ** (-0.5))
        dvalues.append(jnp.concatenate(dvalue, 0))
    dqkv[:, 256:384] = unrotate(jnp.concatenate(dkeys, 1))
    dqkv[:, 384:512] = jnp.concatenate(dvalues, 1).astype(BF16)

    hidden_grad = dot_tn(hidden1[...], dqkv[...])
    for j in range(4):
        piece = hidden_grad[:, 128 * j : 128 * j + 128].reshape(4, 4, 4, 16, 128)
        attn[:, :, :, 16 * j : 16 * j + 16] = piece
    attn_ring.begin()
    step(14)
    for ring in rings:
        ring.turn()
    dhidden1[...] = (
        dot_nt(dqkv[:, :256], w_query[...])
        + dot_nt(dqkv[:, 256:384], w_key[...])
        + dot_nt(dqkv[:, 384:512], w_value[...])
    )
    back1.begin()
    attn_ring.rs1_step(1)
    loop(0, PIECES, back1.middle)
    forward2.begin()
    attn_ring.rs1_step(2)
    for ring in rings:
        ring.back()
    loop(0, PIECES, forward2.middle)
    gather(1)
    attn_ring.rs1_step(3)
    gather(2)
    attn_ring.rs2_step(1)

    def finish1(k):
        gather(3 + k)
        d = back1.total(k)
        at = back1.own(k)
        scaled, inverse = row_norm(tokens[at].astype(F32))
        folded[0:8] += fold(d * scaled)
        input_grad[at] = dresidual[at] + norm_back(d, scaled, inverse, gain1[...])
        back1.three(k, input_grad.at[at], input_grad.at[at]).start()

    loop(0, 2, finish1)
    attn_ring.rs2_step(2)
    loop(2, PIECES, finish1)
    attn_ring.rs2_step(3)
    gains[0] = jnp.concatenate(
        [
            jnp.sum(folded[0:8], 0, keepdims=True),
            jnp.sum(folded[8:16], 0, keepdims=True),
            jnp.zeros((6, gains.shape[2]), F32),
        ],
        0,
    )

    def swap(i):
        device = (place.dp, place.buddy) if i == 0 else (place.pairs[i - 1], place.tensor)
        return pltpu.make_async_remote_copy(
            gains.at[i], gains_in.at[i], gain_s.at[i], gain_r.at[i],
            device_id=device, device_id_type=MESH,
        )

    def add_swap(i):
        swap(i).wait_recv()
        gains[i + 1] = gains[i] + gains_in[i]

    def finish_out(k):
        done = forward2.total(k) + residual[forward2.own(k)]
        at = forward2.local(k)
        output[forward2.own(k)] = done.astype(BF16)
        forward2.land1[at] = done
        forward2.three(k, forward2.land1.at[at], land3.at[at]).start()

    def close_out(k):
        at = forward2.local(k)
        forward2.three(k, forward2.land1.at[at], land3.at[at]).wait_recv()
        output[forward2.other(k)] = land3[at].astype(BF16)

    swap(0).start()
    gather(7)
    attn_ring.back()
    add_swap(0)
    swap(1).start()
    gather(8)
    attn_ring.ag2_step(1)
    add_swap(1)
    swap(2).start()
    gather(9)
    attn_ring.ag2_step(2)
    add_swap(2)
    swap(3).start()
    gather(10)
    attn_ring.ag2_step(3)
    add_swap(3)
    swap(4).start()
    loop(0, PIECES, finish_out)
    gather(11)
    attn_ring.ag1_step(1)
    add_swap(4)
    swap(5).start()
    gather(12)
    attn_ring.ag1_step(2)
    add_swap(5)
    gain_sums[...] = gains[6]
    gather(13)
    loop(0, PIECES, close_out)
    gather(14)
    attn_ring.ag1_step(3)
    for ring in rings:
        ring.end()

    def drain(s):
        for ring in rings:
            ring.drain(s)

    loop(0, 15, drain)
    loop(0, 3, attn_ring.drain)
    attn_ring.close()
    for i in range(6):
        swap(i).wait_send()

    def close(k):
        for work in sums:
            work.one(k).wait_send()
        at = back2.own(k)
        back2.three(k, dresidual.at[at], dresidual.at[at]).wait_send()
        here = forward2.local(k)
        forward2.three(k, forward2.land1.at[here], land3.at[here]).wait_send()
        back1.three(k, input_grad.at[at], input_grad.at[at]).wait()

    loop(0, PIECES, close)


def back_part(grads, *rest):
    rows, width = rest[0].shape
    half = (rows // 2, width)
    m, n = grads.shape[3], 96
    S = pltpu.VMEM
    ring_sems = [DMA((2, 4, 15))] * 4 + [DMA((2, 4))] * 3
    attn_sems = [DMA((4, 3))] * 8 + [DMA((4,))] * 3
    attn = (4, 4, 4, n, 128)
    return pl.pallas_call(
        back_kernel,
        out_shape=(
            jax.ShapeDtypeStruct((rows, width), BF16),
            jax.ShapeDtypeStruct((rows, width), F32),
            jax.ShapeDtypeStruct((8, width), F32),
            jax.ShapeDtypeStruct(grads.shape, F32),
            jax.ShapeDtypeStruct(attn, F32),
        ),
        in_specs=[ANY] + [VMEM] * len(rest),
        out_specs=(VMEM, VMEM, VMEM, ANY, ANY),
        scratch_shapes=[
            S(grads.shape, F32), S(grads.shape, F32), S((2, 4, m, 128), F32),
            S((2, 4, m, 128), F32),
            S(attn, F32), S(attn, F32), S((4, 4, n, 128), F32), S((4, n, 128), F32),
            S((4, n, 128), F32),
            S((3,) + half, F32), S((3,) + half, F32), S(half, F32),
            S((rows, width), F32), S((rows, width), F32), S((rows, 512), BF16),
            S((16, width), F32), S((7, 8, width), F32), S((6, 8, width), F32),
        ]
        + ring_sems
        + attn_sems
        + [DMA((3, PIECES))] * 6
        + [DMA((2,)), DMA((6,)), DMA((6,))],
        compiler_params=pltpu.CompilerParams(
            collective_id=2, has_side_effects=True, vmem_limit_bytes=63 << 20
        ),
    )(grads, *rest)


def unpack_kernel(grads, attn, gains, gate, up, down, query, key, value, out, gain1, gain2):
    gate[0] = grads[0, :, 0:64].reshape(1024, 128)
    up[0] = grads[0, :, 64:128].reshape(1024, 128)
    for j in range(8):
        lanes = slice(128 * j, 128 * j + 128)
        for half in range(2):
            down[0, 64 * half : 64 * half + 64, lanes] = grads[0, 2 * j + half, 128:192]
    query[:, 0:128] = attn[:, 0:16].reshape(128, 128)
    query[:, 128:256] = attn[:, 16:32].reshape(128, 128)
    key[...] = attn[:, 32:48].reshape(128, 128)
    value[...] = attn[:, 48:64].reshape(128, 128)
    out[...] = attn[:, 64:96].reshape(256, 128)
    gain1[...] = gains[0:1]
    gain2[...] = gains[1:2]


def unpack(grads, attn, gains):
    return pl.pallas_call(
        unpack_kernel,
        grid=(8,),
        out_shape=(
            jax.ShapeDtypeStruct((8, 1024, 128), F32),
            jax.ShapeDtypeStruct((8, 1024, 128), F32),
            jax.ShapeDtypeStruct((8, 128, 1024), F32),
            jax.ShapeDtypeStruct((1024, 256), F32),
            jax.ShapeDtypeStruct((1024, 128), F32),
            jax.ShapeDtypeStruct((1024, 128), F32),
            jax.ShapeDtypeStruct((256, 1024), F32),
            jax.ShapeDtypeStruct((1, 1024), F32),
            jax.ShapeDtypeStruct((1, 1024), F32),
        ),
        in_specs=[
            pl.BlockSpec((1, 16, 192, 128), lambda p: (p, 0, 0, 0)),
            pl.BlockSpec((8, 96, 128), lambda p: (p, 0, 0)),
            pl.BlockSpec((8, 128), lambda p: (0, p)),
        ],
        out_specs=(
            pl.BlockSpec((1, 1024, 128), lambda p: (p, 0, 0)),
            pl.BlockSpec((1, 1024, 128), lambda p: (p, 0, 0)),
            pl.BlockSpec((1, 128, 1024), lambda p: (p, 0, 0)),
            pl.BlockSpec((128, 256), lambda p: (p, 0)),
            pl.BlockSpec((128, 128), lambda p: (p, 0)),
            pl.BlockSpec((128, 128), lambda p: (p, 0)),
            pl.BlockSpec((256, 128), lambda p: (0, p)),
            pl.BlockSpec((1, 128), lambda p: (0, p)),
            pl.BlockSpec((1, 128), lambda p: (0, p)),
        ),
        compiler_params=pltpu.CompilerParams(vmem_limit_bytes=32 << 20),
    )(grads, attn, gains)


def tables(seq_count, seq_length, head_width):
    half_width = head_width // 2
    frequency = ROPE_THETA ** (-jnp.arange(half_width, dtype=jnp.float32) * 2.0 / head_width)
    position = jnp.tile(jnp.arange(seq_length), seq_count).astype(jnp.float32)
    angles = position[:, None] * frequency[None, :]
    return (jnp.cos(angles), jnp.sin(angles))


def rotate(values, cos_table, sin_table):
    half_width = values.shape[-1] // 2
    first_half = values[..., :half_width]
    second_half = values[..., half_width:]
    return jnp.concatenate(
        [
            first_half * cos_table - second_half * sin_table,
            second_half * cos_table + first_half * sin_table,
        ],
        -1,
    )


def local(
    tokens,
    norm1_gain,
    w_query,
    w_key,
    w_value,
    w_out,
    norm2_gain,
    expert_gate,
    expert_up,
    expert_down,
    routes,
    gate_weights,
    segments,
    cotangent,
):
    seq_count, seq_length = segments.shape
    tok_rows = tokens.shape[0]
    head_count = w_query.shape[1] // HD
    groups = w_key.shape[1] // HD
    group_size = head_count // groups
    experts = expert_gate.shape[0]
    cos_half, sin_half = tables(seq_count, seq_length, HD)
    cos_table, sin_table = cos_half[:, None, :], sin_half[:, None, :]
    inputs = tokens.astype(F32)
    scaled1, inverse1 = row_norm(inputs)
    hidden1 = (scaled1 * norm1_gain).astype(BF16)
    queries = rotate(
        dot_nn(hidden1, w_query).reshape(tok_rows, head_count, HD), cos_table, sin_table
    ).astype(BF16)
    keys = rotate(
        dot_nn(hidden1, w_key).reshape(tok_rows, groups, HD), cos_table, sin_table
    ).astype(BF16)
    values = dot_nn(hidden1, w_value).astype(BF16)
    query_blocks = queries.reshape(seq_count, seq_length, groups, group_size, HD)
    key_blocks = keys.reshape(seq_count, seq_length, groups, HD)
    value_blocks = values.reshape(seq_count, seq_length, groups, HD)
    raw_scores = jnp.einsum(
        "bqngd,bknd->bngqk", query_blocks, key_blocks, preferred_element_type=F32
    ) * HD ** (-0.5)
    position = jnp.arange(seq_length)
    allowed = (segments[:, :, None] == segments[:, None, :]) & (
        position[:, None] >= position[None, :]
    )
    scores = jnp.where(allowed[:, None, None, :, :], raw_scores, -1e30)
    row_max = jnp.max(scores, -1, keepdims=True)
    weights = jnp.exp(scores - row_max)
    row_total = jnp.sum(weights, -1, keepdims=True)
    probabilities = weights / row_total
    log_total = (row_max + jnp.log(row_total)).reshape(head_count, tok_rows)
    mixed_heads = jnp.einsum(
        "bngqk,bknd->bqngd",
        probabilities.astype(BF16),
        value_blocks,
        preferred_element_type=F32,
    )
    mixed_heads = mixed_heads.reshape(tok_rows, head_count * HD).astype(BF16)
    residual = inputs + sum4(dot_nn(mixed_heads, w_out))
    hidden2 = (row_norm(residual)[0] * norm2_gain).astype(BF16)
    picked = (routes[:, :, None] == jnp.arange(experts)[None, None, :]).astype(F32)
    expert_share = jnp.sum(gate_weights[:, :, None] * picked, 1).T[:, :, None]
    expert_grads, dhidden2, out_part = experts_part(
        hidden2, cotangent, expert_gate, expert_up, expert_down, expert_share
    )
    output, input_grad, gains, grads, attn = back_part(
        expert_grads.reshape(2, 4, 16, 192, 128),
        dhidden2,
        out_part,
        residual,
        tokens,
        cotangent,
        norm1_gain[None],
        norm2_gain[None],
        mixed_heads,
        w_out,
        queries.reshape(tok_rows, -1),
        keys.reshape(tok_rows, -1),
        values,
        log_total,
        segments.reshape(tok_rows, 1),
        segments,
        jnp.tile(cos_half, (1, 4)),
        jnp.tile(jnp.concatenate([sin_half, -sin_half], 1), (1, 2)),
        hidden1,
        w_query,
        w_key,
        w_value,
    )
    (
        gate_grad, up_grad, down_grad, query_grad, key_grad, value_grad, out_grad, gain1_grad,
        gain2_grad,
    ) = unpack(grads.reshape(experts, 16, 192, 128), attn.reshape(64, 96, 128), gains)
    return (
        output,
        input_grad,
        gain1_grad.reshape(-1),
        query_grad,
        key_grad,
        value_grad,
        out_grad,
        gain2_grad.reshape(-1),
        gate_grad,
        up_grad,
        down_grad,
    )


def solution(mesh):
    return jax.shard_map(
        local,
        mesh=mesh,
        in_specs=(
            P("dp", None),
            P(),
            P(None, "tensor"),
            P(None, "tensor"),
            P(None, "tensor"),
            P("tensor", None),
            P(),
            P(None, None, "tensor"),
            P(None, None, "tensor"),
            P(None, "tensor", None),
            P("dp", None),
            P("dp", None),
            P("dp", None),
            P("dp", None),
        ),
        out_specs=(
            P("dp", None),
            P("dp", None),
            P(),
            P(None, "tensor"),
            P(None, "tensor"),
            P(None, "tensor"),
            P("tensor", None),
            P(),
            P(None, None, "tensor"),
            P(None, None, "tensor"),
            P(None, "tensor", None),
        ),
        check_vma=False,
    )
```

```python
import functools

import jax
import jax.numpy as jnp
import numpy as np
from jax import lax
from jax.experimental import pallas as pl
from jax.experimental.pallas import tpu as pltpu
from jax.sharding import PartitionSpec as P

MESH = pl.DeviceIdType.MESH
DMA = pltpu.SemaphoreType.DMA
F32 = jnp.float32
BF16 = jnp.bfloat16

HD = 64
NORM_EPS = 1e-06
ROPE_THETA = 10000.0
FLOWS = ((0, 1), (0, -1), (1, 1), (1, -1))
PIECES = 4
VMEM = pl.BlockSpec(memory_space=pltpu.VMEM)
ANY = pl.BlockSpec(memory_space=pl.ANY)


def dot_nn(first_op, second_op):
    return jnp.dot(first_op, second_op, preferred_element_type=F32)


def dot_tn(first_op, second_op):
    return lax.dot_general(
        first_op, second_op, (((0,), (0,)), ((), ())), preferred_element_type=F32
    )


def dot_nt(first_op, second_op):
    return lax.dot_general(
        first_op, second_op, (((1,), (1,)), ((), ())), preferred_element_type=F32
    )


def ring_pos(dp):
    xy = dp // 2
    x, y = xy % 4, xy // 4
    turn = (x + y) % 4
    return 4 * y + turn, 4 * x + turn


def ring_dp(kind, pos, zhi):
    along = pos // 4
    across = (pos % 4 - along + 4) % 4
    x, y = (across, along) if kind == 0 else (along, across)
    return (y * 4 + x) * 2 + zhi


class Place:
    def __init__(self):
        self.dp = lax.axis_index("dp")
        self.tensor = lax.axis_index("tensor")
        zhi = self.dp % 2
        self.z_far = self.dp + 1 - 2 * zhi
        self.pos = ring_pos(self.dp)
        self.next = [
            ring_dp(kind, (self.pos[kind] + step + 16) % 16, zhi) for kind, step in FLOWS
        ]
        xy = self.dp // 2
        x, y = xy % 4, xy // 4
        self.x, self.y = x, y

        def at(dx, dy):
            return (((y + dy + 4) % 4) * 4 + (x + dx + 4) % 4) * 2 + zhi

        self.across = [at(1, 0), at(-1, 0), at(0, 1), at(0, -1)]
        self.pairs = [
            at(1 - 2 * (x % 2), 0), at(2, 0), at(0, 1 - 2 * (y % 2)), at(0, 2), self.z_far
        ]
        self.core = self.tensor % 2
        self.buddy = self.tensor + 1 - 2 * self.core
        self.z_near = self.tensor + 2 - 4 * (self.tensor // 2)


class Ring:
    def __init__(self, place, first, mine, land, zland, total, out, sems):
        self.place, self.first, self.mine, self.land = place, first, mine, land
        self.zland, self.total, self.out = zland, total, out
        self.rs_s, self.rs_r, self.ag_s, self.ag_r, self.z_s, self.z_r, self.keep_s = sems

    def chunk(self, f, back):
        kind, step = FLOWS[f]
        return (self.place.pos[kind] - step * back + 32) % 16

    def rs(self, f, s, src):
        c = self.chunk(f, 1 + s)
        return pltpu.make_async_remote_copy(
            src.at[f, c], self.land.at[f, c], self.rs_s.at[f, s], self.rs_r.at[f, s],
            device_id=(self.place.next[f], self.place.tensor), device_id_type=MESH,
        )

    def ag(self, f, s, src):
        return pltpu.make_async_remote_copy(
            src, self.out.at[f, self.chunk(f, s)], self.ag_s.at[f, s], self.ag_r.at[f, s],
            device_id=(self.place.next[f], self.place.tensor), device_id_type=MESH,
        )

    def zcopy(self, f):
        return pltpu.make_async_remote_copy(
            self.land.at[f, self.chunk(f, 0)], self.zland.at[f], self.z_s.at[f], self.z_r.at[f],
            device_id=(self.place.z_far, self.place.tensor), device_id_type=MESH,
        )

    def keep(self, f):
        return pltpu.make_async_copy(
            self.total.at[f], self.out.at[f, self.chunk(f, 0)], self.keep_s.at[f]
        )

    def begin(self, f):
        self.rs(f, 0, self.first).start()

    def rs_step(self, s):
        for f in range(4):
            self.rs(f, s - 1, self.land).wait_recv()
            c = self.chunk(f, 1 + s)
            self.land[f, c] = self.land[f, c] + self.mine[f, c]
            self.rs(f, s, self.land).start()

    def turn(self):
        for f in range(4):
            self.rs(f, 14, self.land).wait_recv()
            c = self.chunk(f, 0)
            self.land[f, c] = self.land[f, c] + self.mine[f, c]
            self.zcopy(f).start()

    def back(self):
        for f in range(4):
            self.zcopy(f).wait_recv()
            self.total[f] = self.land[f, self.chunk(f, 0)] + self.zland[f]
            self.ag(f, 0, self.total.at[f]).start()
            self.keep(f).start()

    def ag_step(self, s):
        for f in range(4):
            held = self.out.at[f, self.chunk(f, s)]
            self.ag(f, s - 1, held).wait_recv()
            self.ag(f, s, held).start()

    def end(self):
        for f in range(4):
            self.ag(f, 14, self.total.at[f]).wait_recv()
            self.zcopy(f).wait_send()
            self.keep(f).wait()

    def drain(self, s):
        for f in range(4):
            self.rs(f, s, self.land).wait_send()
            self.ag(f, s, self.total.at[f]).wait_send()


class AxisRing:
    def __init__(self, place, mine, land, land2, zland, total, out, sems):
        self.place, self.mine, self.land, self.land2 = place, mine, land, land2
        self.zland, self.total, self.out, self.sems = zland, total, out, sems

    def spots(self, f, back1, back2):
        step = 1 - 2 * (f % 2)
        pos1, pos2 = self.place.x, self.place.y
        if f >= 2:
            pos1, pos2 = pos2, pos1
        return (pos1 - step * back1 + 8) % 4, (pos2 - step * back2 + 8) % 4

    def send(self, f, s, stage, src, dst):
        axis = f // 2 if stage in (0, 3) else 1 - f // 2
        return pltpu.make_async_remote_copy(
            src, dst, self.sems[2 * stage].at[f, s], self.sems[2 * stage + 1].at[f, s],
            device_id=(self.place.across[2 * axis + f % 2], self.place.tensor),
            device_id_type=MESH,
        )

    def rs1(self, f, s, src):
        i = self.spots(f, 1 + s, 0)[0]
        return self.send(f, s, 0, src.at[f, i], self.land.at[f, i])

    def rs2(self, f, s, src):
        j = self.spots(f, 0, 1 + s)[1]
        return self.send(f, s, 1, src.at[j], self.land2.at[f, j])

    def ag2(self, f, s, src):
        i, j = self.spots(f, 0, s)
        return self.send(f, s, 2, src, self.out.at[f, i, j])

    def ag1(self, f, s, src):
        return self.send(f, s, 3, src, self.out.at[f, self.spots(f, s, 0)[0]])

    def zcopy(self, f):
        return pltpu.make_async_remote_copy(
            self.land2.at[f, self.spots(f, 0, 0)[1]], self.zland.at[f],
            self.sems[8].at[f], self.sems[9].at[f],
            device_id=(self.place.z_far, self.place.tensor), device_id_type=MESH,
        )

    def keep(self, f):
        i, j = self.spots(f, 0, 0)
        return pltpu.make_async_copy(
            self.total.at[f], self.out.at[f, i, j], self.sems[10].at[f]
        )

    def begin(self):
        for f in range(4):
            self.rs1(f, 0, self.mine).start()

    def rs1_step(self, s):
        for f in range(4):
            self.rs1(f, s - 1, self.land).wait_recv()
            if s == 1:
                self.rs1(f, 0, self.mine).wait_send()
            i = self.spots(f, 1 + s, 0)[0]
            self.land[f, i] = self.land[f, i] + self.mine[f, i]
            if s < 3:
                self.rs1(f, s, self.land).start()
            else:
                self.rs2(f, 0, self.land.at[f, i]).start()

    def rs2_step(self, s):
        for f in range(4):
            i, j = self.spots(f, 0, 1 + s)
            self.rs2(f, s - 1, self.land2.at[f]).wait_recv()
            self.land2[f, j] = self.land2[f, j] + self.land[f, i, j]
            if s < 3:
                self.rs2(f, s, self.land2.at[f]).start()
            else:
                self.zcopy(f).start()

    def back(self):
        for f in range(4):
            self.zcopy(f).wait_recv()
            self.total[f] = self.land2[f, self.spots(f, 0, 0)[1]] + self.zland[f]
            self.ag2(f, 0, self.total.at[f]).start()
            self.keep(f).start()

    def ag2_step(self, s):
        for f in range(4):
            self.ag2(f, s - 1, self.total.at[f]).wait_recv()
            i, j = self.spots(f, 0, s)
            if s < 3:
                self.ag2(f, s, self.out.at[f, i, j]).start()
            else:
                self.keep(f).wait()
                self.ag1(f, 0, self.out.at[f, i]).start()

    def ag1_step(self, s):
        for f in range(4):
            held = self.out.at[f, self.spots(f, s, 0)[0]]
            self.ag1(f, s - 1, held).wait_recv()
            if s < 3:
                self.ag1(f, s, held).start()

    def drain(self, s):
        for f in range(4):
            if s > 0:
                self.rs1(f, s, self.land).wait_send()
            self.rs2(f, s, self.land2.at[f]).wait_send()
            self.ag2(f, s, self.total.at[f]).wait_send()
            self.ag1(f, s, self.out.at[f, 0]).wait_send()

    def close(self):
        for f in range(4):
            self.zcopy(f).wait_send()


class Sum4:
    def __init__(self, place, part, land1, land2, sems):
        self.place, self.part, self.land1, self.land2 = place, part, land1, land2
        self.s1, self.r1, self.s2, self.r2, self.s3, self.r3 = sems
        self.half = part.shape[0] // 2
        self.n = self.half // PIECES

    def local(self, k):
        return pl.ds(pl.multiple_of(k * self.n, self.n), self.n)

    def rows(self, k, core):
        return pl.ds(pl.multiple_of((2 * k + core) * self.n, self.n), self.n)

    def own(self, k):
        return self.rows(k, self.place.core)

    def other(self, k):
        return self.rows(k, 1 - self.place.core)

    def one(self, k):
        return pltpu.make_async_remote_copy(
            self.part.at[self.other(k)], self.land1.at[self.local(k)],
            self.s1.at[k], self.r1.at[k],
            device_id=(self.place.dp, self.place.buddy), device_id_type=MESH,
        )

    def two(self, k):
        return pltpu.make_async_remote_copy(
            self.land1.at[self.local(k)], self.land2.at[self.local(k)],
            self.s2.at[k], self.r2.at[k],
            device_id=(self.place.dp, self.place.z_near), device_id_type=MESH,
        )

    def three(self, k, src, dst):
        return pltpu.make_async_remote_copy(
            src, dst, self.s3.at[k], self.r3.at[k],
            device_id=(self.place.dp, self.place.buddy), device_id_type=MESH,
        )

    def begin(self):
        for k in range(PIECES):
            self.one(k).start()

    def middle(self, k):
        self.one(k).wait_recv()
        at = self.local(k)
        self.land1[at] = self.land1[at] + self.part[self.own(k)]
        self.two(k).start()

    def total(self, k):
        self.two(k).wait_recv()
        self.two(k).wait_send()
        at = self.local(k)
        return self.land1[at] + self.land2[at]


def greet(place, rings):
    barrier = pltpu.get_barrier_semaphore()
    peers = [(place.dp, place.buddy), (place.dp, place.z_near)]
    if rings:
        peers += [(q, place.tensor) for q in place.across + [place.z_far]]
        peers += [(place.pairs[1], place.tensor), (place.pairs[3], place.tensor)]
    for peer in peers:
        pl.semaphore_signal(barrier, inc=1, device_id=peer, device_id_type=MESH)
    pl.semaphore_wait(barrier, len(peers))


def loop(low, high, body):
    def one(i, carry):
        body(i)
        return carry

    lax.fori_loop(low, high, one, 0)


def swap_halves(values):
    lane = lax.broadcasted_iota(jnp.int32, values.shape, 1)
    return jnp.where(lane % 64 < 32, pltpu.roll(values, 96, 1), pltpu.roll(values, 32, 1))


def allowed_pairs(seg_col, seg_row, until, block):
    shape = (until, 256)
    return (seg_col[:until] == seg_row[:, 256 * block : 256 * block + 256]) & (
        lax.broadcasted_iota(jnp.int32, shape, 0)
        <= lax.broadcasted_iota(jnp.int32, shape, 1) + 256 * block
    )


def front_kernel(
    *refs
):
    given, refs = refs[:12], refs[12:]
    kept, refs = refs[:9], refs[9:]
    inside, refs = refs[:12], refs[12:]
    made, refs = refs[:9], refs[9:]
    part, land1, land2, in_sem, out_sem = refs[:5]
    (
        tokens, gain1, cos_table, sin_table, w_query, w_key, w_value, seg_row, w_out, gain2,
        routes, route_weights,
    ) = inside
    hidden1, queries, keys, values, lse, mixed, residual, hidden2, side = made
    loads = [
        pltpu.make_async_copy(src, dst, in_sem.at[i])
        for i, (src, dst) in enumerate(zip(given, inside))
    ]
    stores = [
        pltpu.make_async_copy(src, dst, out_sem.at[i])
        for i, (src, dst) in enumerate(zip(made, kept))
    ]
    for load in loads:
        load.start()
    place = Place()
    greet(place, False)
    work = Sum4(place, part, land1, land2, refs[5:])
    for load in loads:
        load.wait()
    rows = [
        jnp.sum(
            jnp.where(routes[...] == e, route_weights[...], 0.0), 0, keepdims=True
        )
        for e in range(8)
    ]
    rows.append(seg_row[...].astype(F32))
    rows.append(jnp.zeros((119, 512), F32))
    side[...] = jnp.concatenate(rows, 0).T
    stores[8].start()
    seg_col = side[:, 8:9].astype(jnp.int32)
    for b in range(2):
        at = slice(256 * b, 256 * b + 256)
        until = 256 * b + 256

        def rotate(projected):
            turned = projected * cos_table[at] - swap_halves(projected) * sin_table[at]
            return turned.astype(BF16)

        normed = (row_norm(tokens[at].astype(F32))[0] * gain1[...]).astype(BF16)
        hidden1[at] = normed
        projected = dot_nn(normed, w_query[...])
        for g in range(2):
            queries[at, 128 * g : 128 * g + 128] = rotate(projected[:, 128 * g : 128 * g + 128])
        keys[at] = rotate(dot_nn(normed, w_key[...]))
        values[at] = dot_nn(normed, w_value[...]).astype(BF16)
        if b == 1:
            work.middle(0)
            work.middle(1)
        allowed = allowed_pairs(seg_col, seg_row, until, b)
        heads = []
        for h in range(4):
            own = slice(64 * (h // 2), 64 * (h // 2) + 64)
            raw = dot_nt(keys[:until, own], queries[at, 64 * h : 64 * h + 64]) * HD ** (-0.5)
            scores = jnp.where(allowed, raw, -1e30)
            top = jnp.max(scores, 0, keepdims=True)
            weights = jnp.exp(scores - top)
            row_total = jnp.sum(weights, 0, keepdims=True)
            lse[h : h + 1, at] = top + jnp.log(row_total)
            heads.append(dot_tn((weights / row_total).astype(BF16), values[:until, own]))
        mixed[at] = jnp.concatenate(heads, 1).astype(BF16)
        part[at] = dot_nn(mixed[at], w_out[...])
        work.one(2 * b).start()
        work.one(2 * b + 1).start()
    work.middle(2)
    work.middle(3)
    for store in stores[:6]:
        store.start()

    def give(rows):
        hidden2[rows] = (row_norm(residual[rows])[0] * gain2[...]).astype(BF16)

    def finish(k):
        at = work.own(k)
        residual[at] = tokens[at].astype(F32) + work.total(k)
        work.three(k, residual.at[at], residual.at[at]).start()
        give(at)

    loop(0, PIECES, finish)

    def close(k):
        at = work.own(k)
        work.three(k, residual.at[at], residual.at[at]).wait()
        give(work.other(k))
        work.one(k).wait_send()

    loop(0, PIECES, close)
    for store in stores[6:8]:
        store.start()
    for store in stores:
        store.wait()


def front_part(*given):
    rows, width = given[0].shape
    half = (rows // 2, width)
    made = (
        jax.ShapeDtypeStruct((rows, width), BF16),
        jax.ShapeDtypeStruct((rows, 256), BF16),
        jax.ShapeDtypeStruct((rows, 128), BF16),
        jax.ShapeDtypeStruct((rows, 128), BF16),
        jax.ShapeDtypeStruct((8, rows), F32),
        jax.ShapeDtypeStruct((rows, 256), BF16),
        jax.ShapeDtypeStruct((rows, width), F32),
        jax.ShapeDtypeStruct((rows, width), BF16),
        jax.ShapeDtypeStruct((rows, 128), F32),
    )
    return pl.pallas_call(
        front_kernel,
        out_shape=made,
        in_specs=[ANY] * len(given),
        out_specs=(ANY,) * len(made),
        scratch_shapes=[pltpu.VMEM(a.shape, a.dtype) for a in given + made]
        + [pltpu.VMEM((rows, width), F32)]
        + [pltpu.VMEM(half, F32)] * 2
        + [DMA((len(given),)), DMA((len(made),))]
        + [DMA((PIECES,))] * 6,
        compiler_params=pltpu.CompilerParams(
            collective_id=1, has_side_effects=True, vmem_limit_bytes=60 << 20
        ),
    )(*given)


def expert_kernel(
    hidden2, dy, w_gate, w_up, w_down, side, grads, dhidden2, out, hidden2_t
):
    step = pl.program_id(0)

    @pl.when(step == 0)
    def _():
        hidden2_t[...] = hidden2[...].T
        dhidden2[...] = jnp.zeros_like(dhidden2)
        out[...] = jnp.zeros_like(out)

    down_pair = w_down[...].reshape(256, 1024)
    dact_pair = dot_nt(dy[...], down_pair)
    acts = []
    for i in range(2):
        both_w = jnp.concatenate([w_gate[i], w_up[i]], 1)
        both = dot_nn(hidden2[...], both_w)
        gate, up = both[:, :128], both[:, 128:]
        sig = 1.0 / (1.0 + jnp.exp(-gate))
        silu = gate * sig
        lane = lax.broadcasted_iota(jnp.int32, side.shape, 1)
        chosen = jnp.where(lane == 2 * step + i, side[...], 0.0)
        weight = jnp.sum(chosen, 1, keepdims=True)
        acts.append((silu * up * weight).astype(BF16))
        dact = dact_pair[:, 128 * i : 128 * i + 128] * weight
        dgate = (dact * up * (sig * (1.0 + gate * (1.0 - sig)))).astype(BF16)
        dup = (dact * silu).astype(BF16)
        dboth = jnp.concatenate([dgate, dup], 1)
        grad = dot_nn(hidden2_t[...], dboth)
        grads[i, :, 0:64] = grad[:, :128].reshape(16, 64, 128)
        grads[i, :, 64:128] = grad[:, 128:].reshape(16, 64, 128)
        dhidden2[...] += dot_nt(dboth, both_w)
    act_pair = jnp.concatenate(acts, 1)
    out[...] += dot_nn(act_pair, down_pair)
    down_grad = dot_tn(act_pair, dy[...])
    for i in range(2):
        for j in range(8):
            for half in range(2):
                at = 128 * i + 64 * half
                grads[i, 2 * j + half, 128:192] = down_grad[at : at + 64, 128 * j : 128 * j + 128]


def experts_part(hidden2, dy, w_gate, w_up, w_down, side):
    rows, width = hidden2.shape
    count = w_gate.shape[0]
    whole = pl.BlockSpec((rows, width), lambda p: (0, 0))
    return pl.pallas_call(
        expert_kernel,
        grid=(count // 2,),
        out_shape=(
            jax.ShapeDtypeStruct((count, 16, 192, 128), F32),
            jax.ShapeDtypeStruct((rows, width), F32),
            jax.ShapeDtypeStruct((rows, width), F32),
        ),
        in_specs=[
            whole,
            whole,
            pl.BlockSpec((2, width, 128), lambda p: (p, 0, 0)),
            pl.BlockSpec((2, width, 128), lambda p: (p, 0, 0)),
            pl.BlockSpec((2, 128, width), lambda p: (p, 0, 0)),
            pl.BlockSpec(side.shape, lambda p: (0, 0)),
        ],
        out_specs=(
            pl.BlockSpec((2, 16, 192, 128), lambda p: (p, 0, 0, 0)),
            whole,
            whole,
        ),
        scratch_shapes=[pltpu.VMEM((width, rows), BF16)],
        compiler_params=pltpu.CompilerParams(vmem_limit_bytes=48 << 20),
    )(hidden2, dy, w_gate, w_up, w_down, side)


def row_norm(values):
    inverse = lax.rsqrt(jnp.mean(values * values, -1, keepdims=True) + NORM_EPS)
    return values * inverse, inverse


def norm_back(gradient, scaled, inverse, gain_vec):
    scaled_grad = gradient * gain_vec
    inner_sum = jnp.mean(scaled_grad * scaled, -1, keepdims=True)
    return inverse * (scaled_grad - scaled * inner_sum)


def fold(values):
    return jnp.sum(values.reshape(-1, 8, values.shape[-1]), 0)


def back_kernel(
    grads, dhidden2, out_part, residual, tokens, dy, gain1, gain2, mixed, w_out, queries, keys,
    values, lse, side, seg_row, cos_table, sin_table, hidden1, w_query, w_key, w_value,
    output, input_grad, gain_sums, mine, attn,
    land, zland, total, attn_land, attn_land2, attn_zland, attn_total,
    land1, land2, dresidual, dhidden1, dqkv, folded, gains, gains_in, *sems
):
    place = Place()
    greet(place, True)
    ring_sems, sems = sems[:7], sems[7:]
    attn_sems, sems = sems[:11], sems[11:]
    sum_sems, sems = sems[:6], sems[6:]
    load_sem, gain_s, gain_r = sems
    rings = [
        Ring(
            place, grads.at[u], mine.at[u], land.at[u], zland.at[u], total.at[u],
            mine.at[u], [sem.at[u] for sem in ring_sems],
        )
        for u in range(2)
    ]
    attn_ring = AxisRing(
        place, attn, attn_land, attn_land2, attn_zland, attn_total, attn, attn_sems
    )
    sums = [
        Sum4(place, part, land1.at[i], land2.at[i], [sem.at[i] for sem in sum_sems])
        for i, part in enumerate((dhidden2, out_part, dhidden1))
    ]
    back2, forward2, back1 = sums
    land3 = back2.land1

    back2.begin()
    for ring in rings:
        for f in range(4):
            ring.begin(f)
    loads = [pltpu.make_async_copy(grads.at[u], mine.at[u], load_sem.at[u]) for u in range(2)]
    for load in loads:
        load.start()
    folded[...] = jnp.zeros_like(folded)
    seg_col = side[:, 8:9].astype(jnp.int32)

    def step(s):
        for ring in rings:
            ring.rs_step(s)

    def gather(s):
        for ring in rings:
            ring.ag_step(s)

    loop(0, PIECES, back2.middle)
    for load in loads:
        load.wait()
    step(1)

    def finish2(k):
        d = back2.total(k)
        at = back2.own(k)
        scaled, inverse = row_norm(residual[at])
        folded[8:16] += fold(d * scaled)
        dresidual[at] = dy[at].astype(F32) + norm_back(d, scaled, inverse, gain2[...])
        back2.three(k, dresidual.at[at], dresidual.at[at]).start()

    step(2)
    finish2(0)
    step(3)
    finish2(1)
    step(4)
    step(5)
    finish2(2)
    step(6)
    finish2(3)
    step(7)

    def close2(k):
        at = back2.own(k)
        back2.three(k, dresidual.at[at], dresidual.at[at]).wait_recv()

    loop(0, PIECES, close2)
    forward2.begin()

    dbranch = dresidual[...].astype(BF16)
    dmixed = dot_nt(dbranch, w_out[...]).astype(BF16)
    out_grad = dot_tn(mixed[...], dbranch)
    for j in range(8):
        piece = out_grad[:, 128 * j : 128 * j + 128].reshape(2, 4, 32, 128)
        attn[j // 2, 2 * (j % 2) : 2 * (j % 2) + 2, :, 64:96] = piece

    step(8)
    loop(0, PIECES, forward2.middle)

    def unrotate(grad):
        return (grad * cos_table[...] + swap_halves(grad) * sin_table[...]).astype(BF16)

    dkeys, dvalues = [], []
    for g in range(2):
        key = keys[:, 64 * g : 64 * g + 64]
        value = values[:, 64 * g : 64 * g + 64]
        dkey = [0.0, 0.0]
        dvalue = [0.0, 0.0]
        dquery = []
        for h in (2 * g, 2 * g + 1):
            blocks = []
            for b in range(2):
                at = slice(256 * b, 256 * b + 256)
                until = 256 * b + 256
                query = queries[at, 64 * h : 64 * h + 64]
                dmix = dmixed[at, 64 * h : 64 * h + 64]
                raw = dot_nt(key[:until], query) * HD ** (-0.5)
                allowed = allowed_pairs(seg_col, seg_row, until, b)
                probs = jnp.exp(jnp.where(allowed, raw, -1e30) - lse[h : h + 1, at])
                dprobs = dot_nt(value[:until], dmix)
                inner = jnp.sum(probs * dprobs, 0, keepdims=True)
                dscores = (probs * (dprobs - inner)).astype(BF16)
                dvalue_part = dot_nn(probs.astype(BF16), dmix)
                dkey_part = dot_nn(dscores, query)
                for t in range(b + 1):
                    dvalue[t] = dvalue[t] + dvalue_part[256 * t : 256 * t + 256]
                    dkey[t] = dkey[t] + dkey_part[256 * t : 256 * t + 256]
                blocks.append(dot_tn(dscores, key[:until]))
                if 2 * h + b < 6:
                    step(9 + 2 * h + b)
            dquery.append(jnp.concatenate(blocks, 0) * HD ** (-0.5))
        dqkv[:, 128 * g : 128 * g + 128] = unrotate(jnp.concatenate(dquery, 1))
        dkeys.append(jnp.concatenate(dkey, 0) * HD ** (-0.5))
        dvalues.append(jnp.concatenate(dvalue, 0))
    dqkv[:, 256:384] = unrotate(jnp.concatenate(dkeys, 1))
    dqkv[:, 384:512] = jnp.concatenate(dvalues, 1).astype(BF16)

    hidden_grad = dot_tn(hidden1[...], dqkv[...])
    for j in range(4):
        piece = hidden_grad[:, 128 * j : 128 * j + 128].reshape(4, 4, 4, 16, 128)
        attn[:, :, :, 16 * j : 16 * j + 16] = piece
    attn_ring.begin()
    for ring in rings:
        ring.turn()
    dhidden1[...] = (
        dot_nt(dqkv[:, :256], w_query[...])
        + dot_nt(dqkv[:, 256:384], w_key[...])
        + dot_nt(dqkv[:, 384:512], w_value[...])
    )
    back1.begin()
    attn_ring.rs1_step(1)
    attn_ring.rs1_step(2)
    for ring in rings:
        ring.back()
    loop(0, PIECES, back1.middle)
    gather(1)
    attn_ring.rs1_step(3)
    gather(2)
    attn_ring.rs2_step(1)

    def finish1(k):
        gather(3 + k)
        d = back1.total(k)
        at = back1.own(k)
        scaled, inverse = row_norm(tokens[at].astype(F32))
        folded[0:8] += fold(d * scaled)
        input_grad[at] = dresidual[at] + norm_back(d, scaled, inverse, gain1[...])
        back1.three(k, input_grad.at[at], input_grad.at[at]).start()

    loop(0, 2, finish1)
    attn_ring.rs2_step(2)
    loop(2, PIECES, finish1)
    attn_ring.rs2_step(3)
    gains[0] = jnp.concatenate(
        [
            jnp.sum(folded[0:8], 0, keepdims=True),
            jnp.sum(folded[8:16], 0, keepdims=True),
            jnp.zeros((6, gains.shape[2]), F32),
        ],
        0,
    )

    def swap(i):
        device = (place.dp, place.buddy) if i == 0 else (place.pairs[i - 1], place.tensor)
        return pltpu.make_async_remote_copy(
            gains.at[i], gains_in.at[i], gain_s.at[i], gain_r.at[i],
            device_id=device, device_id_type=MESH,
        )

    def add_swap(i):
        swap(i).wait_recv()
        gains[i + 1] = gains[i] + gains_in[i]

    def finish_out(k):
        done = forward2.total(k) + residual[forward2.own(k)]
        at = forward2.local(k)
        output[forward2.own(k)] = done.astype(BF16)
        forward2.land1[at] = done
        forward2.three(k, forward2.land1.at[at], land3.at[at]).start()

    def close_out(k):
        at = forward2.local(k)
        forward2.three(k, forward2.land1.at[at], land3.at[at]).wait_recv()
        output[forward2.other(k)] = land3[at].astype(BF16)

    swap(0).start()
    gather(7)
    attn_ring.back()
    add_swap(0)
    swap(1).start()
    gather(8)
    attn_ring.ag2_step(1)
    add_swap(1)
    swap(2).start()
    gather(9)
    attn_ring.ag2_step(2)
    add_swap(2)
    swap(3).start()
    gather(10)
    attn_ring.ag2_step(3)
    add_swap(3)
    swap(4).start()
    loop(0, PIECES, finish_out)
    gather(11)
    attn_ring.ag1_step(1)
    add_swap(4)
    swap(5).start()
    gather(12)
    attn_ring.ag1_step(2)
    add_swap(5)
    gain_sums[...] = gains[6]
    gather(13)
    loop(0, PIECES, close_out)
    gather(14)
    attn_ring.ag1_step(3)
    for ring in rings:
        ring.end()

    def drain(s):
        for ring in rings:
            ring.drain(s)

    loop(0, 15, drain)
    for s in range(3):
        attn_ring.drain(s)
    attn_ring.close()
    for i in range(6):
        swap(i).wait_send()

    def close(k):
        for work in sums:
            work.one(k).wait_send()
        at = back2.own(k)
        back2.three(k, dresidual.at[at], dresidual.at[at]).wait_send()
        here = forward2.local(k)
        forward2.three(k, forward2.land1.at[here], land3.at[here]).wait_send()
        back1.three(k, input_grad.at[at], input_grad.at[at]).wait()

    loop(0, PIECES, close)


def back_part(grads, *rest):
    rows, width = rest[0].shape
    half = (rows // 2, width)
    m, n = grads.shape[3], 96
    S = pltpu.VMEM
    ring_sems = [DMA((2, 4, 15))] * 4 + [DMA((2, 4))] * 3
    attn_sems = [DMA((4, 3))] * 8 + [DMA((4,))] * 3
    attn = (4, 4, 4, n, 128)
    return pl.pallas_call(
        back_kernel,
        out_shape=(
            jax.ShapeDtypeStruct((rows, width), BF16),
            jax.ShapeDtypeStruct((rows, width), F32),
            jax.ShapeDtypeStruct((8, width), F32),
            jax.ShapeDtypeStruct(grads.shape, F32),
            jax.ShapeDtypeStruct(attn, F32),
        ),
        in_specs=[ANY] + [VMEM] * len(rest),
        out_specs=(VMEM,) * 5,
        scratch_shapes=[
            S(grads.shape, F32), S((2, 4, m, 128), F32),
            S((2, 4, m, 128), F32),
            S(attn, F32), S((4, 4, n, 128), F32), S((4, n, 128), F32),
            S((4, n, 128), F32),
            S((3,) + half, F32), S((3,) + half, F32),
            S((rows, width), F32), S((rows, width), F32), S((rows, 512), BF16),
            S((16, width), F32), S((7, 8, width), F32), S((6, 8, width), F32),
        ]
        + ring_sems
        + attn_sems
        + [DMA((3, PIECES))] * 6
        + [DMA((2,)), DMA((6,)), DMA((6,))],
        compiler_params=pltpu.CompilerParams(
            collective_id=2, has_side_effects=True, vmem_limit_bytes=63 << 20
        ),
    )(grads, *rest)


def unpack_kernel(
    grads, attn, gains, forward, backward, gate, up, down, query, key, value, out, gain1, gain2,
    output, input_grad
):
    gate[0] = grads[0, :, 0:64].reshape(1024, 128)
    up[0] = grads[0, :, 64:128].reshape(1024, 128)
    for j in range(8):
        lanes = slice(128 * j, 128 * j + 128)
        for half in range(2):
            down[0, 64 * half : 64 * half + 64, lanes] = grads[0, 2 * j + half, 128:192]
    query[:, 0:128] = attn[:, 0:16].reshape(128, 128)
    query[:, 128:256] = attn[:, 16:32].reshape(128, 128)
    key[...] = attn[:, 32:48].reshape(128, 128)
    value[...] = attn[:, 48:64].reshape(128, 128)
    out[...] = attn[:, 64:96].reshape(256, 128)
    gain1[...] = gains[0:1]
    gain2[...] = gains[1:2]
    output[...] = forward[...]
    input_grad[...] = backward[...]


def unpack(grads, attn, gains, forward, backward):
    return pl.pallas_call(
        unpack_kernel,
        grid=(8,),
        out_shape=(
            jax.ShapeDtypeStruct((8, 1024, 128), F32),
            jax.ShapeDtypeStruct((8, 1024, 128), F32),
            jax.ShapeDtypeStruct((8, 128, 1024), F32),
            jax.ShapeDtypeStruct((1024, 256), F32),
            jax.ShapeDtypeStruct((1024, 128), F32),
            jax.ShapeDtypeStruct((1024, 128), F32),
            jax.ShapeDtypeStruct((256, 1024), F32),
            jax.ShapeDtypeStruct((1, 1024), F32),
            jax.ShapeDtypeStruct((1, 1024), F32),
            jax.ShapeDtypeStruct(forward.shape, BF16),
            jax.ShapeDtypeStruct(backward.shape, F32),
        ),
        in_specs=[
            pl.BlockSpec((1, 16, 192, 128), lambda p: (p, 0, 0, 0)),
            pl.BlockSpec((8, 96, 128), lambda p: (p, 0, 0)),
            pl.BlockSpec((8, 128), lambda p: (0, p)),
            pl.BlockSpec((64, 1024), lambda p: (p, 0)),
            pl.BlockSpec((64, 1024), lambda p: (p, 0)),
        ],
        out_specs=(
            pl.BlockSpec((1, 1024, 128), lambda p: (p, 0, 0)),
            pl.BlockSpec((1, 1024, 128), lambda p: (p, 0, 0)),
            pl.BlockSpec((1, 128, 1024), lambda p: (p, 0, 0)),
            pl.BlockSpec((128, 256), lambda p: (p, 0)),
            pl.BlockSpec((128, 128), lambda p: (p, 0)),
            pl.BlockSpec((128, 128), lambda p: (p, 0)),
            pl.BlockSpec((256, 128), lambda p: (0, p)),
            pl.BlockSpec((1, 128), lambda p: (0, p)),
            pl.BlockSpec((1, 128), lambda p: (0, p)),
            pl.BlockSpec((64, 1024), lambda p: (p, 0)),
            pl.BlockSpec((64, 1024), lambda p: (p, 0)),
        ),
        compiler_params=pltpu.CompilerParams(vmem_limit_bytes=62 << 20),
    )(grads, attn, gains, forward, backward)


def tables(seq_length):
    half_width = HD // 2
    exponent = -np.arange(half_width, dtype=np.float32) * np.float32(2.0) / np.float32(HD)
    frequency = np.power(np.float32(ROPE_THETA), exponent)
    angles = np.arange(seq_length, dtype=np.float32)[:, None] * frequency[None, :]
    cosine, sine = np.cos(angles), np.sin(angles)
    return (
        jnp.asarray(np.concatenate([cosine] * 4, 1)),
        jnp.asarray(np.concatenate([sine, -sine] * 2, 1)),
    )


def local(
    tokens,
    norm1_gain,
    w_query,
    w_key,
    w_value,
    w_out,
    norm2_gain,
    expert_gate,
    expert_up,
    expert_down,
    routes,
    gate_weights,
    segments,
    cotangent,
):
    experts = expert_gate.shape[0]
    cos_table, sin_table = tables(tokens.shape[0])
    gain1, gain2 = norm1_gain[None], norm2_gain[None]
    hidden1, queries, keys, values, lse, mixed, residual, hidden2, side = front_part(
        tokens, gain1, cos_table, sin_table, w_query, w_key, w_value, segments, w_out, gain2,
        routes.T, gate_weights.T,
    )
    expert_grads, dhidden2, out_part = experts_part(
        hidden2, cotangent, expert_gate, expert_up, expert_down, side
    )
    output, input_grad, gains, grads, attn = back_part(
        expert_grads.reshape(2, 4, 16, 192, 128), dhidden2, out_part, residual, tokens,
        cotangent, gain1, gain2, mixed, w_out, queries, keys, values, lse, side, segments,
        cos_table, sin_table, hidden1, w_query, w_key, w_value,
    )
    (
        gate_grad, up_grad, down_grad, query_grad, key_grad, value_grad, out_grad, gain1_grad,
        gain2_grad, output, input_grad,
    ) = unpack(
        grads.reshape(experts, 16, 192, 128), attn.reshape(64, 96, 128), gains, output, input_grad
    )
    return (
        output,
        input_grad,
        gain1_grad.reshape(-1),
        query_grad,
        key_grad,
        value_grad,
        out_grad,
        gain2_grad.reshape(-1),
        gate_grad,
        up_grad,
        down_grad,
    )


def solution(mesh):
    return jax.shard_map(
        local,
        mesh=mesh,
        in_specs=(
            P("dp", None),
            P(),
            P(None, "tensor"),
            P(None, "tensor"),
            P(None, "tensor"),
            P("tensor", None),
            P(),
            P(None, None, "tensor"),
            P(None, None, "tensor"),
            P(None, "tensor", None),
            P("dp", None),
            P("dp", None),
            P("dp", None),
            P("dp", None),
        ),
        out_specs=(
            P("dp", None),
            P("dp", None),
            P(),
            P(None, "tensor"),
            P(None, "tensor"),
            P(None, "tensor"),
            P("tensor", None),
            P(),
            P(None, None, "tensor"),
            P(None, None, "tensor"),
            P(None, "tensor", None),
        ),
        check_vma=False,
    )
```

```python
import functools

import jax
import jax.numpy as jnp
import numpy as np
from jax import lax
from jax.experimental import pallas as pl
from jax.experimental.pallas import tpu as pltpu
from jax.sharding import PartitionSpec as P

MESH = pl.DeviceIdType.MESH
DMA = pltpu.SemaphoreType.DMA
F32 = jnp.float32
BF16 = jnp.bfloat16

HD = 64
NORM_EPS = 1e-06
ROPE_THETA = 10000.0
PIECES = 4
VMEM = pl.BlockSpec(memory_space=pltpu.VMEM)
ANY = pl.BlockSpec(memory_space=pl.ANY)


def dot_nn(first_op, second_op):
    return jnp.dot(first_op, second_op, preferred_element_type=F32)


def dot_tn(first_op, second_op):
    return lax.dot_general(
        first_op, second_op, (((0,), (0,)), ((), ())), preferred_element_type=F32
    )


def dot_nt(first_op, second_op):
    return lax.dot_general(
        first_op, second_op, (((1,), (1,)), ((), ())), preferred_element_type=F32
    )


class Place:
    def __init__(self):
        self.dp = lax.axis_index("dp")
        self.tensor = lax.axis_index("tensor")
        zhi = self.dp % 2
        self.z_far = self.dp + 1 - 2 * zhi
        xy = self.dp // 2
        x, y = xy % 4, xy // 4
        self.x, self.y = x, y

        def at(dx, dy):
            return (((y + dy + 4) % 4) * 4 + (x + dx + 4) % 4) * 2 + zhi

        self.across = [at(1, 0), at(-1, 0), at(0, 1), at(0, -1)]
        self.pairs = [
            at(1 - 2 * (x % 2), 0), at(2, 0), at(0, 1 - 2 * (y % 2)), at(0, 2), self.z_far
        ]
        self.core = self.tensor % 2
        self.buddy = self.tensor + 1 - 2 * self.core
        self.z_near = self.tensor + 2 - 4 * (self.tensor // 2)


class AxisRing:
    def __init__(self, place, mine, land, land2, zland, out, sems):
        self.place, self.mine, self.land, self.land2 = place, mine, land, land2
        self.zland, self.out, self.sems = zland, out, sems

    def spots(self, f, back1, back2):
        step = 1 - 2 * (f % 2)
        pos1, pos2 = self.place.x, self.place.y
        if f >= 2:
            pos1, pos2 = pos2, pos1
        return (pos1 - step * back1 + 8) % 4, (pos2 - step * back2 + 8) % 4

    def send(self, f, s, stage, src, dst):
        axis = f // 2 if stage in (0, 3) else 1 - f // 2
        return pltpu.make_async_remote_copy(
            src, dst, self.sems[2 * stage].at[f, s], self.sems[2 * stage + 1].at[f, s],
            device_id=(self.place.across[2 * axis + f % 2], self.place.tensor),
            device_id_type=MESH,
        )

    def rs1(self, f, s, src):
        i = self.spots(f, 1 + s, 0)[0]
        return self.send(f, s, 0, src.at[f, i], self.land.at[f, i])

    def rs2(self, f, s, src):
        j = self.spots(f, 0, 1 + s)[1]
        return self.send(f, s, 1, src.at[j], self.land2.at[f, j])

    def ag2(self, f, s, src):
        i, j = self.spots(f, 0, s)
        return self.send(f, s, 2, src.at[f, i, j], self.out.at[f, i, j])

    def ag1(self, f, s, src):
        return self.send(f, s, 3, src, self.out.at[f, self.spots(f, s, 0)[0]])

    def zcopy(self, f):
        return pltpu.make_async_remote_copy(
            self.land2.at[f, self.spots(f, 0, 0)[1]], self.zland.at[f],
            self.sems[8].at[f], self.sems[9].at[f],
            device_id=(self.place.z_far, self.place.tensor), device_id_type=MESH,
        )

    def keep(self, f):
        i, j = self.spots(f, 0, 0)
        return pltpu.make_async_copy(
            self.mine.at[f, i, j], self.out.at[f, i, j], self.sems[10].at[f]
        )

    def begin(self):
        for f in range(4):
            self.rs1(f, 0, self.mine).start()

    def rs1_step(self, s):
        for f in range(4):
            self.rs1(f, s - 1, self.land).wait_recv()
            if s == 1:
                self.rs1(f, 0, self.mine).wait_send()
            i = self.spots(f, 1 + s, 0)[0]
            self.land[f, i] = self.land[f, i] + self.mine[f, i]
            if s < 3:
                self.rs1(f, s, self.land).start()
            else:
                self.rs2(f, 0, self.land.at[f, i]).start()

    def rs2_step(self, s):
        for f in range(4):
            i, j = self.spots(f, 0, 1 + s)
            self.rs2(f, s - 1, self.land2.at[f]).wait_recv()
            self.land2[f, j] = self.land2[f, j] + self.land[f, i, j]
            if s < 3:
                self.rs2(f, s, self.land2.at[f]).start()
            else:
                self.zcopy(f).start()

    def back(self):
        for f in range(4):
            self.zcopy(f).wait_recv()
            i, j = self.spots(f, 0, 0)
            self.mine[f, i, j] = self.land2[f, j] + self.zland[f]
            self.ag2(f, 0, self.mine).start()
            self.keep(f).start()

    def ag2_step(self, s):
        for f in range(4):
            self.ag2(f, s - 1, self.out).wait_recv()
            i = self.spots(f, 0, s)[0]
            if s < 3:
                self.ag2(f, s, self.out).start()
            else:
                self.keep(f).wait()
                self.ag1(f, 0, self.out.at[f, i]).start()

    def ag1_step(self, s):
        for f in range(4):
            held = self.out.at[f, self.spots(f, s, 0)[0]]
            self.ag1(f, s - 1, held).wait_recv()
            if s < 3:
                self.ag1(f, s, held).start()

    def op(self, k):
        if k == 0:
            self.begin()
        elif k <= 3:
            self.rs1_step(k)
        elif k <= 6:
            self.rs2_step(k - 3)
        elif k == 7:
            self.back()
        elif k <= 10:
            self.ag2_step(k - 7)
        else:
            self.ag1_step(k - 10)

    def drain(self, s):
        for f in range(4):
            if s > 0:
                self.rs1(f, s, self.land).wait_send()
            self.rs2(f, s, self.land2.at[f]).wait_send()
            self.ag2(f, s, self.mine if s == 0 else self.out).wait_send()
            self.ag1(f, s, self.out.at[f, 0]).wait_send()

    def close(self):
        for f in range(4):
            self.zcopy(f).wait_send()


class Sum4:
    def __init__(self, place, part, land1, land2, sems):
        self.place, self.part, self.land1, self.land2 = place, part, land1, land2
        self.s1, self.r1, self.s2, self.r2, self.s3, self.r3 = sems
        self.half = part.shape[0] // 2
        self.n = self.half // PIECES

    def local(self, k):
        return pl.ds(pl.multiple_of(k * self.n, self.n), self.n)

    def rows(self, k, core):
        return pl.ds(pl.multiple_of((2 * k + core) * self.n, self.n), self.n)

    def own(self, k):
        return self.rows(k, self.place.core)

    def other(self, k):
        return self.rows(k, 1 - self.place.core)

    def one(self, k):
        return pltpu.make_async_remote_copy(
            self.part.at[self.other(k)], self.land1.at[self.local(k)],
            self.s1.at[k], self.r1.at[k],
            device_id=(self.place.dp, self.place.buddy), device_id_type=MESH,
        )

    def two(self, k):
        return pltpu.make_async_remote_copy(
            self.land1.at[self.local(k)], self.land2.at[self.local(k)],
            self.s2.at[k], self.r2.at[k],
            device_id=(self.place.dp, self.place.z_near), device_id_type=MESH,
        )

    def three(self, k, src, dst):
        return pltpu.make_async_remote_copy(
            src, dst, self.s3.at[k], self.r3.at[k],
            device_id=(self.place.dp, self.place.buddy), device_id_type=MESH,
        )

    def begin(self):
        for k in range(PIECES):
            self.one(k).start()

    def middle(self, k):
        self.one(k).wait_recv()
        at = self.local(k)
        self.land1[at] = self.land1[at] + self.part[self.own(k)]
        self.two(k).start()

    def total(self, k):
        self.two(k).wait_recv()
        self.two(k).wait_send()
        at = self.local(k)
        return self.land1[at] + self.land2[at]


def greet(place, rings):
    barrier = pltpu.get_barrier_semaphore()
    peers = [(place.dp, place.buddy), (place.dp, place.z_near)]
    if rings:
        peers += [(q, place.tensor) for q in place.across + [place.z_far]]
        peers += [(place.pairs[1], place.tensor), (place.pairs[3], place.tensor)]
    for peer in peers:
        pl.semaphore_signal(barrier, inc=1, device_id=peer, device_id_type=MESH)
    pl.semaphore_wait(barrier, len(peers))


def loop(low, high, body):
    def one(i, carry):
        body(i)
        return carry

    lax.fori_loop(low, high, one, 0)


def swap_halves(values):
    lane = lax.broadcasted_iota(jnp.int32, values.shape, 1)
    return jnp.where(lane % 64 < 32, pltpu.roll(values, 96, 1), pltpu.roll(values, 32, 1))


def allowed_pairs(seg_col, seg_row, until, block):
    shape = (until, 256)
    return (seg_col[:until] == seg_row[:, 256 * block : 256 * block + 256]) & (
        lax.broadcasted_iota(jnp.int32, shape, 0)
        <= lax.broadcasted_iota(jnp.int32, shape, 1) + 256 * block
    )


def front_kernel(
    *refs
):
    given, refs = refs[:12], refs[12:]
    kept, refs = refs[:9], refs[9:]
    inside, refs = refs[:12], refs[12:]
    made, refs = refs[:9], refs[9:]
    part, land1, land2, in_sem, out_sem, own_sem = refs[:6]
    (
        tokens, gain1, cos_table, sin_table, w_query, w_key, w_value, seg_row, w_out, gain2,
        routes, route_weights,
    ) = inside
    hidden1, queries, keys, values, lse, mixed, residual, hidden2, side = made
    loads = [
        pltpu.make_async_copy(src, dst, in_sem.at[i])
        for i, (src, dst) in enumerate(zip(given, inside))
    ]
    stores = [
        pltpu.make_async_copy(src, dst, out_sem.at[i])
        for i, (src, dst) in enumerate(zip(made, kept))
        if i != 6
    ]
    stores.insert(6, None)
    for load in loads:
        load.start()
    place = Place()
    greet(place, False)
    work = Sum4(place, part, land1, land2, refs[6:])
    for load in loads:
        load.wait()
    rows = [
        jnp.sum(
            jnp.where(routes[...] == e, route_weights[...], 0.0), 0, keepdims=True
        )
        for e in range(8)
    ]
    rows.append(seg_row[...].astype(F32))
    rows.append(jnp.zeros((119, 512), F32))
    side[...] = jnp.concatenate(rows, 0).T
    stores[8].start()
    seg_col = side[:, 8:9].astype(jnp.int32)
    for b in range(2):
        at = slice(256 * b, 256 * b + 256)
        until = 256 * b + 256

        def rotate(projected):
            turned = projected * cos_table[at] - swap_halves(projected) * sin_table[at]
            return turned.astype(BF16)

        normed = (row_norm(tokens[at].astype(F32))[0] * gain1[...]).astype(BF16)
        hidden1[at] = normed
        projected = dot_nn(normed, w_query[...])
        for g in range(2):
            queries[at, 128 * g : 128 * g + 128] = rotate(projected[:, 128 * g : 128 * g + 128])
        keys[at] = rotate(dot_nn(normed, w_key[...]))
        values[at] = dot_nn(normed, w_value[...]).astype(BF16)
        if b == 1:
            work.middle(0)
            work.middle(1)
        allowed = allowed_pairs(seg_col, seg_row, until, b)
        heads = []
        for h in range(4):
            own = slice(64 * (h // 2), 64 * (h // 2) + 64)
            raw = dot_nt(keys[:until, own], queries[at, 64 * h : 64 * h + 64]) * HD ** (-0.5)
            scores = jnp.where(allowed, raw, -1e30)
            top = jnp.max(scores, 0, keepdims=True)
            weights = jnp.exp(scores - top)
            row_total = jnp.sum(weights, 0, keepdims=True)
            lse[h : h + 1, at] = top + jnp.log(row_total)
            heads.append(dot_tn((weights / row_total).astype(BF16), values[:until, own]))
        mixed[at] = jnp.concatenate(heads, 1).astype(BF16)
        part[at] = dot_nn(mixed[at], w_out[...])
        work.one(2 * b).start()
        work.one(2 * b + 1).start()
    work.middle(2)
    work.middle(3)
    for store in stores[:6]:
        store.start()

    def give(rows):
        hidden2[rows] = (row_norm(residual[rows])[0] * gain2[...]).astype(BF16)

    def finish(k):
        at = work.own(k)
        residual[at] = tokens[at].astype(F32) + work.total(k)
        work.three(k, residual.at[at], residual.at[at]).start()
        give(at)

    loop(0, PIECES, finish)

    def own_rows(k):
        return pltpu.make_async_copy(
            residual.at[work.own(k)], kept[6].at[work.local(k)], own_sem.at[k]
        )

    def close(k):
        at = work.own(k)
        work.three(k, residual.at[at], residual.at[at]).wait()
        own_rows(k).start()
        give(work.other(k))
        work.one(k).wait_send()

    loop(0, PIECES, close)
    stores[7].start()
    for i, store in enumerate(stores):
        if i != 6:
            store.wait()
    loop(0, PIECES, lambda k: own_rows(k).wait())


def front_part(*given):
    rows, width = given[0].shape
    half = (rows // 2, width)
    made = (
        jax.ShapeDtypeStruct((rows, width), BF16),
        jax.ShapeDtypeStruct((rows, 256), BF16),
        jax.ShapeDtypeStruct((rows, 128), BF16),
        jax.ShapeDtypeStruct((rows, 128), BF16),
        jax.ShapeDtypeStruct((8, rows), F32),
        jax.ShapeDtypeStruct((rows, 256), BF16),
        jax.ShapeDtypeStruct((rows, width), F32),
        jax.ShapeDtypeStruct((rows, width), BF16),
        jax.ShapeDtypeStruct((rows, 128), F32),
    )
    return pl.pallas_call(
        front_kernel,
        out_shape=made[:6] + (jax.ShapeDtypeStruct(half, F32),) + made[7:],
        in_specs=[ANY] * len(given),
        out_specs=(ANY,) * len(made),
        scratch_shapes=[pltpu.VMEM(a.shape, a.dtype) for a in given + made]
        + [pltpu.VMEM((rows, width), F32)]
        + [pltpu.VMEM(half, F32)] * 2
        + [DMA((len(given),)), DMA((len(made),)), DMA((PIECES,))]
        + [DMA((PIECES,))] * 6,
        compiler_params=pltpu.CompilerParams(
            collective_id=1, has_side_effects=True, vmem_limit_bytes=60 << 20
        ),
    )(*given)


def row_norm(values):
    inverse = lax.rsqrt(jnp.mean(values * values, -1, keepdims=True) + NORM_EPS)
    return values * inverse, inverse


def norm_back(gradient, scaled, inverse, gain_vec):
    scaled_grad = gradient * gain_vec
    inner_sum = jnp.mean(scaled_grad * scaled, -1, keepdims=True)
    return inverse * (scaled_grad - scaled * inner_sum)


def fold(values):
    return jnp.sum(values.reshape(-1, 8, values.shape[-1]), 0)


def back_kernel(*refs):
    given, refs = refs[:23], refs[23:]
    output_hbm, input_grad_hbm, gain_sums, grads_sum, attn_sum = refs[:5]
    inside, refs = refs[5:24], refs[24:]
    (
        hidden2, dy, side, residual, gain2, mixed, w_out, queries, keys, values, lse, seg_row,
        cos_table, sin_table, w_query, w_key, w_value, tokens, gain1,
    ) = inside
    gate_w, up_w, down_w = refs[:3]
    (
        mine, land, ring_land2, zland, attn, attn_land, attn_land2, attn_zland, output, dresidual,
        dhidden2, out_part, hidden2_t, land1, land2, land3, folded, gains, gains_in,
    ) = refs[3:22]
    sems = refs[22:]
    ring_sems, sems = sems[:11], sems[11:]
    attn_sems, sems = sems[:11], sems[11:]
    sum_sems, sems = sems[:6], sems[6:]
    load_sem, weight_sem, late_sem, gain_s, gain_r = sems
    dqkv = hidden2_t.at[0:512]
    weights = given[19:22]
    hidden1_hbm = given[22]

    def weight_loads(p):
        slot = p % 2
        return [
            pltpu.make_async_copy(
                src.at[2 * p : 2 * p + 2], dst.at[slot], weight_sem.at[slot, i]
            )
            for i, (src, dst) in enumerate(zip(weights, (gate_w, up_w, down_w)))
        ]

    loads = [
        pltpu.make_async_copy(src, dst, load_sem.at[i])
        for i, (src, dst) in enumerate(zip(given[:19], inside))
    ]
    for load in loads[:3]:
        load.start()
    for p in range(2):
        for load in weight_loads(p):
            load.start()
    for load in loads[3:]:
        load.start()
    place = Place()
    greet(place, True)
    rings = [
        AxisRing(
            place, mine.at[u], land.at[u], ring_land2.at[u], zland.at[u], grads_sum.at[u],
            [sem.at[u] for sem in ring_sems],
        )
        for u in range(4)
    ]
    rings.append(
        AxisRing(place, attn, attn_land, attn_land2, attn_zland, attn_sum, attn_sems)
    )

    def go(k, *units):
        for u in units:
            rings[u].op(k)

    sums = [
        Sum4(place, part, land1.at[which], land2.at[which], [sem.at[i] for sem in sum_sems])
        for i, (part, which) in enumerate(((dhidden2, 0), (out_part, 1), (dhidden2, 0)))
    ]
    back2, forward2, back1 = sums

    folded[...] = jnp.zeros_like(folded)
    for load in loads[:3]:
        load.wait()
    hidden2_t[...] = hidden2[...].T
    for p in range(4):
        slot = p % 2
        for load in weight_loads(p):
            load.wait()
        down_pair = down_w[slot].reshape(256, 1024)
        dact_pair = dot_nt(dy[...], down_pair)
        acts, dboths, both_ws = [], [], []
        for i in range(2):
            e = 2 * p + i
            both_w = jnp.concatenate([gate_w[slot, i], up_w[slot, i]], 1)
            both = dot_nn(hidden2[...], both_w)
            gate, up = both[:, :128], both[:, 128:]
            sig = 1.0 / (1.0 + jnp.exp(-gate))
            silu = gate * sig
            weight = side[:, e : e + 1]
            acts.append((silu * up * weight).astype(BF16))
            dact = dact_pair[:, 128 * i : 128 * i + 128] * weight
            dgate = (dact * up * (sig * (1.0 + gate * (1.0 - sig)))).astype(BF16)
            dup = (dact * silu).astype(BF16)
            dboth = jnp.concatenate([dgate, dup], 1)
            grad = dot_nn(hidden2_t[...], dboth)
            for h in range(2):
                rows = slice(512 * h, 512 * h + 512)
                mine[p, 2 * i + h, :, :, 0:32] = grad[rows, :128].reshape(4, 4, 32, 128)
                mine[p, 2 * i + h, :, :, 32:64] = grad[rows, 128:].reshape(4, 4, 32, 128)
            part = dot_nt(dboth, both_w)
            dhidden2[...] = part if e == 0 else dhidden2[...] + part
        act_pair = jnp.concatenate(acts, 1)
        down_grad = dot_tn(act_pair, dy[...])
        for i in range(2):
            for j in range(8):
                piece = down_grad[128 * i : 128 * i + 128, 128 * j : 128 * j + 128]
                mine[p, 2 * i + j // 4, j % 4, :, 64:96] = piece.reshape(4, 32, 128)
        if p >= 2:
            go(1, p - 2)
        go(0, p)
        part = dot_nn(act_pair, down_pair)
        out_part[...] = part if p == 0 else out_part[...] + part
        if p < 2:
            for load in weight_loads(p + 2):
                load.start()
    late = [
        pltpu.make_async_copy(hidden1_hbm, hidden2, late_sem.at[0]),
    ]
    for load in late:
        load.start()
    back2.begin()
    for load in loads[3:]:
        load.wait()
    seg_col = side[:, 8:9].astype(jnp.int32)
    loop(0, PIECES, back2.middle)
    go(2, 0)

    def finish2(k):
        d = back2.total(k)
        at = back2.own(k)
        scaled, inverse = row_norm(residual[back2.local(k)])
        folded[8:16] += fold(d * scaled)
        dresidual[at] = dy[at].astype(F32) + norm_back(d, scaled, inverse, gain2[...])
        back2.three(k, dresidual.at[at], dresidual.at[at]).start()

    finish2(0)
    go(2, 1)
    finish2(1)
    go(1, 2, 3)
    go(3, 0)
    finish2(2)
    go(3, 1)
    go(4, 0)
    finish2(3)
    go(2, 2)
    go(4, 1)

    def close2(k):
        at = back2.own(k)
        back2.three(k, dresidual.at[at], dresidual.at[at]).wait()
        back2.one(k).wait_send()

    loop(0, PIECES, close2)
    forward2.begin()

    dbranch = dresidual[...].astype(BF16)
    dmixed = dot_nt(dbranch, w_out[...]).astype(BF16)
    out_grad = dot_tn(mixed[...], dbranch)
    for j in range(8):
        piece = out_grad[:, 128 * j : 128 * j + 128].reshape(2, 4, 32, 128)
        attn[j // 2, 2 * (j % 2) : 2 * (j % 2) + 2, :, 64:96] = piece

    go(5, 0)
    loop(0, PIECES, forward2.middle)
    go(2, 3)
    go(5, 1)

    def unrotate(grad):
        return (grad * cos_table[...] + swap_halves(grad) * sin_table[...]).astype(BF16)

    def between(h):
        if h == 0:
            go(6, 0, 1)
            go(3, 2)
        elif h == 1:
            go(3, 3)
            go(7, 0)
        elif h == 2:
            go(7, 1)
            go(4, 2, 3)
        else:
            go(8, 0, 1)
            go(5, 2, 3)

    dkeys, dvalues = [], []
    for g in range(2):
        key = keys[:, 64 * g : 64 * g + 64]
        value = values[:, 64 * g : 64 * g + 64]
        dkey = [0.0, 0.0]
        dvalue = [0.0, 0.0]
        dquery = []
        for h in (2 * g, 2 * g + 1):
            blocks = []
            for b in range(2):
                at = slice(256 * b, 256 * b + 256)
                until = 256 * b + 256
                query = queries[at, 64 * h : 64 * h + 64]
                dmix = dmixed[at, 64 * h : 64 * h + 64]
                raw = dot_nt(key[:until], query) * HD ** (-0.5)
                allowed = allowed_pairs(seg_col, seg_row, until, b)
                probs = jnp.exp(jnp.where(allowed, raw, -1e30) - lse[h : h + 1, at])
                dprobs = dot_nt(value[:until], dmix)
                inner = jnp.sum(probs * dprobs, 0, keepdims=True)
                dscores = (probs * (dprobs - inner)).astype(BF16)
                dvalue_part = dot_nn(probs.astype(BF16), dmix)
                dkey_part = dot_nn(dscores, query)
                for t in range(b + 1):
                    dvalue[t] = dvalue[t] + dvalue_part[256 * t : 256 * t + 256]
                    dkey[t] = dkey[t] + dkey_part[256 * t : 256 * t + 256]
                blocks.append(dot_tn(dscores, key[:until]))
                if b == 1:
                    between(h)
            dquery.append(jnp.concatenate(blocks, 0) * HD ** (-0.5))
        dqkv[:, 128 * g : 128 * g + 128] = unrotate(jnp.concatenate(dquery, 1))
        dkeys.append(jnp.concatenate(dkey, 0) * HD ** (-0.5))
        dvalues.append(jnp.concatenate(dvalue, 0))
    dqkv[:, 256:384] = unrotate(jnp.concatenate(dkeys, 1))
    dqkv[:, 384:512] = jnp.concatenate(dvalues, 1).astype(BF16)

    for load in late:
        load.wait()
    hidden_grad = dot_tn(hidden2[...], dqkv[...])
    for j in range(4):
        piece = hidden_grad[:, 128 * j : 128 * j + 128].reshape(4, 4, 4, 16, 128)
        attn[:, :, :, 16 * j : 16 * j + 16] = piece
    go(9, 0, 1)
    go(6, 2, 3)
    go(0, 4)
    go(10, 0, 1)
    dhidden2[...] = (
        dot_nt(dqkv[:, :256], w_query[...])
        + dot_nt(dqkv[:, 256:384], w_key[...])
        + dot_nt(dqkv[:, 384:512], w_value[...])
    )
    back1.begin()
    go(7, 2, 3)
    go(1, 4)

    def finish_out(k):
        done = forward2.total(k) + residual[forward2.local(k)]
        at = forward2.local(k)
        output[forward2.own(k)] = done.astype(BF16)
        forward2.land1[at] = done
        forward2.three(k, forward2.land1.at[at], land3.at[at]).start()

    def close_out(k):
        at = forward2.local(k)
        forward2.three(k, forward2.land1.at[at], land3.at[at]).wait()
        output[forward2.other(k)] = land3[at].astype(BF16)

    loop(0, PIECES, finish_out)
    go(11, 0)
    loop(0, PIECES, back1.middle)
    go(8, 2, 3)
    go(11, 1)
    go(2, 4)
    go(9, 2, 3)
    loop(0, PIECES, close_out)
    stores = [
        pltpu.make_async_copy(output, output_hbm, late_sem.at[1]),
        pltpu.make_async_copy(dresidual, input_grad_hbm, late_sem.at[2]),
    ]
    stores[0].start()
    go(12, 0, 1)
    go(10, 2)
    go(3, 4)
    go(10, 3)

    def finish1(k):
        d = back1.total(k)
        at = back1.own(k)
        scaled, inverse = row_norm(tokens[at].astype(F32))
        folded[0:8] += fold(d * scaled)
        dresidual[at] = dresidual[at] + norm_back(d, scaled, inverse, gain1[...])
        back1.three(k, dresidual.at[at], dresidual.at[at]).start()

    finish1(0)
    finish1(1)
    go(13, 0, 1)
    go(4, 4)
    finish1(2)
    go(11, 2)
    go(5, 4)
    finish1(3)
    gains[0] = jnp.concatenate(
        [
            jnp.sum(folded[0:8], 0, keepdims=True),
            jnp.sum(folded[8:16], 0, keepdims=True),
            jnp.zeros((6, gains.shape[2]), F32),
        ],
        0,
    )

    def swap(i):
        device = (place.dp, place.buddy) if i == 0 else (place.pairs[i - 1], place.tensor)
        return pltpu.make_async_remote_copy(
            gains.at[i], gains_in.at[i], gain_s.at[i], gain_r.at[i],
            device_id=device, device_id_type=MESH,
        )

    def add_swap(i):
        swap(i).wait_recv()
        gains[i + 1] = gains[i] + gains_in[i]

    swap(0).start()
    go(11, 3)
    go(6, 4)
    add_swap(0)
    swap(1).start()

    def close1(k):
        at = back1.own(k)
        back1.three(k, dresidual.at[at], dresidual.at[at]).wait()

    loop(0, PIECES, close1)
    stores[1].start()
    go(12, 2)
    add_swap(1)
    swap(2).start()
    go(7, 4)
    go(12, 3)
    add_swap(2)
    swap(3).start()
    go(8, 4)
    go(13, 2)
    add_swap(3)
    swap(4).start()
    go(9, 4)
    go(13, 3)
    add_swap(4)
    swap(5).start()
    go(10, 4)
    add_swap(5)
    gain_sums[...] = gains[6]
    go(11, 4)
    go(12, 4)
    go(13, 4)
    for ring in rings:
        for s in range(3):
            ring.drain(s)
        ring.close()
    for i in range(6):
        swap(i).wait_send()

    def close(k):
        forward2.one(k).wait_send()
        back1.one(k).wait_send()

    loop(0, PIECES, close)
    for store in stores:
        store.wait()


def back_part(*given):
    rows, width = given[0].shape
    half = (rows // 2, width)
    grads, attn = (4, 4, 4, 4, 96, 128), (4, 4, 4, 96, 128)
    S = pltpu.VMEM
    ring_sems = [DMA((4, 4, 3))] * 8 + [DMA((4, 4))] * 3
    attn_sems = [DMA((4, 3))] * 8 + [DMA((4,))] * 3
    return pl.pallas_call(
        back_kernel,
        out_shape=(
            jax.ShapeDtypeStruct((rows, width), BF16),
            jax.ShapeDtypeStruct((rows, width), F32),
            jax.ShapeDtypeStruct((8, width), F32),
            jax.ShapeDtypeStruct(grads, F32),
            jax.ShapeDtypeStruct(attn, F32),
        ),
        in_specs=[ANY] * len(given),
        out_specs=(ANY, ANY, VMEM, ANY, ANY),
        scratch_shapes=[S(a.shape, a.dtype) for a in given[:19]]
        + [S((2, 2, width, 128), BF16), S((2, 2, width, 128), BF16), S((2, 2, 128, width), BF16)]
        + [
            S(grads, F32), S(grads, F32), S((4, 4, 4, 96, 128), F32), S((4, 4, 96, 128), F32),
            S(attn, F32), S(attn, F32), S((4, 4, 96, 128), F32), S((4, 96, 128), F32),
            S((rows, width), BF16), S((rows, width), F32),
            S((rows, width), F32), S((rows, width), F32), S((width, rows), BF16),
            S((2,) + half, F32), S((2,) + half, F32), S(half, F32),
            S((16, width), F32), S((7, 8, width), F32), S((6, 8, width), F32),
        ]
        + ring_sems
        + attn_sems
        + [DMA((3, PIECES))] * 6
        + [DMA((19,)), DMA((2, 3)), DMA((3,)), DMA((6,)), DMA((6,))],
        compiler_params=pltpu.CompilerParams(
            collective_id=2, has_side_effects=True, vmem_limit_bytes=64 << 20
        ),
    )(*given)


def unpack_kernel(
    grads, attn, gains, forward, backward, gate, up, down, query, key, value, out, gain1, gain2,
    output, input_grad
):
    for h in range(2):
        rows = slice(512 * h, 512 * h + 512)
        gate[0, rows] = grads[0, h, :, 0:32].reshape(512, 128)
        up[0, rows] = grads[0, h, :, 32:64].reshape(512, 128)
        for a in range(4):
            lanes = slice(128 * (4 * h + a), 128 * (4 * h + a) + 128)
            down[0, :, lanes] = grads[0, h, 4 * a : 4 * a + 4, 64:96].reshape(128, 128)
    query[:, 0:128] = attn[:, 0:16].reshape(128, 128)
    query[:, 128:256] = attn[:, 16:32].reshape(128, 128)
    key[...] = attn[:, 32:48].reshape(128, 128)
    value[...] = attn[:, 48:64].reshape(128, 128)
    out[...] = attn[:, 64:96].reshape(256, 128)
    gain1[...] = gains[0:1]
    gain2[...] = gains[1:2]
    output[...] = forward[...]
    input_grad[...] = backward[...]


def unpack(grads, attn, gains, forward, backward):
    return pl.pallas_call(
        unpack_kernel,
        grid=(8,),
        out_shape=(
            jax.ShapeDtypeStruct((8, 1024, 128), F32),
            jax.ShapeDtypeStruct((8, 1024, 128), F32),
            jax.ShapeDtypeStruct((8, 128, 1024), F32),
            jax.ShapeDtypeStruct((1024, 256), F32),
            jax.ShapeDtypeStruct((1024, 128), F32),
            jax.ShapeDtypeStruct((1024, 128), F32),
            jax.ShapeDtypeStruct((256, 1024), F32),
            jax.ShapeDtypeStruct((1, 1024), F32),
            jax.ShapeDtypeStruct((1, 1024), F32),
            jax.ShapeDtypeStruct(forward.shape, BF16),
            jax.ShapeDtypeStruct(backward.shape, F32),
        ),
        in_specs=[
            pl.BlockSpec((1, 2, 16, 96, 128), lambda p: (p, 0, 0, 0, 0)),
            pl.BlockSpec((8, 96, 128), lambda p: (p, 0, 0)),
            pl.BlockSpec((8, 128), lambda p: (0, p)),
            pl.BlockSpec((64, 1024), lambda p: (p, 0)),
            pl.BlockSpec((64, 1024), lambda p: (p, 0)),
        ],
        out_specs=(
            pl.BlockSpec((1, 1024, 128), lambda p: (p, 0, 0)),
            pl.BlockSpec((1, 1024, 128), lambda p: (p, 0, 0)),
            pl.BlockSpec((1, 128, 1024), lambda p: (p, 0, 0)),
            pl.BlockSpec((128, 256), lambda p: (p, 0)),
            pl.BlockSpec((128, 128), lambda p: (p, 0)),
            pl.BlockSpec((128, 128), lambda p: (p, 0)),
            pl.BlockSpec((256, 128), lambda p: (0, p)),
            pl.BlockSpec((1, 128), lambda p: (0, p)),
            pl.BlockSpec((1, 128), lambda p: (0, p)),
            pl.BlockSpec((64, 1024), lambda p: (p, 0)),
            pl.BlockSpec((64, 1024), lambda p: (p, 0)),
        ),
        compiler_params=pltpu.CompilerParams(vmem_limit_bytes=62 << 20),
    )(grads, attn, gains, forward, backward)


def tables(seq_length):
    half_width = HD // 2
    exponent = -np.arange(half_width, dtype=np.float32) * np.float32(2.0) / np.float32(HD)
    frequency = np.power(np.float32(ROPE_THETA), exponent)
    angles = np.arange(seq_length, dtype=np.float32)[:, None] * frequency[None, :]
    cosine, sine = np.cos(angles), np.sin(angles)
    return (
        jnp.asarray(np.concatenate([cosine] * 4, 1)),
        jnp.asarray(np.concatenate([sine, -sine] * 2, 1)),
    )


def local(
    tokens,
    norm1_gain,
    w_query,
    w_key,
    w_value,
    w_out,
    norm2_gain,
    expert_gate,
    expert_up,
    expert_down,
    routes,
    gate_weights,
    segments,
    cotangent,
):
    experts = expert_gate.shape[0]
    cos_table, sin_table = tables(tokens.shape[0])
    gain1, gain2 = norm1_gain[None], norm2_gain[None]
    hidden1, queries, keys, values, lse, mixed, residual, hidden2, side = front_part(
        tokens, gain1, cos_table, sin_table, w_query, w_key, w_value, segments, w_out, gain2,
        routes.T, gate_weights.T,
    )
    output, input_grad, gains, grads, attn = back_part(
        hidden2, cotangent, side, residual, gain2, mixed, w_out, queries, keys, values, lse,
        segments, cos_table, sin_table, w_query, w_key, w_value, tokens, gain1, expert_gate,
        expert_up, expert_down, hidden1,
    )
    (
        gate_grad, up_grad, down_grad, query_grad, key_grad, value_grad, out_grad, gain1_grad,
        gain2_grad, output, input_grad,
    ) = unpack(
        grads.reshape(experts, 2, 16, 96, 128), attn.reshape(64, 96, 128), gains, output, input_grad
    )
    return (
        output,
        input_grad,
        gain1_grad.reshape(-1),
        query_grad,
        key_grad,
        value_grad,
        out_grad,
        gain2_grad.reshape(-1),
        gate_grad,
        up_grad,
        down_grad,
    )


def solution(mesh):
    return jax.shard_map(
        local,
        mesh=mesh,
        in_specs=(
            P("dp", None),
            P(),
            P(None, "tensor"),
            P(None, "tensor"),
            P(None, "tensor"),
            P("tensor", None),
            P(),
            P(None, None, "tensor"),
            P(None, None, "tensor"),
            P(None, "tensor", None),
            P("dp", None),
            P("dp", None),
            P("dp", None),
            P("dp", None),
        ),
        out_specs=(
            P("dp", None),
            P("dp", None),
            P(),
            P(None, "tensor"),
            P(None, "tensor"),
            P(None, "tensor"),
            P("tensor", None),
            P(),
            P(None, None, "tensor"),
            P(None, None, "tensor"),
            P(None, "tensor", None),
        ),
        check_vma=False,
    )
```

```python
import functools

import jax
import jax.numpy as jnp
import numpy as np
from jax import lax
from jax.experimental import pallas as pl
from jax.experimental.pallas import tpu as pltpu
from jax.sharding import PartitionSpec as P

MESH = pl.DeviceIdType.MESH
DMA = pltpu.SemaphoreType.DMA
F32 = jnp.float32
BF16 = jnp.bfloat16

HD = 64
NORM_EPS = 1e-06
ROPE_THETA = 10000.0
PIECES = 4
ORDER = (
    ((0, 0),),
    (),
    (),
    ((0, 1),),
    (),
    ((0, 2),),
    (),
    (),
    ((0, 3), (1, 0),),
    ((1, 1), (2, 0),),
    (),
    ((1, 2), (1, 3), (3, 0),),
    ((2, 2),),
    ((2, 1), (2, 3), (4, 0),),
    (),
    (),
    (),
    (),
    (),
    ((3, 2), (3, 1),),
    ((4, 2), (3, 3),),
    ((5, 0), (4, 1), (5, 2), (4, 3),),
    ((0, 4), (6, 2), (5, 3), (5, 1),),
    ((6, 0), (1, 4),),
    ((7, 2), (6, 1),),
    ((6, 3), (7, 0), (2, 4), (7, 1), (8, 0), (8, 2),),
    ((7, 3), (3, 4), (9, 0), (8, 1), (8, 3), (9, 2),),
    ((10, 0),),
    ((4, 4), (10, 2), (9, 3), (9, 1),),
    (),
    ((5, 4), (11, 2), (10, 1),),
    ((6, 4),),
    (),
    ((11, 0),),
    (),
    (),
    ((10, 3), (7, 4), (11, 1), (8, 4), (12, 0),),
    ((9, 4), (11, 3), (10, 4), (13, 0), (12, 2),),
    (),
    ((11, 4), (12, 3),),
    (),
    ((12, 4), (12, 1), (13, 3),),
    (),
    ((13, 2), (13, 4),),
    ((13, 1),),
)
VMEM = pl.BlockSpec(memory_space=pltpu.VMEM)
ANY = pl.BlockSpec(memory_space=pl.ANY)


def dot_nn(first_op, second_op):
    return jnp.dot(first_op, second_op, preferred_element_type=F32)


def dot_tn(first_op, second_op):
    return lax.dot_general(
        first_op, second_op, (((0,), (0,)), ((), ())), preferred_element_type=F32
    )


def dot_nt(first_op, second_op):
    return lax.dot_general(
        first_op, second_op, (((1,), (1,)), ((), ())), preferred_element_type=F32
    )


class Place:
    def __init__(self):
        self.dp = lax.axis_index("dp")
        self.tensor = lax.axis_index("tensor")
        zhi = self.dp % 2
        self.z_far = self.dp + 1 - 2 * zhi
        xy = self.dp // 2
        x, y = xy % 4, xy // 4
        self.x, self.y = x, y

        def at(dx, dy):
            return (((y + dy + 4) % 4) * 4 + (x + dx + 4) % 4) * 2 + zhi

        self.across = [at(1, 0), at(-1, 0), at(0, 1), at(0, -1)]
        self.pairs = [
            at(1 - 2 * (x % 2), 0), at(2, 0), at(0, 1 - 2 * (y % 2)), at(0, 2), self.z_far
        ]
        self.core = self.tensor % 2
        self.buddy = self.tensor + 1 - 2 * self.core
        self.z_near = self.tensor + 2 - 4 * (self.tensor // 2)


class AxisRing:
    def __init__(self, place, mine, land, land2, zland, out, sems):
        self.place, self.mine, self.land, self.land2 = place, mine, land, land2
        self.zland, self.out, self.sems = zland, out, sems

    def spots(self, f, back1, back2):
        step = 1 - 2 * (f % 2)
        pos1, pos2 = self.place.x, self.place.y
        if f >= 2:
            pos1, pos2 = pos2, pos1
        return (pos1 - step * back1 + 8) % 4, (pos2 - step * back2 + 8) % 4

    def send(self, f, s, stage, src, dst):
        axis = f // 2 if stage in (0, 3) else 1 - f // 2
        return pltpu.make_async_remote_copy(
            src, dst, self.sems[2 * stage].at[f, s], self.sems[2 * stage + 1].at[f, s],
            device_id=(self.place.across[2 * axis + f % 2], self.place.tensor),
            device_id_type=MESH,
        )

    def rs1(self, f, s, src):
        i = self.spots(f, 1 + s, 0)[0]
        return self.send(f, s, 0, src.at[f, i], self.land.at[f, i])

    def rs2(self, f, s, src):
        j = self.spots(f, 0, 1 + s)[1]
        return self.send(f, s, 1, src.at[j], self.land2.at[f, j])

    def ag2(self, f, s, src):
        i, j = self.spots(f, 0, s)
        return self.send(f, s, 2, src.at[f, i, j], self.out.at[f, i, j])

    def ag1(self, f, s, src):
        return self.send(f, s, 3, src, self.out.at[f, self.spots(f, s, 0)[0]])

    def zcopy(self, f):
        return pltpu.make_async_remote_copy(
            self.land2.at[f, self.spots(f, 0, 0)[1]], self.zland.at[f],
            self.sems[8].at[f], self.sems[9].at[f],
            device_id=(self.place.z_far, self.place.tensor), device_id_type=MESH,
        )

    def keep(self, f):
        i, j = self.spots(f, 0, 0)
        return pltpu.make_async_copy(
            self.mine.at[f, i, j], self.out.at[f, i, j], self.sems[10].at[f]
        )

    def begin(self):
        for f in range(4):
            self.rs1(f, 0, self.mine).start()

    def rs1_step(self, s):
        for f in range(4):
            self.rs1(f, s - 1, self.land).wait_recv()
            if s == 1:
                self.rs1(f, 0, self.mine).wait_send()
            i = self.spots(f, 1 + s, 0)[0]
            self.land[f, i] = self.land[f, i] + self.mine[f, i]
            if s < 3:
                self.rs1(f, s, self.land).start()
            else:
                self.rs2(f, 0, self.land.at[f, i]).start()

    def rs2_step(self, s):
        for f in range(4):
            i, j = self.spots(f, 0, 1 + s)
            self.rs2(f, s - 1, self.land2.at[f]).wait_recv()
            self.land2[f, j] = self.land2[f, j] + self.land[f, i, j]
            if s < 3:
                self.rs2(f, s, self.land2.at[f]).start()
            else:
                self.zcopy(f).start()

    def back(self):
        for f in range(4):
            self.zcopy(f).wait_recv()
            i, j = self.spots(f, 0, 0)
            self.mine[f, i, j] = self.land2[f, j] + self.zland[f]
            self.ag2(f, 0, self.mine).start()
            self.keep(f).start()

    def ag2_step(self, s):
        for f in range(4):
            self.ag2(f, s - 1, self.out).wait_recv()
            i = self.spots(f, 0, s)[0]
            if s < 3:
                self.ag2(f, s, self.out).start()
            else:
                self.keep(f).wait()
                self.ag1(f, 0, self.out.at[f, i]).start()

    def ag1_step(self, s):
        for f in range(4):
            held = self.out.at[f, self.spots(f, s, 0)[0]]
            self.ag1(f, s - 1, held).wait_recv()
            if s < 3:
                self.ag1(f, s, held).start()

    def op(self, k):
        if k == 0:
            self.begin()
        elif k <= 3:
            self.rs1_step(k)
        elif k <= 6:
            self.rs2_step(k - 3)
        elif k == 7:
            self.back()
        elif k <= 10:
            self.ag2_step(k - 7)
        else:
            self.ag1_step(k - 10)

    def drain(self, s):
        for f in range(4):
            if s > 0:
                self.rs1(f, s, self.land).wait_send()
            self.rs2(f, s, self.land2.at[f]).wait_send()
            self.ag2(f, s, self.mine if s == 0 else self.out).wait_send()
            self.ag1(f, s, self.out.at[f, 0]).wait_send()

    def close(self):
        for f in range(4):
            self.zcopy(f).wait_send()


class Sum4:
    def __init__(self, place, part, land1, land2, sems):
        self.place, self.part, self.land1, self.land2 = place, part, land1, land2
        self.s1, self.r1, self.s2, self.r2, self.s3, self.r3 = sems
        self.half = part.shape[0] // 2
        self.n = self.half // PIECES

    def local(self, k):
        return pl.ds(pl.multiple_of(k * self.n, self.n), self.n)

    def rows(self, k, core):
        return pl.ds(pl.multiple_of((2 * k + core) * self.n, self.n), self.n)

    def own(self, k):
        return self.rows(k, self.place.core)

    def other(self, k):
        return self.rows(k, 1 - self.place.core)

    def one(self, k):
        return pltpu.make_async_remote_copy(
            self.part.at[self.other(k)], self.land1.at[self.local(k)],
            self.s1.at[k], self.r1.at[k],
            device_id=(self.place.dp, self.place.buddy), device_id_type=MESH,
        )

    def two(self, k):
        return pltpu.make_async_remote_copy(
            self.land1.at[self.local(k)], self.land2.at[self.local(k)],
            self.s2.at[k], self.r2.at[k],
            device_id=(self.place.dp, self.place.z_near), device_id_type=MESH,
        )

    def three(self, k, src, dst):
        return pltpu.make_async_remote_copy(
            src, dst, self.s3.at[k], self.r3.at[k],
            device_id=(self.place.dp, self.place.buddy), device_id_type=MESH,
        )

    def begin(self):
        for k in range(PIECES):
            self.one(k).start()

    def middle(self, k):
        self.one(k).wait_recv()
        at = self.local(k)
        self.land1[at] = self.land1[at] + self.part[self.own(k)]
        self.two(k).start()

    def total(self, k):
        self.two(k).wait_recv()
        self.two(k).wait_send()
        at = self.local(k)
        return self.land1[at] + self.land2[at]


def greet(place, rings):
    barrier = pltpu.get_barrier_semaphore()
    peers = [(place.dp, place.buddy), (place.dp, place.z_near)]
    if rings:
        peers += [(q, place.tensor) for q in place.across + [place.z_far]]
        peers += [(place.pairs[1], place.tensor), (place.pairs[3], place.tensor)]
    for peer in peers:
        pl.semaphore_signal(barrier, inc=1, device_id=peer, device_id_type=MESH)
    pl.semaphore_wait(barrier, len(peers))


def loop(low, high, body):
    def one(i, carry):
        body(i)
        return carry

    lax.fori_loop(low, high, one, 0)


def swap_halves(values):
    lane = lax.broadcasted_iota(jnp.int32, values.shape, 1)
    return jnp.where(lane % 64 < 32, pltpu.roll(values, 96, 1), pltpu.roll(values, 32, 1))


def allowed_pairs(seg_col, seg_row, until, block):
    shape = (until, 256)
    return (seg_col[:until] == seg_row[:, 256 * block : 256 * block + 256]) & (
        lax.broadcasted_iota(jnp.int32, shape, 0)
        <= lax.broadcasted_iota(jnp.int32, shape, 1) + 256 * block
    )


def front_kernel(
    *refs
):
    given, refs = refs[:12], refs[12:]
    kept, refs = refs[:9], refs[9:]
    inside, refs = refs[:12], refs[12:]
    made, refs = refs[:9], refs[9:]
    part, land1, land2, in_sem, out_sem, own_sem = refs[:6]
    (
        tokens, gain1, cos_table, sin_table, w_query, w_key, w_value, seg_row, w_out, gain2,
        routes, route_weights,
    ) = inside
    hidden1, queries, keys, values, lse, mixed, residual, hidden2, side = made
    loads = [
        pltpu.make_async_copy(src, dst, in_sem.at[i])
        for i, (src, dst) in enumerate(zip(given, inside))
    ]
    stores = [
        pltpu.make_async_copy(src, dst, out_sem.at[i])
        for i, (src, dst) in enumerate(zip(made, kept))
        if i != 6
    ]
    stores.insert(6, None)
    for load in loads:
        load.start()
    place = Place()
    greet(place, False)
    work = Sum4(place, part, land1, land2, refs[6:])
    for load in loads:
        load.wait()
    rows = [
        jnp.sum(
            jnp.where(routes[...] == e, route_weights[...], 0.0), 0, keepdims=True
        )
        for e in range(8)
    ]
    rows.append(seg_row[...].astype(F32))
    rows.append(jnp.zeros((119, 512), F32))
    side[...] = jnp.concatenate(rows, 0).T
    stores[8].start()
    seg_col = side[:, 8:9].astype(jnp.int32)
    for b in range(2):
        at = slice(256 * b, 256 * b + 256)
        until = 256 * b + 256

        def rotate(projected):
            turned = projected * cos_table[at] - swap_halves(projected) * sin_table[at]
            return turned.astype(BF16)

        normed = (row_norm(tokens[at].astype(F32))[0] * gain1[...]).astype(BF16)
        hidden1[at] = normed
        projected = dot_nn(normed, w_query[...])
        for g in range(2):
            queries[at, 128 * g : 128 * g + 128] = rotate(projected[:, 128 * g : 128 * g + 128])
        keys[at] = rotate(dot_nn(normed, w_key[...]))
        values[at] = dot_nn(normed, w_value[...]).astype(BF16)
        if b == 1:
            work.middle(0)
            work.middle(1)
        allowed = allowed_pairs(seg_col, seg_row, until, b)
        heads = []
        for h in range(4):
            own = slice(64 * (h // 2), 64 * (h // 2) + 64)
            raw = dot_nt(keys[:until, own], queries[at, 64 * h : 64 * h + 64]) * HD ** (-0.5)
            scores = jnp.where(allowed, raw, -1e30)
            top = jnp.max(scores, 0, keepdims=True)
            weights = jnp.exp(scores - top)
            row_total = jnp.sum(weights, 0, keepdims=True)
            lse[h : h + 1, at] = top + jnp.log(row_total)
            heads.append(dot_tn((weights / row_total).astype(BF16), values[:until, own]))
        mixed[at] = jnp.concatenate(heads, 1).astype(BF16)
        part[at] = dot_nn(mixed[at], w_out[...])
        work.one(2 * b).start()
        work.one(2 * b + 1).start()
    work.middle(2)
    work.middle(3)
    for store in stores[:6]:
        store.start()

    def give(rows):
        hidden2[rows] = (row_norm(residual[rows])[0] * gain2[...]).astype(BF16)

    def finish(k):
        at = work.own(k)
        residual[at] = tokens[at].astype(F32) + work.total(k)
        work.three(k, residual.at[at], residual.at[at]).start()
        give(at)

    loop(0, PIECES, finish)

    def own_rows(k):
        return pltpu.make_async_copy(
            residual.at[work.own(k)], kept[6].at[work.local(k)], own_sem.at[k]
        )

    def close(k):
        at = work.own(k)
        work.three(k, residual.at[at], residual.at[at]).wait()
        own_rows(k).start()
        give(work.other(k))
        work.one(k).wait_send()

    loop(0, PIECES, close)
    stores[7].start()
    for i, store in enumerate(stores):
        if i != 6:
            store.wait()
    loop(0, PIECES, lambda k: own_rows(k).wait())


def front_part(*given):
    rows, width = given[0].shape
    half = (rows // 2, width)
    made = (
        jax.ShapeDtypeStruct((rows, width), BF16),
        jax.ShapeDtypeStruct((rows, 256), BF16),
        jax.ShapeDtypeStruct((rows, 128), BF16),
        jax.ShapeDtypeStruct((rows, 128), BF16),
        jax.ShapeDtypeStruct((8, rows), F32),
        jax.ShapeDtypeStruct((rows, 256), BF16),
        jax.ShapeDtypeStruct((rows, width), F32),
        jax.ShapeDtypeStruct((rows, width), BF16),
        jax.ShapeDtypeStruct((rows, 128), F32),
    )
    return pl.pallas_call(
        front_kernel,
        out_shape=made[:6] + (jax.ShapeDtypeStruct(half, F32),) + made[7:],
        in_specs=[ANY] * len(given),
        out_specs=(ANY,) * len(made),
        scratch_shapes=[pltpu.VMEM(a.shape, a.dtype) for a in given + made]
        + [pltpu.VMEM((rows, width), F32)]
        + [pltpu.VMEM(half, F32)] * 2
        + [DMA((len(given),)), DMA((len(made),)), DMA((PIECES,))]
        + [DMA((PIECES,))] * 6,
        compiler_params=pltpu.CompilerParams(
            collective_id=1, has_side_effects=True, vmem_limit_bytes=60 << 20
        ),
    )(*given)


def row_norm(values):
    inverse = lax.rsqrt(jnp.mean(values * values, -1, keepdims=True) + NORM_EPS)
    return values * inverse, inverse


def norm_back(gradient, scaled, inverse, gain_vec):
    scaled_grad = gradient * gain_vec
    inner_sum = jnp.mean(scaled_grad * scaled, -1, keepdims=True)
    return inverse * (scaled_grad - scaled * inner_sum)


def fold(values):
    return jnp.sum(values.reshape(-1, 8, values.shape[-1]), 0)


def back_kernel(*refs):
    given, refs = refs[:23], refs[23:]
    output_hbm, input_grad_hbm, gain_sums, grads_sum, attn_sum = refs[:5]
    inside, refs = refs[5:24], refs[24:]
    (
        hidden2, dy, side, residual, gain2, mixed, w_out, queries, keys, values, lse, seg_row,
        cos_table, sin_table, w_query, w_key, w_value, tokens, gain1,
    ) = inside
    gate_w, up_w, down_w = refs[:3]
    (
        mine, land, ring_land2, zland, attn, attn_land, attn_land2, attn_zland, output, dresidual,
        dhidden2, out_part, hidden2_t, land1, land2, land3, folded, gains, gains_in,
    ) = refs[3:22]
    sems = refs[22:]
    ring_sems, sems = sems[:11], sems[11:]
    attn_sems, sems = sems[:11], sems[11:]
    sum_sems, sems = sems[:6], sems[6:]
    load_sem, weight_sem, late_sem, gain_s, gain_r = sems
    dqkv = hidden2_t.at[0:512]
    weights = given[19:22]
    hidden1_hbm = given[22]

    def weight_loads(p):
        slot = p % 2
        return [
            pltpu.make_async_copy(
                src.at[2 * p : 2 * p + 2], dst.at[slot], weight_sem.at[slot, i]
            )
            for i, (src, dst) in enumerate(zip(weights, (gate_w, up_w, down_w)))
        ]

    loads = [
        pltpu.make_async_copy(src, dst, load_sem.at[i])
        for i, (src, dst) in enumerate(zip(given[:19], inside))
    ]
    for load in loads[:3]:
        load.start()
    for p in range(2):
        for load in weight_loads(p):
            load.start()
    for load in loads[3:]:
        load.start()
    place = Place()
    greet(place, True)
    rings = [
        AxisRing(
            place, mine.at[u], land.at[u], ring_land2.at[u], zland.at[u], grads_sum.at[u],
            [sem.at[u] for sem in ring_sems],
        )
        for u in range(4)
    ]
    rings.append(
        AxisRing(place, attn, attn_land, attn_land2, attn_zland, attn_sum, attn_sems)
    )

    def after(place_in_order):
        for k, u in ORDER[place_in_order]:
            rings[u].op(k)

    sums = [
        Sum4(place, part, land1.at[which], land2.at[which], [sem.at[i] for sem in sum_sems])
        for i, (part, which) in enumerate(((dhidden2, 0), (out_part, 1), (dhidden2, 0)))
    ]
    back2, forward2, back1 = sums

    folded[...] = jnp.zeros_like(folded)
    for load in loads[:3]:
        load.wait()
    hidden2_t[...] = hidden2[...].T
    for p in range(4):
        slot = p % 2
        for load in weight_loads(p):
            load.wait()
        down_pair = down_w[slot].reshape(256, 1024)
        dact_pair = dot_nt(dy[...], down_pair)
        acts, dboths, both_ws = [], [], []
        for i in range(2):
            e = 2 * p + i
            both_w = jnp.concatenate([gate_w[slot, i], up_w[slot, i]], 1)
            both = dot_nn(hidden2[...], both_w)
            gate, up = both[:, :128], both[:, 128:]
            sig = 1.0 / (1.0 + jnp.exp(-gate))
            silu = gate * sig
            weight = side[:, e : e + 1]
            acts.append((silu * up * weight).astype(BF16))
            dact = dact_pair[:, 128 * i : 128 * i + 128] * weight
            dgate = (dact * up * (sig * (1.0 + gate * (1.0 - sig)))).astype(BF16)
            dup = (dact * silu).astype(BF16)
            dboth = jnp.concatenate([dgate, dup], 1)
            grad = dot_nn(hidden2_t[...], dboth)
            for h in range(2):
                rows = slice(512 * h, 512 * h + 512)
                mine[p, 2 * i + h, :, :, 0:32] = grad[rows, :128].reshape(4, 4, 32, 128)
                mine[p, 2 * i + h, :, :, 32:64] = grad[rows, 128:].reshape(4, 4, 32, 128)
            part = dot_nt(dboth, both_w)
            dhidden2[...] = part if e == 0 else dhidden2[...] + part
        act_pair = jnp.concatenate(acts, 1)
        down_grad = dot_tn(act_pair, dy[...])
        for i in range(2):
            for j in range(8):
                piece = down_grad[128 * i : 128 * i + 128, 128 * j : 128 * j + 128]
                mine[p, 2 * i + j // 4, j % 4, :, 64:96] = piece.reshape(4, 32, 128)
        after(2 * p)
        part = dot_nn(act_pair, down_pair)
        out_part[...] = part if p == 0 else out_part[...] + part
        if p < 2:
            for load in weight_loads(p + 2):
                load.start()
        after(2 * p + 1)
    late = [
        pltpu.make_async_copy(hidden1_hbm, hidden2, late_sem.at[0]),
    ]
    for load in late:
        load.start()
    back2.begin()
    after(8)
    for load in loads[3:]:
        load.wait()
    seg_col = side[:, 8:9].astype(jnp.int32)
    loop(0, PIECES, back2.middle)
    after(9)

    def finish2(k):
        d = back2.total(k)
        at = back2.own(k)
        scaled, inverse = row_norm(residual[back2.local(k)])
        folded[8:16] += fold(d * scaled)
        dresidual[at] = dy[at].astype(F32) + norm_back(d, scaled, inverse, gain2[...])
        back2.three(k, dresidual.at[at], dresidual.at[at]).start()

    finish2(0)
    after(10)
    finish2(1)
    after(11)
    finish2(2)
    after(12)
    finish2(3)
    after(13)

    def close2(k):
        at = back2.own(k)
        back2.three(k, dresidual.at[at], dresidual.at[at]).wait()
        back2.one(k).wait_send()

    loop(0, PIECES, close2)
    after(14)
    forward2.begin()
    after(15)

    dbranch = dresidual[...].astype(BF16)
    dmixed = dot_nt(dbranch, w_out[...]).astype(BF16)
    out_grad = dot_tn(mixed[...], dbranch)
    for j in range(8):
        piece = out_grad[:, 128 * j : 128 * j + 128].reshape(2, 4, 32, 128)
        attn[j // 2, 2 * (j % 2) : 2 * (j % 2) + 2, :, 64:96] = piece

    after(16)
    loop(0, PIECES, forward2.middle)
    after(17)

    def unrotate(grad):
        return (grad * cos_table[...] + swap_halves(grad) * sin_table[...]).astype(BF16)

    dkeys, dvalues = [], []
    for g in range(2):
        key = keys[:, 64 * g : 64 * g + 64]
        value = values[:, 64 * g : 64 * g + 64]
        dkey = [0.0, 0.0]
        dvalue = [0.0, 0.0]
        dquery = []
        for h in (2 * g, 2 * g + 1):
            blocks = []
            for b in range(2):
                at = slice(256 * b, 256 * b + 256)
                until = 256 * b + 256
                query = queries[at, 64 * h : 64 * h + 64]
                dmix = dmixed[at, 64 * h : 64 * h + 64]
                raw = dot_nt(key[:until], query) * HD ** (-0.5)
                allowed = allowed_pairs(seg_col, seg_row, until, b)
                probs = jnp.exp(jnp.where(allowed, raw, -1e30) - lse[h : h + 1, at])
                dprobs = dot_nt(value[:until], dmix)
                inner = jnp.sum(probs * dprobs, 0, keepdims=True)
                dscores = (probs * (dprobs - inner)).astype(BF16)
                dvalue_part = dot_nn(probs.astype(BF16), dmix)
                dkey_part = dot_nn(dscores, query)
                for t in range(b + 1):
                    dvalue[t] = dvalue[t] + dvalue_part[256 * t : 256 * t + 256]
                    dkey[t] = dkey[t] + dkey_part[256 * t : 256 * t + 256]
                blocks.append(dot_tn(dscores, key[:until]))
                if b == 1:
                    after(18 + h)
            dquery.append(jnp.concatenate(blocks, 0) * HD ** (-0.5))
        dqkv[:, 128 * g : 128 * g + 128] = unrotate(jnp.concatenate(dquery, 1))
        dkeys.append(jnp.concatenate(dkey, 0) * HD ** (-0.5))
        dvalues.append(jnp.concatenate(dvalue, 0))
    dqkv[:, 256:384] = unrotate(jnp.concatenate(dkeys, 1))
    dqkv[:, 384:512] = jnp.concatenate(dvalues, 1).astype(BF16)

    for load in late:
        load.wait()
    hidden_grad = dot_tn(hidden2[...], dqkv[...])
    for j in range(4):
        piece = hidden_grad[:, 128 * j : 128 * j + 128].reshape(4, 4, 4, 16, 128)
        attn[:, :, :, 16 * j : 16 * j + 16] = piece
    after(22)
    dhidden2[...] = (
        dot_nt(dqkv[:, :256], w_query[...])
        + dot_nt(dqkv[:, 256:384], w_key[...])
        + dot_nt(dqkv[:, 384:512], w_value[...])
    )
    after(23)
    back1.begin()
    after(24)

    def finish_out(k):
        done = forward2.total(k) + residual[forward2.local(k)]
        at = forward2.local(k)
        output[forward2.own(k)] = done.astype(BF16)
        forward2.land1[at] = done
        forward2.three(k, forward2.land1.at[at], land3.at[at]).start()

    def close_out(k):
        at = forward2.local(k)
        forward2.three(k, forward2.land1.at[at], land3.at[at]).wait()
        output[forward2.other(k)] = land3[at].astype(BF16)

    loop(0, PIECES, finish_out)
    after(25)
    loop(0, PIECES, back1.middle)
    after(26)
    loop(0, PIECES, close_out)
    after(27)
    stores = [
        pltpu.make_async_copy(output, output_hbm, late_sem.at[1]),
        pltpu.make_async_copy(dresidual, input_grad_hbm, late_sem.at[2]),
    ]
    stores[0].start()

    def finish1(k):
        d = back1.total(k)
        at = back1.own(k)
        scaled, inverse = row_norm(tokens[at].astype(F32))
        folded[0:8] += fold(d * scaled)
        dresidual[at] = dresidual[at] + norm_back(d, scaled, inverse, gain1[...])
        back1.three(k, dresidual.at[at], dresidual.at[at]).start()

    finish1(0)
    after(28)
    finish1(1)
    after(29)
    finish1(2)
    after(30)
    finish1(3)
    after(31)
    gains[0] = jnp.concatenate(
        [
            jnp.sum(folded[0:8], 0, keepdims=True),
            jnp.sum(folded[8:16], 0, keepdims=True),
            jnp.zeros((6, gains.shape[2]), F32),
        ],
        0,
    )

    def swap(i):
        device = (place.dp, place.buddy) if i == 0 else (place.pairs[i - 1], place.tensor)
        return pltpu.make_async_remote_copy(
            gains.at[i], gains_in.at[i], gain_s.at[i], gain_r.at[i],
            device_id=device, device_id_type=MESH,
        )

    def add_swap(i):
        swap(i).wait_recv()
        gains[i + 1] = gains[i] + gains_in[i]

    swap(0).start()
    after(32)
    add_swap(0)
    after(33)
    swap(1).start()
    after(34)

    def close1(k):
        at = back1.own(k)
        back1.three(k, dresidual.at[at], dresidual.at[at]).wait()

    loop(0, PIECES, close1)
    after(35)
    stores[1].start()
    add_swap(1)
    after(36)
    swap(2).start()
    after(37)
    add_swap(2)
    after(38)
    swap(3).start()
    after(39)
    add_swap(3)
    after(40)
    swap(4).start()
    after(41)
    add_swap(4)
    after(42)
    swap(5).start()
    after(43)
    add_swap(5)
    gain_sums[...] = gains[6]
    after(44)
    for ring in rings:
        for s in range(3):
            ring.drain(s)
        ring.close()
    for i in range(6):
        swap(i).wait_send()

    def close(k):
        forward2.one(k).wait_send()
        back1.one(k).wait_send()

    loop(0, PIECES, close)
    for store in stores:
        store.wait()


def back_part(*given):
    rows, width = given[0].shape
    half = (rows // 2, width)
    grads, attn = (4, 4, 4, 4, 96, 128), (4, 4, 4, 96, 128)
    S = pltpu.VMEM
    ring_sems = [DMA((4, 4, 3))] * 8 + [DMA((4, 4))] * 3
    attn_sems = [DMA((4, 3))] * 8 + [DMA((4,))] * 3
    return pl.pallas_call(
        back_kernel,
        out_shape=(
            jax.ShapeDtypeStruct((rows, width), BF16),
            jax.ShapeDtypeStruct((rows, width), F32),
            jax.ShapeDtypeStruct((8, width), F32),
            jax.ShapeDtypeStruct(grads, F32),
            jax.ShapeDtypeStruct(attn, F32),
        ),
        in_specs=[ANY] * len(given),
        out_specs=(ANY, ANY, VMEM, ANY, ANY),
        scratch_shapes=[S(a.shape, a.dtype) for a in given[:19]]
        + [S((2, 2, width, 128), BF16), S((2, 2, width, 128), BF16), S((2, 2, 128, width), BF16)]
        + [
            S(grads, F32), S(grads, F32), S((4, 4, 4, 96, 128), F32), S((4, 4, 96, 128), F32),
            S(attn, F32), S(attn, F32), S((4, 4, 96, 128), F32), S((4, 96, 128), F32),
            S((rows, width), BF16), S((rows, width), F32),
            S((rows, width), F32), S((rows, width), F32), S((width, rows), BF16),
            S((2,) + half, F32), S((2,) + half, F32), S(half, F32),
            S((16, width), F32), S((7, 8, width), F32), S((6, 8, width), F32),
        ]
        + ring_sems
        + attn_sems
        + [DMA((3, PIECES))] * 6
        + [DMA((19,)), DMA((2, 3)), DMA((3,)), DMA((6,)), DMA((6,))],
        compiler_params=pltpu.CompilerParams(
            collective_id=2, has_side_effects=True, vmem_limit_bytes=64 << 20
        ),
    )(*given)


def unpack_kernel(
    grads, attn, gains, forward, backward, gate, up, down, query, key, value, out, gain1, gain2,
    output, input_grad
):
    for h in range(2):
        rows = slice(512 * h, 512 * h + 512)
        gate[0, rows] = grads[0, h, :, 0:32].reshape(512, 128)
        up[0, rows] = grads[0, h, :, 32:64].reshape(512, 128)
        for a in range(4):
            lanes = slice(128 * (4 * h + a), 128 * (4 * h + a) + 128)
            down[0, :, lanes] = grads[0, h, 4 * a : 4 * a + 4, 64:96].reshape(128, 128)
    query[:, 0:128] = attn[:, 0:16].reshape(128, 128)
    query[:, 128:256] = attn[:, 16:32].reshape(128, 128)
    key[...] = attn[:, 32:48].reshape(128, 128)
    value[...] = attn[:, 48:64].reshape(128, 128)
    out[...] = attn[:, 64:96].reshape(256, 128)
    gain1[...] = gains[0:1]
    gain2[...] = gains[1:2]
    output[...] = forward[...]
    input_grad[...] = backward[...]


def unpack(grads, attn, gains, forward, backward):
    return pl.pallas_call(
        unpack_kernel,
        grid=(8,),
        out_shape=(
            jax.ShapeDtypeStruct((8, 1024, 128), F32),
            jax.ShapeDtypeStruct((8, 1024, 128), F32),
            jax.ShapeDtypeStruct((8, 128, 1024), F32),
            jax.ShapeDtypeStruct((1024, 256), F32),
            jax.ShapeDtypeStruct((1024, 128), F32),
            jax.ShapeDtypeStruct((1024, 128), F32),
            jax.ShapeDtypeStruct((256, 1024), F32),
            jax.ShapeDtypeStruct((1, 1024), F32),
            jax.ShapeDtypeStruct((1, 1024), F32),
            jax.ShapeDtypeStruct(forward.shape, BF16),
            jax.ShapeDtypeStruct(backward.shape, F32),
        ),
        in_specs=[
            pl.BlockSpec((1, 2, 16, 96, 128), lambda p: (p, 0, 0, 0, 0)),
            pl.BlockSpec((8, 96, 128), lambda p: (p, 0, 0)),
            pl.BlockSpec((8, 128), lambda p: (0, p)),
            pl.BlockSpec((64, 1024), lambda p: (p, 0)),
            pl.BlockSpec((64, 1024), lambda p: (p, 0)),
        ],
        out_specs=(
            pl.BlockSpec((1, 1024, 128), lambda p: (p, 0, 0)),
            pl.BlockSpec((1, 1024, 128), lambda p: (p, 0, 0)),
            pl.BlockSpec((1, 128, 1024), lambda p: (p, 0, 0)),
            pl.BlockSpec((128, 256), lambda p: (p, 0)),
            pl.BlockSpec((128, 128), lambda p: (p, 0)),
            pl.BlockSpec((128, 128), lambda p: (p, 0)),
            pl.BlockSpec((256, 128), lambda p: (0, p)),
            pl.BlockSpec((1, 128), lambda p: (0, p)),
            pl.BlockSpec((1, 128), lambda p: (0, p)),
            pl.BlockSpec((64, 1024), lambda p: (p, 0)),
            pl.BlockSpec((64, 1024), lambda p: (p, 0)),
        ),
        compiler_params=pltpu.CompilerParams(vmem_limit_bytes=62 << 20),
    )(grads, attn, gains, forward, backward)


def tables(seq_length):
    half_width = HD // 2
    exponent = -np.arange(half_width, dtype=np.float32) * np.float32(2.0) / np.float32(HD)
    frequency = np.power(np.float32(ROPE_THETA), exponent)
    angles = np.arange(seq_length, dtype=np.float32)[:, None] * frequency[None, :]
    cosine, sine = np.cos(angles), np.sin(angles)
    return (
        jnp.asarray(np.concatenate([cosine] * 4, 1)),
        jnp.asarray(np.concatenate([sine, -sine] * 2, 1)),
    )


def local(
    tokens,
    norm1_gain,
    w_query,
    w_key,
    w_value,
    w_out,
    norm2_gain,
    expert_gate,
    expert_up,
    expert_down,
    routes,
    gate_weights,
    segments,
    cotangent,
):
    experts = expert_gate.shape[0]
    cos_table, sin_table = tables(tokens.shape[0])
    gain1, gain2 = norm1_gain[None], norm2_gain[None]
    hidden1, queries, keys, values, lse, mixed, residual, hidden2, side = front_part(
        tokens, gain1, cos_table, sin_table, w_query, w_key, w_value, segments, w_out, gain2,
        routes.T, gate_weights.T,
    )
    output, input_grad, gains, grads, attn = back_part(
        hidden2, cotangent, side, residual, gain2, mixed, w_out, queries, keys, values, lse,
        segments, cos_table, sin_table, w_query, w_key, w_value, tokens, gain1, expert_gate,
        expert_up, expert_down, hidden1,
    )
    (
        gate_grad, up_grad, down_grad, query_grad, key_grad, value_grad, out_grad, gain1_grad,
        gain2_grad, output, input_grad,
    ) = unpack(
        grads.reshape(experts, 2, 16, 96, 128), attn.reshape(64, 96, 128), gains, output, input_grad
    )
    return (
        output,
        input_grad,
        gain1_grad.reshape(-1),
        query_grad,
        key_grad,
        value_grad,
        out_grad,
        gain2_grad.reshape(-1),
        gate_grad,
        up_grad,
        down_grad,
    )


def solution(mesh):
    return jax.shard_map(
        local,
        mesh=mesh,
        in_specs=(
            P("dp", None),
            P(),
            P(None, "tensor"),
            P(None, "tensor"),
            P(None, "tensor"),
            P("tensor", None),
            P(),
            P(None, None, "tensor"),
            P(None, None, "tensor"),
            P(None, "tensor", None),
            P("dp", None),
            P("dp", None),
            P("dp", None),
            P("dp", None),
        ),
        out_specs=(
            P("dp", None),
            P("dp", None),
            P(),
            P(None, "tensor"),
            P(None, "tensor"),
            P(None, "tensor"),
            P("tensor", None),
            P(),
            P(None, None, "tensor"),
            P(None, None, "tensor"),
            P(None, "tensor", None),
        ),
        check_vma=False,
    )
```

```python
import functools

import jax
import jax.numpy as jnp
import numpy as np
from jax import lax
from jax.experimental import pallas as pl
from jax.experimental.pallas import tpu as pltpu
from jax.sharding import PartitionSpec as P

MESH = pl.DeviceIdType.MESH
DMA = pltpu.SemaphoreType.DMA
F32 = jnp.float32
BF16 = jnp.bfloat16

HD = 64
NORM_EPS = 1e-06
ROPE_THETA = 10000.0
PIECES = 4
ORDER = (
    ((0, 0),),
    (),
    (),
    ((0, 1),),
    (),
    ((0, 2),),
    (),
    (),
    ((0, 3), (1, 0),),
    ((1, 1), (2, 0),),
    (),
    ((1, 2), (1, 3), (3, 0),),
    ((2, 2),),
    ((2, 1), (2, 3), (4, 0),),
    (),
    (),
    (),
    (),
    (),
    ((3, 2), (3, 1),),
    ((4, 2), (3, 3),),
    ((5, 0), (4, 1), (5, 2), (4, 3),),
    ((0, 4), (6, 2), (5, 3), (5, 1),),
    ((6, 0), (1, 4),),
    ((7, 2), (6, 1),),
    ((6, 3), (7, 0), (2, 4), (7, 1), (8, 0), (8, 2),),
    ((7, 3), (3, 4), (9, 0), (8, 1), (8, 3), (9, 2),),
    ((10, 0),),
    ((4, 4), (10, 2), (9, 3), (9, 1),),
    (),
    ((5, 4), (11, 2), (10, 1),),
    ((6, 4),),
    (),
    ((11, 0),),
    (),
    (),
    ((10, 3), (7, 4), (11, 1), (8, 4), (12, 0),),
    ((9, 4), (11, 3), (10, 4), (13, 0), (12, 2),),
    (),
    ((11, 4), (12, 3),),
    (),
    ((12, 4), (12, 1), (13, 3),),
    (),
    ((13, 2), (13, 4),),
    ((13, 1),),
)
VMEM = pl.BlockSpec(memory_space=pltpu.VMEM)
ANY = pl.BlockSpec(memory_space=pl.ANY)


def dot_nn(first_op, second_op):
    return jnp.dot(first_op, second_op, preferred_element_type=F32)


def dot_tn(first_op, second_op):
    return lax.dot_general(
        first_op, second_op, (((0,), (0,)), ((), ())), preferred_element_type=F32
    )


def dot_nt(first_op, second_op):
    return lax.dot_general(
        first_op, second_op, (((1,), (1,)), ((), ())), preferred_element_type=F32
    )


class Place:
    def __init__(self):
        self.dp = lax.axis_index("dp")
        self.tensor = lax.axis_index("tensor")
        zhi = self.dp % 2
        self.z_far = self.dp + 1 - 2 * zhi
        xy = self.dp // 2
        x, y = xy % 4, xy // 4
        self.x, self.y = x, y

        def at(dx, dy):
            return (((y + dy + 4) % 4) * 4 + (x + dx + 4) % 4) * 2 + zhi

        self.across = [at(1, 0), at(-1, 0), at(0, 1), at(0, -1)]
        self.pairs = [
            at(1 - 2 * (x % 2), 0), at(2, 0), at(0, 1 - 2 * (y % 2)), at(0, 2), self.z_far
        ]
        self.core = self.tensor % 2
        self.buddy = self.tensor + 1 - 2 * self.core
        self.z_near = self.tensor + 2 - 4 * (self.tensor // 2)


class AxisRing:
    def __init__(self, place, mine, land, land2, zland, out, sems):
        self.place, self.mine, self.land, self.land2 = place, mine, land, land2
        self.zland, self.out = zland, out
        self.sent, self.got1, self.got2, self.got3, self.got4, self.gotz, self.keep_s = sems

    def spots(self, f, back1, back2):
        step = 1 - 2 * (f % 2)
        pos1, pos2 = self.place.x, self.place.y
        if f >= 2:
            pos1, pos2 = pos2, pos1
        return (pos1 - step * back1 + 8) % 4, (pos2 - step * back2 + 8) % 4

    def send(self, f, n):
        axis = f // 2
        if n < 3:
            i = self.spots(f, 1 + n, 0)[0]
            src = (self.mine if n == 0 else self.land).at[f, i]
            dst, got = self.land.at[f, i], self.got1.at[f, n]
        elif n < 6:
            i, j = self.spots(f, 0, n - 2)
            src = self.land.at[f, i, j] if n == 3 else self.land2.at[f, j]
            dst, got, axis = self.land2.at[f, j], self.got2.at[f, n - 3], 1 - axis
        elif n == 6:
            j = self.spots(f, 0, 0)[1]
            src, dst, got = self.land2.at[f, j], self.zland.at[f], self.gotz.at[f]
        elif n < 10:
            i, j = self.spots(f, 0, n - 7)
            src = (self.mine if n == 7 else self.out).at[f, i, j]
            dst, got, axis = self.out.at[f, i, j], self.got4.at[f, n - 7], 1 - axis
        else:
            i = self.spots(f, n - 10, 0)[0]
            src, dst, got = self.out.at[f, i], self.out.at[f, i], self.got3.at[f, n - 10]
        to = self.place.z_far if n == 6 else self.place.across[2 * axis + f % 2]
        return pltpu.make_async_remote_copy(
            src, dst, self.sent.at[f], got,
            device_id=(to, self.place.tensor), device_id_type=MESH,
        )

    def keep(self, f):
        i, j = self.spots(f, 0, 0)
        return pltpu.make_async_copy(
            self.mine.at[f, i, j], self.out.at[f, i, j], self.keep_s.at[f]
        )

    def op(self, k):
        for f in range(4):
            if k > 0:
                self.send(f, k - 1).wait_recv()
            if 1 <= k <= 3:
                i = self.spots(f, 1 + k, 0)[0]
                self.land[f, i] = self.land[f, i] + self.mine[f, i]
            elif 4 <= k <= 6:
                i, j = self.spots(f, 0, k - 2)
                self.land2[f, j] = self.land2[f, j] + self.land[f, i, j]
            elif k == 7:
                i, j = self.spots(f, 0, 0)
                self.mine[f, i, j] = self.land2[f, j] + self.zland[f]
                self.keep(f).start()
            elif k == 10:
                self.keep(f).wait()
            if k > 0:
                self.send(f, k - 1).wait_send()
            if k < 13:
                self.send(f, k).start()


class Sum4:
    def __init__(self, place, part, land1, land2, sems):
        self.place, self.part, self.land1, self.land2 = place, part, land1, land2
        self.s1, self.r1, self.s2, self.r2, self.s3, self.r3 = sems
        self.half = part.shape[0] // 2
        self.n = self.half // PIECES

    def local(self, k):
        return pl.ds(pl.multiple_of(k * self.n, self.n), self.n)

    def rows(self, k, core):
        return pl.ds(pl.multiple_of((2 * k + core) * self.n, self.n), self.n)

    def own(self, k):
        return self.rows(k, self.place.core)

    def other(self, k):
        return self.rows(k, 1 - self.place.core)

    def one(self, k):
        return pltpu.make_async_remote_copy(
            self.part.at[self.other(k)], self.land1.at[self.local(k)],
            self.s1.at[k], self.r1.at[k],
            device_id=(self.place.dp, self.place.buddy), device_id_type=MESH,
        )

    def two(self, k):
        return pltpu.make_async_remote_copy(
            self.land1.at[self.local(k)], self.land2.at[self.local(k)],
            self.s2.at[k], self.r2.at[k],
            device_id=(self.place.dp, self.place.z_near), device_id_type=MESH,
        )

    def three(self, k, src, dst):
        return pltpu.make_async_remote_copy(
            src, dst, self.s3.at[k], self.r3.at[k],
            device_id=(self.place.dp, self.place.buddy), device_id_type=MESH,
        )

    def begin(self):
        for k in range(PIECES):
            self.one(k).start()

    def middle(self, k):
        self.one(k).wait_recv()
        at = self.local(k)
        self.land1[at] = self.land1[at] + self.part[self.own(k)]
        self.two(k).start()

    def total(self, k):
        self.two(k).wait_recv()
        self.two(k).wait_send()
        at = self.local(k)
        return self.land1[at] + self.land2[at]


def greet(place, rings):
    barrier = pltpu.get_barrier_semaphore()
    peers = [(place.dp, place.buddy), (place.dp, place.z_near)]
    if rings:
        peers += [(q, place.tensor) for q in place.across + [place.z_far]]
        peers += [(place.pairs[1], place.tensor), (place.pairs[3], place.tensor)]
    for peer in peers:
        pl.semaphore_signal(barrier, inc=1, device_id=peer, device_id_type=MESH)
    pl.semaphore_wait(barrier, len(peers))


def loop(low, high, body):
    def one(i, carry):
        body(i)
        return carry

    lax.fori_loop(low, high, one, 0)


def swap_halves(values):
    lane = lax.broadcasted_iota(jnp.int32, values.shape, 1)
    return jnp.where(lane % 64 < 32, pltpu.roll(values, 96, 1), pltpu.roll(values, 32, 1))


def allowed_pairs(seg_col, seg_row, until, block):
    shape = (until, 256)
    return (seg_col[:until] == seg_row[:, 256 * block : 256 * block + 256]) & (
        lax.broadcasted_iota(jnp.int32, shape, 0)
        <= lax.broadcasted_iota(jnp.int32, shape, 1) + 256 * block
    )


def front_kernel(
    *refs
):
    given, refs = refs[:12], refs[12:]
    kept, refs = refs[:9], refs[9:]
    inside, refs = refs[:12], refs[12:]
    made, refs = refs[:9], refs[9:]
    part, land1, land2, in_sem, out_sem, own_sem = refs[:6]
    (
        tokens, gain1, cos_table, sin_table, w_query, w_key, w_value, seg_row, w_out, gain2,
        routes, route_weights,
    ) = inside
    hidden1, queries, keys, values, lse, mixed, residual, hidden2, side = made
    loads = [
        pltpu.make_async_copy(src, dst, in_sem.at[i])
        for i, (src, dst) in enumerate(zip(given, inside))
    ]
    stores = [
        pltpu.make_async_copy(src, dst, out_sem.at[i])
        for i, (src, dst) in enumerate(zip(made, kept))
        if i != 6
    ]
    stores.insert(6, None)
    for load in loads:
        load.start()
    place = Place()
    greet(place, False)
    work = Sum4(place, part, land1, land2, refs[6:])
    for load in loads:
        load.wait()
    rows = [
        jnp.sum(
            jnp.where(routes[...] == e, route_weights[...], 0.0), 0, keepdims=True
        )
        for e in range(8)
    ]
    rows.append(seg_row[...].astype(F32))
    rows.append(jnp.zeros((119, 512), F32))
    side[...] = jnp.concatenate(rows, 0).T
    stores[8].start()
    seg_col = side[:, 8:9].astype(jnp.int32)
    for b in range(2):
        at = slice(256 * b, 256 * b + 256)
        until = 256 * b + 256

        def rotate(projected):
            turned = projected * cos_table[at] - swap_halves(projected) * sin_table[at]
            return turned.astype(BF16)

        normed = (row_norm(tokens[at].astype(F32))[0] * gain1[...]).astype(BF16)
        hidden1[at] = normed
        projected = dot_nn(normed, w_query[...])
        for g in range(2):
            queries[at, 128 * g : 128 * g + 128] = rotate(projected[:, 128 * g : 128 * g + 128])
        keys[at] = rotate(dot_nn(normed, w_key[...]))
        values[at] = dot_nn(normed, w_value[...]).astype(BF16)
        if b == 1:
            work.middle(0)
            work.middle(1)
        allowed = allowed_pairs(seg_col, seg_row, until, b)
        heads = []
        for h in range(4):
            own = slice(64 * (h // 2), 64 * (h // 2) + 64)
            raw = dot_nt(keys[:until, own], queries[at, 64 * h : 64 * h + 64]) * HD ** (-0.5)
            scores = jnp.where(allowed, raw, -1e30)
            top = jnp.max(scores, 0, keepdims=True)
            weights = jnp.exp(scores - top)
            row_total = jnp.sum(weights, 0, keepdims=True)
            lse[h : h + 1, at] = top + jnp.log(row_total)
            heads.append(dot_tn((weights / row_total).astype(BF16), values[:until, own]))
        mixed[at] = jnp.concatenate(heads, 1).astype(BF16)
        part[at] = dot_nn(mixed[at], w_out[...])
        work.one(2 * b).start()
        work.one(2 * b + 1).start()
    work.middle(2)
    work.middle(3)
    for store in stores[:6]:
        store.start()

    def give(rows):
        hidden2[rows] = (row_norm(residual[rows])[0] * gain2[...]).astype(BF16)

    def finish(k):
        at = work.own(k)
        residual[at] = tokens[at].astype(F32) + work.total(k)
        work.three(k, residual.at[at], residual.at[at]).start()
        give(at)

    loop(0, PIECES, finish)

    def own_rows(k):
        return pltpu.make_async_copy(
            residual.at[work.own(k)], kept[6].at[work.local(k)], own_sem.at[k]
        )

    def close(k):
        at = work.own(k)
        work.three(k, residual.at[at], residual.at[at]).wait()
        own_rows(k).start()
        give(work.other(k))
        work.one(k).wait_send()

    loop(0, PIECES, close)
    stores[7].start()
    for i, store in enumerate(stores):
        if i != 6:
            store.wait()
    loop(0, PIECES, lambda k: own_rows(k).wait())


def front_part(*given):
    rows, width = given[0].shape
    half = (rows // 2, width)
    made = (
        jax.ShapeDtypeStruct((rows, width), BF16),
        jax.ShapeDtypeStruct((rows, 256), BF16),
        jax.ShapeDtypeStruct((rows, 128), BF16),
        jax.ShapeDtypeStruct((rows, 128), BF16),
        jax.ShapeDtypeStruct((8, rows), F32),
        jax.ShapeDtypeStruct((rows, 256), BF16),
        jax.ShapeDtypeStruct((rows, width), F32),
        jax.ShapeDtypeStruct((rows, width), BF16),
        jax.ShapeDtypeStruct((rows, 128), F32),
    )
    return pl.pallas_call(
        front_kernel,
        out_shape=made[:6] + (jax.ShapeDtypeStruct(half, F32),) + made[7:],
        in_specs=[ANY] * len(given),
        out_specs=(ANY,) * len(made),
        scratch_shapes=[pltpu.VMEM(a.shape, a.dtype) for a in given + made]
        + [pltpu.VMEM((rows, width), F32)]
        + [pltpu.VMEM(half, F32)] * 2
        + [DMA((len(given),)), DMA((len(made),)), DMA((PIECES,))]
        + [DMA((PIECES,))] * 6,
        compiler_params=pltpu.CompilerParams(
            collective_id=1, has_side_effects=True, vmem_limit_bytes=60 << 20
        ),
    )(*given)


def row_norm(values):
    inverse = lax.rsqrt(jnp.mean(values * values, -1, keepdims=True) + NORM_EPS)
    return values * inverse, inverse


def norm_back(gradient, scaled, inverse, gain_vec):
    scaled_grad = gradient * gain_vec
    inner_sum = jnp.mean(scaled_grad * scaled, -1, keepdims=True)
    return inverse * (scaled_grad - scaled * inner_sum)


def fold(values):
    return jnp.sum(values.reshape(-1, 8, values.shape[-1]), 0)


def back_kernel(*refs):
    given, refs = refs[:23], refs[23:]
    output_hbm, input_grad_hbm, gain_sums, grads_sum, attn_sum = refs[:5]
    inside, refs = refs[5:24], refs[24:]
    (
        hidden2, dy, side, residual, gain2, mixed, w_out, queries, keys, values, lse, seg_row,
        cos_table, sin_table, w_query, w_key, w_value, tokens, gain1,
    ) = inside
    gate_w, up_w, down_w = refs[:3]
    (
        mine, land, ring_land2, zland, attn, attn_land, attn_land2, attn_zland, output, dresidual,
        dhidden2, out_part, hidden2_t, land1, land2, land3, folded, gains, gains_in,
    ) = refs[3:22]
    sems = refs[22:]
    ring_sems, sems = sems[:7], sems[7:]
    attn_sems, sems = sems[:7], sems[7:]
    sum_sems, sems = sems[:6], sems[6:]
    load_sem, weight_sem, late_sem, gain_s, gain_r = sems
    dqkv = hidden2_t.at[0:512]
    weights = given[19:22]
    hidden1_hbm = given[22]

    def weight_loads(p):
        slot = p % 2
        return [
            pltpu.make_async_copy(
                src.at[2 * p : 2 * p + 2], dst.at[slot], weight_sem.at[slot, i]
            )
            for i, (src, dst) in enumerate(zip(weights, (gate_w, up_w, down_w)))
        ]

    loads = [
        pltpu.make_async_copy(src, dst, load_sem.at[i])
        for i, (src, dst) in enumerate(zip(given[:19], inside))
    ]
    for load in loads[:3]:
        load.start()
    for p in range(2):
        for load in weight_loads(p):
            load.start()
    for load in loads[3:]:
        load.start()
    place = Place()
    greet(place, True)
    rings = [
        AxisRing(
            place, mine.at[u], land.at[u], ring_land2.at[u], zland.at[u], grads_sum.at[u],
            [sem.at[u] for sem in ring_sems],
        )
        for u in range(4)
    ]
    rings.append(
        AxisRing(place, attn, attn_land, attn_land2, attn_zland, attn_sum, attn_sems)
    )

    def after(place_in_order):
        for k, u in ORDER[place_in_order]:
            rings[u].op(k)

    sums = [
        Sum4(place, part, land1.at[which], land2.at[which], [sem.at[i] for sem in sum_sems])
        for i, (part, which) in enumerate(((dhidden2, 0), (out_part, 1), (dhidden2, 0)))
    ]
    back2, forward2, back1 = sums

    folded[...] = jnp.zeros_like(folded)
    for load in loads[:3]:
        load.wait()
    hidden2_t[...] = hidden2[...].T
    for p in range(4):
        slot = p % 2
        for load in weight_loads(p):
            load.wait()
        down_pair = down_w[slot].reshape(256, 1024)
        dact_pair = dot_nt(dy[...], down_pair)
        acts, dboths, both_ws = [], [], []
        for i in range(2):
            e = 2 * p + i
            both_w = jnp.concatenate([gate_w[slot, i], up_w[slot, i]], 1)
            both = dot_nn(hidden2[...], both_w)
            gate, up = both[:, :128], both[:, 128:]
            sig = 1.0 / (1.0 + jnp.exp(-gate))
            silu = gate * sig
            weight = side[:, e : e + 1]
            acts.append((silu * up * weight).astype(BF16))
            dact = dact_pair[:, 128 * i : 128 * i + 128] * weight
            dgate = (dact * up * (sig * (1.0 + gate * (1.0 - sig)))).astype(BF16)
            dup = (dact * silu).astype(BF16)
            dboth = jnp.concatenate([dgate, dup], 1)
            grad = dot_nn(hidden2_t[...], dboth)
            for h in range(2):
                rows = slice(512 * h, 512 * h + 512)
                mine[p, 2 * i + h, :, :, 0:32] = grad[rows, :128].reshape(4, 4, 32, 128)
                mine[p, 2 * i + h, :, :, 32:64] = grad[rows, 128:].reshape(4, 4, 32, 128)
            part = dot_nt(dboth, both_w)
            dhidden2[...] = part if e == 0 else dhidden2[...] + part
        act_pair = jnp.concatenate(acts, 1)
        down_grad = dot_tn(act_pair, dy[...])
        for i in range(2):
            for j in range(8):
                piece = down_grad[128 * i : 128 * i + 128, 128 * j : 128 * j + 128]
                mine[p, 2 * i + j // 4, j % 4, :, 64:96] = piece.reshape(4, 32, 128)
        after(2 * p)
        part = dot_nn(act_pair, down_pair)
        out_part[...] = part if p == 0 else out_part[...] + part
        if p < 2:
            for load in weight_loads(p + 2):
                load.start()
        after(2 * p + 1)
    late = [
        pltpu.make_async_copy(hidden1_hbm, hidden2, late_sem.at[0]),
    ]
    for load in late:
        load.start()
    back2.begin()
    after(8)
    for load in loads[3:]:
        load.wait()
    seg_col = side[:, 8:9].astype(jnp.int32)
    loop(0, PIECES, back2.middle)
    after(9)

    def finish2(k):
        d = back2.total(k)
        at = back2.own(k)
        scaled, inverse = row_norm(residual[back2.local(k)])
        folded[8:16] += fold(d * scaled)
        dresidual[at] = dy[at].astype(F32) + norm_back(d, scaled, inverse, gain2[...])
        back2.three(k, dresidual.at[at], dresidual.at[at]).start()

    finish2(0)
    after(10)
    finish2(1)
    after(11)
    finish2(2)
    after(12)
    finish2(3)
    after(13)

    def close2(k):
        at = back2.own(k)
        back2.three(k, dresidual.at[at], dresidual.at[at]).wait()
        back2.one(k).wait_send()

    loop(0, PIECES, close2)
    after(14)
    forward2.begin()
    after(15)

    dbranch = dresidual[...].astype(BF16)
    dmixed = dot_nt(dbranch, w_out[...]).astype(BF16)
    out_grad = dot_tn(mixed[...], dbranch)
    for j in range(8):
        piece = out_grad[:, 128 * j : 128 * j + 128].reshape(2, 4, 32, 128)
        attn[j // 2, 2 * (j % 2) : 2 * (j % 2) + 2, :, 64:96] = piece

    after(16)
    loop(0, PIECES, forward2.middle)
    after(17)

    def unrotate(grad):
        return (grad * cos_table[...] + swap_halves(grad) * sin_table[...]).astype(BF16)

    dkeys, dvalues = [], []
    for g in range(2):
        key = keys[:, 64 * g : 64 * g + 64]
        value = values[:, 64 * g : 64 * g + 64]
        dkey = [0.0, 0.0]
        dvalue = [0.0, 0.0]
        dquery = []
        for h in (2 * g, 2 * g + 1):
            blocks = []
            for b in range(2):
                at = slice(256 * b, 256 * b + 256)
                until = 256 * b + 256
                query = queries[at, 64 * h : 64 * h + 64]
                dmix = dmixed[at, 64 * h : 64 * h + 64]
                raw = dot_nt(key[:until], query) * HD ** (-0.5)
                allowed = allowed_pairs(seg_col, seg_row, until, b)
                probs = jnp.exp(jnp.where(allowed, raw, -1e30) - lse[h : h + 1, at])
                dprobs = dot_nt(value[:until], dmix)
                inner = jnp.sum(probs * dprobs, 0, keepdims=True)
                dscores = (probs * (dprobs - inner)).astype(BF16)
                dvalue_part = dot_nn(probs.astype(BF16), dmix)
                dkey_part = dot_nn(dscores, query)
                for t in range(b + 1):
                    dvalue[t] = dvalue[t] + dvalue_part[256 * t : 256 * t + 256]
                    dkey[t] = dkey[t] + dkey_part[256 * t : 256 * t + 256]
                blocks.append(dot_tn(dscores, key[:until]))
                if b == 1:
                    after(18 + h)
            dquery.append(jnp.concatenate(blocks, 0) * HD ** (-0.5))
        dqkv[:, 128 * g : 128 * g + 128] = unrotate(jnp.concatenate(dquery, 1))
        dkeys.append(jnp.concatenate(dkey, 0) * HD ** (-0.5))
        dvalues.append(jnp.concatenate(dvalue, 0))
    dqkv[:, 256:384] = unrotate(jnp.concatenate(dkeys, 1))
    dqkv[:, 384:512] = jnp.concatenate(dvalues, 1).astype(BF16)

    for load in late:
        load.wait()
    hidden_grad = dot_tn(hidden2[...], dqkv[...])
    for j in range(4):
        piece = hidden_grad[:, 128 * j : 128 * j + 128].reshape(4, 4, 4, 16, 128)
        attn[:, :, :, 16 * j : 16 * j + 16] = piece
    after(22)
    dhidden2[...] = (
        dot_nt(dqkv[:, :256], w_query[...])
        + dot_nt(dqkv[:, 256:384], w_key[...])
        + dot_nt(dqkv[:, 384:512], w_value[...])
    )
    after(23)
    back1.begin()
    after(24)

    def finish_out(k):
        done = forward2.total(k) + residual[forward2.local(k)]
        at = forward2.local(k)
        output[forward2.own(k)] = done.astype(BF16)
        forward2.land1[at] = done
        forward2.three(k, forward2.land1.at[at], land3.at[at]).start()

    def close_out(k):
        at = forward2.local(k)
        forward2.three(k, forward2.land1.at[at], land3.at[at]).wait()
        output[forward2.other(k)] = land3[at].astype(BF16)

    loop(0, PIECES, finish_out)
    after(25)
    loop(0, PIECES, back1.middle)
    after(26)
    loop(0, PIECES, close_out)
    after(27)
    stores = [
        pltpu.make_async_copy(output, output_hbm, late_sem.at[1]),
        pltpu.make_async_copy(dresidual, input_grad_hbm, late_sem.at[2]),
    ]
    stores[0].start()

    def finish1(k):
        d = back1.total(k)
        at = back1.own(k)
        scaled, inverse = row_norm(tokens[at].astype(F32))
        folded[0:8] += fold(d * scaled)
        dresidual[at] = dresidual[at] + norm_back(d, scaled, inverse, gain1[...])
        back1.three(k, dresidual.at[at], dresidual.at[at]).start()

    finish1(0)
    after(28)
    finish1(1)
    after(29)
    finish1(2)
    after(30)
    finish1(3)
    after(31)
    gains[0] = jnp.concatenate(
        [
            jnp.sum(folded[0:8], 0, keepdims=True),
            jnp.sum(folded[8:16], 0, keepdims=True),
            jnp.zeros((6, gains.shape[2]), F32),
        ],
        0,
    )

    def swap(i):
        device = (place.dp, place.buddy) if i == 0 else (place.pairs[i - 1], place.tensor)
        return pltpu.make_async_remote_copy(
            gains.at[i], gains_in.at[i], gain_s.at[i], gain_r.at[i],
            device_id=device, device_id_type=MESH,
        )

    def add_swap(i):
        swap(i).wait_recv()
        gains[i + 1] = gains[i] + gains_in[i]

    swap(0).start()
    after(32)
    add_swap(0)
    after(33)
    swap(1).start()
    after(34)

    def close1(k):
        at = back1.own(k)
        back1.three(k, dresidual.at[at], dresidual.at[at]).wait()

    loop(0, PIECES, close1)
    after(35)
    stores[1].start()
    add_swap(1)
    after(36)
    swap(2).start()
    after(37)
    add_swap(2)
    after(38)
    swap(3).start()
    after(39)
    add_swap(3)
    after(40)
    swap(4).start()
    after(41)
    add_swap(4)
    after(42)
    swap(5).start()
    after(43)
    add_swap(5)
    gain_sums[...] = gains[6]
    after(44)
    for i in range(6):
        swap(i).wait_send()

    def close(k):
        forward2.one(k).wait_send()
        back1.one(k).wait_send()

    loop(0, PIECES, close)
    for store in stores:
        store.wait()


def back_part(*given):
    rows, width = given[0].shape
    half = (rows // 2, width)
    grads, attn = (4, 4, 4, 4, 96, 128), (4, 4, 4, 96, 128)
    S = pltpu.VMEM
    ring_sems = [DMA((4, 4))] + [DMA((4, 4, 3))] * 4 + [DMA((4, 4))] * 2
    attn_sems = [DMA((4,))] + [DMA((4, 3))] * 4 + [DMA((4,))] * 2
    return pl.pallas_call(
        back_kernel,
        out_shape=(
            jax.ShapeDtypeStruct((rows, width), BF16),
            jax.ShapeDtypeStruct((rows, width), F32),
            jax.ShapeDtypeStruct((8, width), F32),
            jax.ShapeDtypeStruct(grads, F32),
            jax.ShapeDtypeStruct(attn, F32),
        ),
        in_specs=[ANY] * len(given),
        out_specs=(ANY, ANY, VMEM, ANY, ANY),
        scratch_shapes=[S(a.shape, a.dtype) for a in given[:19]]
        + [S((2, 2, width, 128), BF16), S((2, 2, width, 128), BF16), S((2, 2, 128, width), BF16)]
        + [
            S(grads, F32), S(grads, F32), S((4, 4, 4, 96, 128), F32), S((4, 4, 96, 128), F32),
            S(attn, F32), S(attn, F32), S((4, 4, 96, 128), F32), S((4, 96, 128), F32),
            S((rows, width), BF16), S((rows, width), F32),
            S((rows, width), F32), S((rows, width), F32), S((width, rows), BF16),
            S((2,) + half, F32), S((2,) + half, F32), S(half, F32),
            S((16, width), F32), S((7, 8, width), F32), S((6, 8, width), F32),
        ]
        + ring_sems
        + attn_sems
        + [DMA((3, PIECES))] * 6
        + [DMA((19,)), DMA((2, 3)), DMA((3,)), DMA((6,)), DMA((6,))],
        compiler_params=pltpu.CompilerParams(
            collective_id=2, has_side_effects=True, vmem_limit_bytes=64 << 20
        ),
    )(*given)


def unpack_kernel(
    grads, attn, gains, forward, backward, gate, up, down, query, key, value, out, gain1, gain2,
    output, input_grad
):
    for h in range(2):
        rows = slice(512 * h, 512 * h + 512)
        gate[0, rows] = grads[0, h, :, 0:32].reshape(512, 128)
        up[0, rows] = grads[0, h, :, 32:64].reshape(512, 128)
        for a in range(4):
            lanes = slice(128 * (4 * h + a), 128 * (4 * h + a) + 128)
            down[0, :, lanes] = grads[0, h, 4 * a : 4 * a + 4, 64:96].reshape(128, 128)
    query[:, 0:128] = attn[:, 0:16].reshape(128, 128)
    query[:, 128:256] = attn[:, 16:32].reshape(128, 128)
    key[...] = attn[:, 32:48].reshape(128, 128)
    value[...] = attn[:, 48:64].reshape(128, 128)
    out[...] = attn[:, 64:96].reshape(256, 128)
    gain1[...] = gains[0:1]
    gain2[...] = gains[1:2]
    output[...] = forward[...]
    input_grad[...] = backward[...]


def unpack(grads, attn, gains, forward, backward):
    return pl.pallas_call(
        unpack_kernel,
        grid=(8,),
        out_shape=(
            jax.ShapeDtypeStruct((8, 1024, 128), F32),
            jax.ShapeDtypeStruct((8, 1024, 128), F32),
            jax.ShapeDtypeStruct((8, 128, 1024), F32),
            jax.ShapeDtypeStruct((1024, 256), F32),
            jax.ShapeDtypeStruct((1024, 128), F32),
            jax.ShapeDtypeStruct((1024, 128), F32),
            jax.ShapeDtypeStruct((256, 1024), F32),
            jax.ShapeDtypeStruct((1, 1024), F32),
            jax.ShapeDtypeStruct((1, 1024), F32),
            jax.ShapeDtypeStruct(forward.shape, BF16),
            jax.ShapeDtypeStruct(backward.shape, F32),
        ),
        in_specs=[
            pl.BlockSpec((1, 2, 16, 96, 128), lambda p: (p, 0, 0, 0, 0)),
            pl.BlockSpec((8, 96, 128), lambda p: (p, 0, 0)),
            pl.BlockSpec((8, 128), lambda p: (0, p)),
            pl.BlockSpec((64, 1024), lambda p: (p, 0)),
            pl.BlockSpec((64, 1024), lambda p: (p, 0)),
        ],
        out_specs=(
            pl.BlockSpec((1, 1024, 128), lambda p: (p, 0, 0)),
            pl.BlockSpec((1, 1024, 128), lambda p: (p, 0, 0)),
            pl.BlockSpec((1, 128, 1024), lambda p: (p, 0, 0)),
            pl.BlockSpec((128, 256), lambda p: (p, 0)),
            pl.BlockSpec((128, 128), lambda p: (p, 0)),
            pl.BlockSpec((128, 128), lambda p: (p, 0)),
            pl.BlockSpec((256, 128), lambda p: (0, p)),
            pl.BlockSpec((1, 128), lambda p: (0, p)),
            pl.BlockSpec((1, 128), lambda p: (0, p)),
            pl.BlockSpec((64, 1024), lambda p: (p, 0)),
            pl.BlockSpec((64, 1024), lambda p: (p, 0)),
        ),
        compiler_params=pltpu.CompilerParams(vmem_limit_bytes=62 << 20),
    )(grads, attn, gains, forward, backward)


def tables(seq_length):
    half_width = HD // 2
    exponent = -np.arange(half_width, dtype=np.float32) * np.float32(2.0) / np.float32(HD)
    frequency = np.power(np.float32(ROPE_THETA), exponent)
    angles = np.arange(seq_length, dtype=np.float32)[:, None] * frequency[None, :]
    cosine, sine = np.cos(angles), np.sin(angles)
    return (
        jnp.asarray(np.concatenate([cosine] * 4, 1)),
        jnp.asarray(np.concatenate([sine, -sine] * 2, 1)),
    )


def local(
    tokens,
    norm1_gain,
    w_query,
    w_key,
    w_value,
    w_out,
    norm2_gain,
    expert_gate,
    expert_up,
    expert_down,
    routes,
    gate_weights,
    segments,
    cotangent,
):
    experts = expert_gate.shape[0]
    cos_table, sin_table = tables(tokens.shape[0])
    gain1, gain2 = norm1_gain[None], norm2_gain[None]
    hidden1, queries, keys, values, lse, mixed, residual, hidden2, side = front_part(
        tokens, gain1, cos_table, sin_table, w_query, w_key, w_value, segments, w_out, gain2,
        routes.T, gate_weights.T,
    )
    output, input_grad, gains, grads, attn = back_part(
        hidden2, cotangent, side, residual, gain2, mixed, w_out, queries, keys, values, lse,
        segments, cos_table, sin_table, w_query, w_key, w_value, tokens, gain1, expert_gate,
        expert_up, expert_down, hidden1,
    )
    (
        gate_grad, up_grad, down_grad, query_grad, key_grad, value_grad, out_grad, gain1_grad,
        gain2_grad, output, input_grad,
    ) = unpack(
        grads.reshape(experts, 2, 16, 96, 128), attn.reshape(64, 96, 128), gains, output, input_grad
    )
    return (
        output,
        input_grad,
        gain1_grad.reshape(-1),
        query_grad,
        key_grad,
        value_grad,
        out_grad,
        gain2_grad.reshape(-1),
        gate_grad,
        up_grad,
        down_grad,
    )


def solution(mesh):
    return jax.shard_map(
        local,
        mesh=mesh,
        in_specs=(
            P("dp", None),
            P(),
            P(None, "tensor"),
            P(None, "tensor"),
            P(None, "tensor"),
            P("tensor", None),
            P(),
            P(None, None, "tensor"),
            P(None, None, "tensor"),
            P(None, "tensor", None),
            P("dp", None),
            P("dp", None),
            P("dp", None),
            P("dp", None),
        ),
        out_specs=(
            P("dp", None),
            P("dp", None),
            P(),
            P(None, "tensor"),
            P(None, "tensor"),
            P(None, "tensor"),
            P("tensor", None),
            P(),
            P(None, None, "tensor"),
            P(None, None, "tensor"),
            P(None, "tensor", None),
        ),
        check_vma=False,
    )
```
